256 devices in a mesh: blk: 128 (over y, x_hi, z, core), rhs: 2 (over x_lo).
Axes of the slice: x: 4 (x_hi: 2, x_lo: 2; x = x_hi * 2 + x_lo), y: 4, z: 8, core: 2. Of those that a mesh axis runs over, the one named last changes fastest.
Arguments:
- directions: bfloat16 [262144, 256], P('blk', 'rhs'), may hold values from -6 to 6
- axial_pos: bfloat16 [262144], P('blk'), may hold values from 0 to 8
- azimuth: bfloat16 [262144], P('blk'), may hold values from -3.140625 to 3.140625
- panel_area: bfloat16 [262144], P('blk'), may hold values from 0.5 to 2
Outputs:
- product: float32 [262144, 256], P('blk', 'rhs')
- gram: float32 [256, 256], P(None, 'rhs')
The draws below stay inside these ranges and needn't reach their ends.
All inputs are finite; a program needn't handle non-finite values.
Results may differ from the reference program's by a relative error of at most 0.0029.
Values may be sent and summed in bfloat16 or wider, within the bound.
No kernel may reach another device: no remote copies, remote signals or barrier semaphores. Data moves between devices by JAX's collectives and lax.ppermute only.
A program may use at most 64 MiB of HBM per device.

```python
import math
import jax
import jax.numpy as jnp
from jax import lax

PAN_DEV = 2048
RHS = 256
ROUNDS = 3
PANELS = 262144
N_BLK = 128


def steps_of(stream_key, shape, pieces, least, high):
    def one(axis_at, shards_of):
        heights = jax.random.uniform(jax.random.fold_in(jax.random.fold_in(stream_key, 6), axis_at), (shards_of,), jnp.float32, least / len(pieces), high / len(pieces))
        return jnp.repeat(jnp.exp(heights), shape[axis_at] // shards_of).reshape((-1,) + (1,) * (len(shape) - axis_at - 1))

    level = one(*pieces[0])
    for cut in pieces[1:]:
        level = level * one(*cut)
    return level


def gaussian(rng, extent, deviation, limit, split=(), held_as=jnp.bfloat16):
    loudness = steps_of(rng, extent, split, -0.22, 0.18) if split else 1.0
    values = jax.random.normal(rng, extent, jnp.float32) * deviation * loudness
    return jnp.minimum(jnp.maximum(values, -limit), limit).astype(held_as)


def setup_inputs(seed: int = 0) -> dict:
    splits = jax.random.split(jax.random.key(seed), 5)
    return {
        "directions": gaussian(splits[0], (PANELS, RHS), 1.0, 6.0, ((0, 128), (1, 2))),
        "axial_pos": jnp.clip(8.0 * jax.random.uniform(splits[1], (PANELS,), jnp.float32) ** steps_of(splits[1], (PANELS,), ((0, 128),), -0.2, 0.2), 0.0, 8.0).astype(jnp.bfloat16),
        "azimuth": jnp.clip(jax.random.uniform(splits[2], (PANELS,), jnp.float32, -3.140625, 3.140625), -3.140625, 3.140625).astype(jnp.bfloat16),
        "panel_area": jnp.clip(jnp.exp(math.log(2.0) - 1.3862944 * jax.random.uniform(splits[3], (PANELS,), jnp.float32) ** steps_of(splits[3], (PANELS,), ((0, 128),), -0.2, 0.2)), 0.5, 2.0).astype(jnp.bfloat16),
    }


def kernel_tile(row_geom, col_geom, count):
    row_axial, row_cos, row_sin, row_weight = row_geom
    col_axial, col_cos, col_sin, col_weight = col_geom
    delta_a = row_axial[:, None] - col_axial[None, :]
    delta_c = row_cos[:, None] - col_cos[None, :]
    delta_s = row_sin[:, None] - col_sin[None, :]
    square = delta_a * delta_a + delta_c * delta_c + delta_s * delta_s
    weights = row_weight[:, None] * col_weight[None, :]
    value = weights * lax.rsqrt(square + 0.01) / jnp.sqrt(jnp.float32(count))
    return value.astype(jnp.bfloat16)

def reference(directions, axial_pos, azimuth, panel_area):
    axial_f = axial_pos.astype(jnp.float32).reshape(N_BLK, PAN_DEV)
    angle_f = azimuth.astype(jnp.float32).reshape(N_BLK, PAN_DEV)
    cos_f = jnp.cos(angle_f)
    sin_f = jnp.sin(angle_f)
    weight_f = panel_area.astype(jnp.float32).reshape(N_BLK, PAN_DEV)
    blocked = directions.astype(jnp.float32).reshape(N_BLK, PAN_DEV, RHS)

    def one_block(index):
        row_geom = (axial_f[index], cos_f[index], sin_f[index], weight_f[index])
        total = jnp.zeros((PAN_DEV, RHS), jnp.float32)
        for offset in range(-ROUNDS, ROUNDS + 1):
            other = ((index + offset) % N_BLK).astype(jnp.int32)
            col_geom = (axial_f[other], cos_f[other], sin_f[other], weight_f[other])
            values = kernel_tile(row_geom, col_geom, PAN_DEV).astype(jnp.float32)
            total = total + jnp.dot(values, blocked[other], precision=lax.Precision.HIGHEST)
        return total
    product = lax.map(one_block, jnp.arange(N_BLK, dtype=jnp.int32)).reshape(PANELS, RHS)
    gram = jnp.dot(directions.astype(jnp.float32).T, product, precision=lax.Precision.HIGHEST) / PANELS
    return (product, gram)
```

```python
import functools

import jax
import jax.numpy as jnp
from jax import lax
from jax.experimental import pallas as pl
from jax.experimental.pallas import tpu as pltpu
from jax.sharding import Mesh, PartitionSpec as P

LANES = 128
VMEM_BYTES = 24 * 2**20
ROW_STEP = 1024
COL_STEP = 256
BLK = ("y", "xh", "z", "core")


def split_parts(base):
    high = base.astype(jnp.bfloat16).astype(jnp.float32)
    rest = base - high
    mid = rest.astype(jnp.bfloat16).astype(jnp.float32)
    low = (rest - mid).astype(jnp.bfloat16).astype(jnp.float32)
    return high, mid, low


def point_values(axial, angle, area):
    axial = axial.astype(jnp.float32) - 4.0
    angle = angle.astype(jnp.float32)
    area = area.astype(jnp.float32)
    cos, sin = jnp.cos(angle), jnp.sin(angle)
    return axial, cos, sin, axial * axial + cos * cos + sin * sin, 1.0 / (area * area)


def lay_rows(base_ref, features):
    groups = features[0].shape[0]
    base_ref[...] = jnp.zeros_like(base_ref)
    for row, feature in enumerate(features):
        for group in range(groups):
            base_ref[row : row + 1, group * LANES : (group + 1) * LANES] = feature[group : group + 1, :]


def column_factors(geometry, base_ref, col_ref):
    axial, cos, sin, norm, scale = point_values(*geometry)
    lay_rows(base_ref, (scale, norm * scale, axial * scale, cos * scale, sin * scale))
    high, mid, low = split_parts(base_ref[...])
    col_ref[...] = jnp.concatenate([high, high, high, mid, mid, low], axis=0).astype(jnp.bfloat16)


def row_factors(geometry, base_ref, row_ref):
    axial, cos, sin, norm, scale = point_values(*geometry)
    count = base_ref.shape[1]
    scale = scale * count
    double = -2.0 * scale
    lay_rows(base_ref, ((norm + 0.01) * scale, scale, axial * double, cos * double, sin * double))
    high, mid, low = split_parts(base_ref[...])
    stacked = jnp.concatenate([high, mid, low, high, mid, high], axis=0)
    for group in range(count // LANES):
        part = stacked[:, group * LANES : (group + 1) * LANES]
        row_ref[group * LANES : (group + 1) * LANES, :] = part.T.astype(jnp.bfloat16)


def tile_product(row_ref, col_ref, message_ref, total_ref, out_ref):
    count = row_ref.shape[0]

    def step_fn(step, carried):
        rows = pl.ds(pl.multiple_of(step * ROW_STEP, ROW_STEP), ROW_STEP)
        factor = row_ref[rows, :]
        total = jnp.zeros((ROW_STEP, LANES), jnp.float32) if total_ref is None else total_ref[rows, :]
        for start in range(0, count, COL_STEP):
            inverse = jnp.dot(factor, col_ref[:, start : start + COL_STEP], preferred_element_type=jnp.float32)
            values = lax.rsqrt(inverse).astype(jnp.bfloat16)
            total = total + jnp.dot(
                values, message_ref[start : start + COL_STEP, :], preferred_element_type=jnp.float32
            )
        out_ref[rows, :] = total
        return carried

    lax.fori_loop(0, count // ROW_STEP, step_fn, 0)


def message_geometry(message_ref, count):
    groups = count // LANES
    return tuple(message_ref[count + k * groups : count + (k + 1) * groups, :] for k in range(3))


def home_body(message_ref, out_ref, row_ref, base_ref, col_ref):
    count = row_ref.shape[0]
    geometry = message_geometry(message_ref, count)
    row_factors(geometry, base_ref, row_ref)
    column_factors(geometry, base_ref, col_ref)
    tile_product(row_ref, col_ref, message_ref, None, out_ref)


def guest_body(has_total, row_ref, message_ref, *refs):
    total_ref = refs[0] if has_total else None
    out_ref, base_ref, col_ref = refs[has_total:]
    column_factors(message_geometry(message_ref, row_ref.shape[0]), base_ref, col_ref)
    tile_product(row_ref, col_ref, message_ref, total_ref, out_ref)


def tile_scratch(count):
    return [pltpu.VMEM((8, count), jnp.float32), pltpu.VMEM((48, count), jnp.bfloat16)]


def tile_cost(count):
    flops = 2 * count * count * 256 * 2
    return pl.CostEstimate(flops=flops, bytes_accessed=3 * count * LANES * 4, transcendentals=0)


def home_tile(message, count):
    vmem = pl.BlockSpec(memory_space=pltpu.VMEM)
    return pl.pallas_call(
        home_body,
        out_shape=[
            jax.ShapeDtypeStruct((count, LANES), jnp.float32),
            jax.ShapeDtypeStruct((count, 48), jnp.bfloat16),
        ],
        in_specs=[vmem],
        out_specs=[vmem, vmem],
        scratch_shapes=tile_scratch(count),
        cost_estimate=tile_cost(count),
        compiler_params=pltpu.CompilerParams(vmem_limit_bytes=VMEM_BYTES),
        name="home_tile",
    )(message)


def guest_tile(rows, message, total, count):
    vmem = pl.BlockSpec(memory_space=pltpu.VMEM)
    operands = (rows, message) if total is None else (rows, message, total)
    return pl.pallas_call(
        functools.partial(guest_body, total is not None),
        out_shape=jax.ShapeDtypeStruct((count, LANES), jnp.float32),
        in_specs=[vmem] * len(operands),
        out_specs=vmem,
        input_output_aliases={} if total is None else {2: 0},
        scratch_shapes=tile_scratch(count),
        cost_estimate=tile_cost(count),
        compiler_params=pltpu.CompilerParams(vmem_limit_bytes=VMEM_BYTES),
        name="guest_tile",
    )(*operands)


def half_gram_body(own_ref, pair_ref, first_ref, second_ref, out_ref):
    value = 0.5 * first_ref[...] + second_ref[...]
    high = value.astype(jnp.bfloat16)
    low = (value - high.astype(jnp.float32)).astype(jnp.bfloat16)
    both = jnp.concatenate([high, low], axis=1)
    for k, ref in enumerate((own_ref, pair_ref)):
        part = lax.dot_general(
            ref[: value.shape[0], :], both, (((0,), (0,)), ((), ())), preferred_element_type=jnp.float32
        )
        out_ref[k * LANES : (k + 1) * LANES, :] = part[:, :LANES] + part[:, LANES:]


def half_gram(own, pair, first, second):
    vmem = pl.BlockSpec(memory_space=pltpu.VMEM)
    return pl.pallas_call(
        half_gram_body,
        out_shape=jax.ShapeDtypeStruct((2 * LANES, LANES), jnp.float32),
        in_specs=[vmem] * 4,
        out_specs=vmem,
        cost_estimate=pl.CostEstimate(flops=2 * 2048 * 256 * 256, bytes_accessed=3 * 2**20, transcendentals=0),
        compiler_params=pltpu.CompilerParams(vmem_limit_bytes=VMEM_BYTES),
        name="half_gram",
    )(own, pair, first, second)


def along_blk(value, sizes, target):
    ny, nx, nz, nc = sizes

    def index(y, x, z, c):
        return ((y % ny * nx + x % nx) * nz + z % nz) * nc + c % nc

    pairs = []
    for y in range(ny):
        for x in range(nx):
            for z in range(nz):
                for c in range(nc):
                    pairs.append((index(y, x, z, c), index(*target(y, x, z, c))))
    return lax.ppermute(value, BLK, pairs)


def from_shift(value, steps):
    count = lax.axis_size(BLK)
    return lax.ppermute(value, BLK, [(source, (source - steps) % count) for source in range(count)])


def from_far(value):
    count = lax.axis_size(BLK)
    return lax.ppermute(
        value, BLK, [(b, (b - 3 if b % 2 == 0 else b + 3) % count) for b in range(count)]
    )


def core_swap(value):
    return lax.ppermute(value, "core", [(0, 1), (1, 0)])


def shards(sizes, directions, axial_pos, azimuth, panel_area):
    count = axial_pos.shape[0]
    geometry = [part.reshape(count // LANES, LANES) for part in (axial_pos, azimuth, panel_area)]
    message = jnp.concatenate([directions] + geometry, axis=0)
    other = core_swap(message)
    ahead = from_shift(message, 2)
    far = from_far(message)
    pair = lax.ppermute(directions, "rhs", [(0, 1), (1, 0)])
    behind = from_shift(message, -2)
    ahead_other = core_swap(ahead)
    behind_other = core_swap(behind)

    first, rows = home_tile(message, count)
    first = guest_tile(rows, other, first, count)
    second = guest_tile(rows, ahead, None, count)
    second = guest_tile(rows, ahead_other, second, count)
    first = guest_tile(rows, far, first, count)
    half = half_gram(directions, pair, first, second)

    third = guest_tile(rows, behind, first + second, count)
    product = guest_tile(rows, behind_other, third, count)

    core = lax.axis_index("core")
    keep = jnp.where(core == 0, half[:LANES], half[LANES:])
    give = jnp.where(core == 0, half[LANES:], half[:LANES])
    value = keep + core_swap(give)
    for stage in (
        [(0, 0, 1), (0, 0, 2), (0, 0, 3)],
        [(1, 0, 0), (2, 0, 0), (3, 0, 0)],
        [(0, 0, 4), (0, 1, 0), (0, 1, 4)],
    ):
        moved = [
            along_blk(value, sizes, lambda y, x, z, c, d=d: (y + d[0], x + d[1], z + d[2], c)) for d in stage
        ]
        value = (value + moved[0]) + (moved[1] + moved[2])
    swapped = core_swap(value)
    crossed = lax.ppermute(value, ("core", "rhs"), [(3, 0), (2, 1)])
    direct = lax.ppermute(value, ("core", "rhs"), [(2, 3), (3, 2)])
    own = jnp.where(core == 0, value, swapped)
    cross = jnp.where(core == 0, swapped, value)
    cross_pair = jnp.where(core == 0, crossed, direct)
    own = own + own.T
    cross = cross + cross_pair.T
    rhs = lax.axis_index("rhs")
    gram = jnp.concatenate([jnp.where(rhs == 0, own, cross), jnp.where(rhs == 0, cross, own)], axis=0)
    return product, gram / (count * lax.axis_size(BLK))


def solution(mesh):
    sizes = (4, 2, 8, 2)
    fine = Mesh(mesh.devices.reshape(sizes + (2,)), BLK + ("rhs",))
    in_specs = (P(BLK, "rhs"), P(BLK), P(BLK), P(BLK))
    out_specs = (P(BLK, "rhs"), P(None, "rhs"))
    return jax.shard_map(
        functools.partial(shards, sizes), mesh=fine, in_specs=in_specs, out_specs=out_specs, check_vma=False
    )
```

```python
import functools

import jax
import jax.numpy as jnp
from jax import lax
from jax.experimental import pallas as pl
from jax.experimental.pallas import tpu as pltpu
from jax.sharding import Mesh, PartitionSpec as P

LANES = 128
VMEM_BYTES = 8 * 2**20
COL_STEP = 256
BLK = ("y", "xh", "z", "core")


def split_parts(base):
    high = base.astype(jnp.bfloat16).astype(jnp.float32)
    rest = base - high
    mid = rest.astype(jnp.bfloat16).astype(jnp.float32)
    low = (rest - mid).astype(jnp.bfloat16).astype(jnp.float32)
    return high, mid, low


def point_values(axial, angle, area):
    axial = axial.astype(jnp.float32) - 4.0
    angle = angle.astype(jnp.float32)
    area = area.astype(jnp.float32)
    cos, sin = jnp.cos(angle), jnp.sin(angle)
    return axial, cos, sin, axial * axial + cos * cos + sin * sin, 1.0 / (area * area)


def lay_rows(base_ref, features):
    groups = features[0].shape[0]
    base_ref[...] = jnp.zeros_like(base_ref)
    for row, feature in enumerate(features):
        for group in range(groups):
            base_ref[row : row + 1, group * LANES : (group + 1) * LANES] = feature[group : group + 1, :]


def column_factors(geometry, base_ref, col_ref):
    axial, cos, sin, norm, scale = point_values(*geometry)
    lay_rows(base_ref, (scale, norm * scale, axial * scale, cos * scale, sin * scale))
    high, mid, low = split_parts(base_ref[...])
    col_ref[...] = jnp.concatenate([high, high, high, mid, mid, low], axis=0).astype(jnp.bfloat16)


def row_factors(geometry, base_ref, row_ref):
    axial, cos, sin, norm, scale = point_values(*geometry)
    count = base_ref.shape[1]
    scale = scale * count
    double = -2.0 * scale
    lay_rows(base_ref, ((norm + 0.01) * scale, scale, axial * double, cos * double, sin * double))
    high, mid, low = split_parts(base_ref[...])
    stacked = jnp.concatenate([high, mid, low, high, mid, high], axis=0)
    for group in range(count // LANES):
        part = stacked[:, group * LANES : (group + 1) * LANES]
        row_ref[group * LANES : (group + 1) * LANES, :] = part.T.astype(jnp.bfloat16)


def tile_product(row_ref, col_ref, message_ref, total_refs, out_ref):
    factor = row_ref[...]
    total = None
    for ref in total_refs:
        total = ref[...] if total is None else total + ref[...]
    for start in range(0, col_ref.shape[1], COL_STEP):
        inverse = jnp.dot(factor, col_ref[:, start : start + COL_STEP], preferred_element_type=jnp.float32)
        values = lax.rsqrt(inverse).astype(jnp.bfloat16)
        part = jnp.dot(values, message_ref[start : start + COL_STEP, :], preferred_element_type=jnp.float32)
        total = part if total is None else total + part
    out_ref[...] = total


def message_geometry(message_ref, count):
    groups = count // LANES
    return tuple(message_ref[count + k * groups : count + (k + 1) * groups, :] for k in range(3))


def home_body(message_ref, out_ref, row_ref, base_ref, col_ref):
    count = row_ref.shape[0]
    geometry = message_geometry(message_ref, count)
    row_factors(geometry, base_ref, row_ref)
    column_factors(geometry, base_ref, col_ref)
    tile_product(row_ref, col_ref, message_ref, (), out_ref)


def guest_body(row_ref, message_ref, *refs):
    *total_refs, out_ref, base_ref, col_ref = refs
    column_factors(message_geometry(message_ref, col_ref.shape[1]), base_ref, col_ref)
    tile_product(row_ref, col_ref, message_ref, total_refs, out_ref)


def tile_scratch(count):
    return [pltpu.VMEM((8, count), jnp.float32), pltpu.VMEM((48, count), jnp.bfloat16)]


def tile_cost(count):
    flops = count * count * 256
    return pl.CostEstimate(flops=flops, bytes_accessed=3 * count * LANES * 4, transcendentals=0)


def home_tile(message, count):
    vmem = pl.BlockSpec(memory_space=pltpu.VMEM)
    return pl.pallas_call(
        home_body,
        out_shape=[
            jax.ShapeDtypeStruct((count, LANES), jnp.float32),
            jax.ShapeDtypeStruct((count, 48), jnp.bfloat16),
        ],
        in_specs=[vmem],
        out_specs=[vmem, vmem],
        scratch_shapes=tile_scratch(count),
        cost_estimate=tile_cost(count),
        compiler_params=pltpu.CompilerParams(vmem_limit_bytes=VMEM_BYTES),
        name="home_tile",
    )(message)


def guest_tile(rows, message, totals, count, piece=0, pieces=1):
    height = count // pieces
    block = pl.BlockSpec((height, LANES), lambda step: (piece, 0))
    return pl.pallas_call(
        guest_body,
        grid=(1,),
        out_shape=jax.ShapeDtypeStruct((count, LANES), jnp.float32),
        in_specs=[
            pl.BlockSpec((height, rows.shape[1]), lambda step: (piece, 0)),
            pl.BlockSpec(message.shape, lambda step: (0, 0)),
        ]
        + [block] * len(totals),
        out_specs=block,
        input_output_aliases={2: 0} if totals else {},
        scratch_shapes=tile_scratch(count),
        cost_estimate=tile_cost(count),
        compiler_params=pltpu.CompilerParams(vmem_limit_bytes=VMEM_BYTES),
        name="guest_tile",
    )(rows, message, *totals)


def half_gram_body(own_ref, pair_ref, first_ref, second_ref, out_ref):
    value = 0.5 * first_ref[...] + second_ref[...]
    high = value.astype(jnp.bfloat16)
    low = (value - high.astype(jnp.float32)).astype(jnp.bfloat16)
    both = jnp.concatenate([high, low], axis=1)
    for k, ref in enumerate((own_ref, pair_ref)):
        part = lax.dot_general(
            ref[: value.shape[0], :], both, (((0,), (0,)), ((), ())), preferred_element_type=jnp.float32
        )
        out_ref[k] = part[:, :LANES] + part[:, LANES:]


def half_gram(own, pair, first, second):
    vmem = pl.BlockSpec(memory_space=pltpu.VMEM)
    return pl.pallas_call(
        half_gram_body,
        out_shape=jax.ShapeDtypeStruct((2, LANES, LANES), jnp.float32),
        in_specs=[vmem] * 4,
        out_specs=vmem,
        cost_estimate=pl.CostEstimate(flops=2 * 2048 * 256 * 256, bytes_accessed=3 * 2**20, transcendentals=0),
        compiler_params=pltpu.CompilerParams(vmem_limit_bytes=VMEM_BYTES),
        name="half_gram",
    )(own, pair, first, second)


def along_blk(value, sizes, target):
    ny, nx, nz, nc = sizes

    def index(y, x, z, c):
        return ((y % ny * nx + x % nx) * nz + z % nz) * nc + c % nc

    pairs = []
    for y in range(ny):
        for x in range(nx):
            for z in range(nz):
                for c in range(nc):
                    pairs.append((index(y, x, z, c), index(*target(y, x, z, c))))
    return lax.ppermute(value, BLK, pairs)


def from_shift(value, steps):
    count = lax.axis_size(BLK)
    return lax.ppermute(value, BLK, [(source, (source - steps) % count) for source in range(count)])


def from_far(value):
    count = lax.axis_size(BLK)
    return lax.ppermute(
        value, BLK, [(b, (b - 3 if b % 2 == 0 else b + 3) % count) for b in range(count)]
    )


def core_swap(value):
    return lax.ppermute(value, "core", [(0, 1), (1, 0)])


def shards(sizes, directions, axial_pos, azimuth, panel_area):
    count = axial_pos.shape[0]
    geometry = [part.reshape(count // LANES, LANES) for part in (axial_pos, azimuth, panel_area)]
    message = jnp.concatenate([directions] + geometry, axis=0)
    other = core_swap(message)
    ahead = from_shift(message, 2)
    far = from_far(message)
    pair = lax.ppermute(directions, "rhs", [(0, 1), (1, 0)])

    first, rows = home_tile(message, count)
    first = guest_tile(rows, other, (first,), count)
    first, ahead = lax.optimization_barrier((first, ahead))
    ahead_other = core_swap(ahead)
    late, ahead = lax.optimization_barrier((message, ahead))
    behind = from_shift(late, -2)
    second = guest_tile(rows, ahead, (), count)
    second = guest_tile(rows, ahead_other, (second,), count)
    first = guest_tile(rows, far, (first,), count)
    half = half_gram(message, pair, first, second)
    behind_other = core_swap(behind)

    core = lax.axis_index("core")
    keep = lax.dynamic_index_in_dim(half, core, 0, keepdims=False)
    value = keep + core_swap(lax.dynamic_index_in_dim(half, 1 - core, 0, keepdims=False))

    value, first, second = lax.optimization_barrier((value, first, second))
    crossed = lax.ppermute(value, ("core", "rhs"), [(2, 3), (3, 2)])
    product = guest_tile(rows, behind, (first, second), count, 0, 2)
    value, crossed, product = lax.optimization_barrier((value, crossed, product))
    value = value + jnp.where(core == 0, value, crossed).T

    work = (
        lambda product: guest_tile(rows, behind, (product, second), count, 1, 2),
        lambda product: guest_tile(rows, behind_other, (product,), count, 0, 2),
        lambda product: guest_tile(rows, behind_other, (product,), count, 1, 2),
    )
    stages = (
        [(0, 0, 1), (0, 0, -1), (0, 0, 2)],
        [(1, 0, 0), (-1, 0, 0), (2, 0, 0)],
        [(0, 0, 4), (0, 1, 0), (0, 1, 4)],
    )
    for stage, part in zip(stages, work):
        value, product = lax.optimization_barrier((value, product))
        moved = [
            along_blk(value, sizes, lambda y, x, z, c, d=d: (y + d[0], x + d[1], z + d[2], c)) for d in stage
        ]
        product = part(product)
        value, product, *moved = lax.optimization_barrier((value, product, *moved))
        value = (value + moved[0]) + (moved[1] + moved[2])
    value = value / (count * lax.axis_size(BLK))
    swapped = core_swap(value)
    upper = core == lax.axis_index("rhs")
    gram = jnp.concatenate([jnp.where(upper, value, swapped), jnp.where(upper, swapped, value)], axis=0)
    return product, gram


def solution(mesh):
    sizes = (4, 2, 8, 2)
    fine = Mesh(mesh.devices.reshape(sizes + (2,)), BLK + ("rhs",))
    in_specs = (P(BLK, "rhs"), P(BLK), P(BLK), P(BLK))
    out_specs = (P(BLK, "rhs"), P(None, "rhs"))
    return jax.shard_map(
        functools.partial(shards, sizes), mesh=fine, in_specs=in_specs, out_specs=out_specs, check_vma=False
    )
```

```python
import functools

import jax
import jax.numpy as jnp
from jax import lax
from jax.experimental import pallas as pl
from jax.experimental.pallas import tpu as pltpu
from jax.sharding import Mesh, PartitionSpec as P

LANES = 128
VMEM_BYTES = 12 * 2**20
ROW_STEP = 256
COL_STEP = 1024
PIECES = 4
BLK = ("y", "xh", "z", "core")


def split_parts(base):
    high = base.astype(jnp.bfloat16).astype(jnp.float32)
    rest = base - high
    mid = rest.astype(jnp.bfloat16).astype(jnp.float32)
    low = (rest - mid).astype(jnp.bfloat16).astype(jnp.float32)
    return high, mid, low


def point_values(axial, angle, area):
    axial = axial.astype(jnp.float32) - 4.0
    angle = angle.astype(jnp.float32)
    area = area.astype(jnp.float32)
    cos, sin = jnp.cos(angle), jnp.sin(angle)
    return axial, cos, sin, axial * axial + cos * cos + sin * sin, 1.0 / (area * area)


def lay_rows(base_ref, features):
    groups = features[0].shape[0]
    base_ref[...] = jnp.zeros_like(base_ref)
    for row, feature in enumerate(features):
        for group in range(groups):
            base_ref[row : row + 1, group * LANES : (group + 1) * LANES] = feature[group : group + 1, :]


def column_factors(geometry, base_ref, col_ref):
    axial, cos, sin, norm, scale = point_values(*geometry)
    lay_rows(base_ref, (scale, norm * scale, axial * scale, cos * scale, sin * scale))
    high, mid, low = split_parts(base_ref[...])
    col_ref[...] = jnp.concatenate([high, high, high, mid, mid, low], axis=0).astype(jnp.bfloat16)


def row_factors(geometry, base_ref, row_ref):
    axial, cos, sin, norm, scale = point_values(*geometry)
    count = base_ref.shape[1]
    scale = scale * count
    double = -2.0 * scale
    lay_rows(base_ref, ((norm + 0.01) * scale, scale, axial * double, cos * double, sin * double))
    high, mid, low = split_parts(base_ref[...])
    stacked = jnp.concatenate([high, mid, low, high, mid, high], axis=0)
    for group in range(count // LANES):
        part = stacked[:, group * LANES : (group + 1) * LANES]
        row_ref[group * LANES : (group + 1) * LANES, :] = part.T.astype(jnp.bfloat16)


def tile_product(row_ref, col_ref, message_ref, offset, out_ref):
    height, width = row_ref.shape[0], col_ref.shape[1]
    step_cols = min(COL_STEP, width)

    def step_fn(step, carried):
        start = pl.multiple_of(step * step_cols, step_cols)
        factor = col_ref[:, pl.ds(start, step_cols)]
        directions = message_ref[pl.ds(offset + start, step_cols), :]
        for low in range(0, height, ROW_STEP):
            rows = slice(low, low + ROW_STEP)
            inverse = jnp.dot(row_ref[rows, :], factor, preferred_element_type=jnp.float32)
            values = lax.rsqrt(inverse).astype(jnp.bfloat16)
            out_ref[rows, :] += jnp.dot(values, directions, preferred_element_type=jnp.float32)
        return carried

    lax.fori_loop(0, width // step_cols, step_fn, 0)


def message_geometry(message_ref, count, offset=0, width=None):
    groups = count // LANES
    part = slice(offset // LANES, (offset + (width or count)) // LANES)
    values = (message_ref[count + k * groups : count + (k + 1) * groups, :] for k in range(3))
    return tuple(value.astype(jnp.float32)[part] for value in values)


def home_body(message_ref, out_ref, row_ref, base_ref, col_ref):
    geometry = message_geometry(message_ref, row_ref.shape[0])
    row_factors(geometry, base_ref, row_ref)
    column_factors(geometry, base_ref, col_ref)
    out_ref[...] = jnp.zeros_like(out_ref)
    tile_product(row_ref, col_ref, message_ref, 0, out_ref)


def guest_body(offset, row_ref, message_ref, *refs):
    *total_refs, out_ref, base_ref, col_ref = refs
    column_factors(
        message_geometry(message_ref, row_ref.shape[0], offset, col_ref.shape[1]), base_ref, col_ref
    )
    if total_refs:
        if len(total_refs) > 1:
            out_ref[...] = total_refs[0][...] + total_refs[1][...]
    else:
        out_ref[...] = jnp.zeros_like(out_ref)
    tile_product(row_ref, col_ref, message_ref, offset, out_ref)


def tile_scratch(width):
    return [pltpu.VMEM((8, width), jnp.float32), pltpu.VMEM((48, width), jnp.bfloat16)]


def tile_cost(count):
    return pl.CostEstimate(flops=count * count * 128, bytes_accessed=0, transcendentals=0)


def near(value):
    return pltpu.with_memory_space_constraint(value, pltpu.VMEM)


def home_tile(message, count):
    vmem = pl.BlockSpec(memory_space=pltpu.VMEM)
    return pl.pallas_call(
        home_body,
        out_shape=[pltpu.VMEM((count, LANES), jnp.float32), pltpu.VMEM((count, 48), jnp.bfloat16)],
        in_specs=[vmem],
        out_specs=[vmem, vmem],
        scratch_shapes=tile_scratch(count),
        cost_estimate=tile_cost(count),
        compiler_params=pltpu.CompilerParams(vmem_limit_bytes=VMEM_BYTES),
        name="home_tile",
    )(near(message))


def guest_tile(rows, message, totals, piece=0, pieces=1):
    count = rows.shape[0]
    width = count // pieces
    vmem = pl.BlockSpec(memory_space=pltpu.VMEM)
    operands = [near(value) for value in (rows, message, *totals)]
    return pl.pallas_call(
        functools.partial(guest_body, piece * width),
        out_shape=pltpu.VMEM((count, LANES), jnp.float32),
        in_specs=[vmem] * len(operands),
        out_specs=vmem,
        input_output_aliases={2: 0} if totals else {},
        scratch_shapes=tile_scratch(width),
        cost_estimate=tile_cost(count),
        compiler_params=pltpu.CompilerParams(vmem_limit_bytes=VMEM_BYTES),
        name="guest_tile",
    )(*operands)


def half_gram_body(own_ref, pair_ref, first_ref, second_ref, out_ref):
    value = 0.5 * first_ref[...] + second_ref[...]
    high = value.astype(jnp.bfloat16)
    low = (value - high.astype(jnp.float32)).astype(jnp.bfloat16)
    both = jnp.concatenate([high, low], axis=1)
    for k, ref in enumerate((own_ref, pair_ref)):
        part = lax.dot_general(
            ref[: value.shape[0], :], both, (((0,), (0,)), ((), ())), preferred_element_type=jnp.float32
        )
        out_ref[k] = part[:, :LANES] + part[:, LANES:]


def half_gram(own, pair, first, second):
    vmem = pl.BlockSpec(memory_space=pltpu.VMEM)
    return pl.pallas_call(
        half_gram_body,
        out_shape=jax.ShapeDtypeStruct((2, LANES, LANES), jnp.float32),
        in_specs=[vmem] * 4,
        out_specs=vmem,
        cost_estimate=pl.CostEstimate(flops=2 * 2048 * 256 * 256, bytes_accessed=3 * 2**20, transcendentals=0),
        compiler_params=pltpu.CompilerParams(vmem_limit_bytes=VMEM_BYTES),
        name="half_gram",
    )(near(own), near(pair), near(first), near(second))


def along_blk(value, sizes, target):
    ny, nx, nz, nc = sizes

    def index(y, x, z, c):
        return ((y % ny * nx + x % nx) * nz + z % nz) * nc + c % nc

    pairs = []
    for y in range(ny):
        for x in range(nx):
            for z in range(nz):
                for c in range(nc):
                    pairs.append((index(y, x, z, c), index(*target(y, x, z, c))))
    return lax.ppermute(value, BLK, pairs)


def from_neighbour(value, parity):
    count = lax.axis_size(BLK)
    pairs = []
    for block in range(count):
        chip, core = divmod(block, 2)
        first = chip % 2 == parity
        other = 2 * (chip + 1) + 1 - core if first else 2 * (chip - 1) + core
        pairs.append((block, other % count))
    return lax.ppermute(value, BLK, pairs)


def from_far(value):
    count = lax.axis_size(BLK)
    return lax.ppermute(
        value, BLK, [(b, (b - 3 if b % 2 == 0 else b + 3) % count) for b in range(count)]
    )


def core_swap(value):
    return lax.ppermute(value, "core", [(0, 1), (1, 0)])


def shards(sizes, directions, axial_pos, azimuth, panel_area):
    count = axial_pos.shape[0]
    geometry = [part.reshape(count // LANES, LANES) for part in (axial_pos, azimuth, panel_area)]
    message = jnp.concatenate([directions] + geometry, axis=0)
    other = core_swap(message)
    even = from_neighbour(message, 0)
    odd = from_neighbour(message, 1)

    first, rows = home_tile(message, count)
    first, late = lax.optimization_barrier((first, message))
    far = from_far(late)
    first = guest_tile(rows, other, (first,))
    first, even, later = lax.optimization_barrier((first, even, directions))
    pair = lax.ppermute(later, "rhs", [(0, 1), (1, 0)])
    even_other = core_swap(even)
    second = guest_tile(rows, even, ())
    second, odd = lax.optimization_barrier((second, odd))
    odd_other = core_swap(odd)
    second = guest_tile(rows, odd, (second,))
    second, far = lax.optimization_barrier((second, far))
    first = guest_tile(rows, far, (first,))
    half = half_gram(message, pair, first, second)

    core = lax.axis_index("core")
    keep = lax.dynamic_index_in_dim(half, core, 0, keepdims=False)
    value = keep + core_swap(lax.dynamic_index_in_dim(half, 1 - core, 0, keepdims=False))

    value, first, second = lax.optimization_barrier((value, first, second))
    crossed = lax.ppermute(value, ("core", "rhs"), [(2, 3), (3, 2)])
    product = guest_tile(rows, even_other, (first, second), 0, PIECES)
    value, crossed, product = lax.optimization_barrier((value, crossed, product))
    value = value + jnp.where(core == 0, value, crossed).T

    work = [(even_other, piece) for piece in range(1, PIECES)] + [(odd_other, piece) for piece in range(PIECES)]
    stages = (
        ((0, 0, 4), 2), ((0, 0, 2), 1), ((0, 0, 1), 1), ((2, 0, 0), 1), ((1, 0, 0), 1), ((0, 1, 0), 1),
    )
    for move, pieces in stages:
        value, product = lax.optimization_barrier((value, product))
        moved = along_blk(
            value, sizes, lambda y, x, z, c, d=move: (y + d[0], x + d[1], z + d[2], c)
        )
        for _ in range(pieces):
            guest, piece = work.pop(0)
            product = guest_tile(rows, guest, (product,), piece, PIECES)
        value, product, moved = lax.optimization_barrier((value, product, moved))
        value = value + moved
    value = value / (count * lax.axis_size(BLK))
    swapped = core_swap(value)
    upper = core == lax.axis_index("rhs")
    gram = jnp.concatenate([jnp.where(upper, value, swapped), jnp.where(upper, swapped, value)], axis=0)
    return product, gram


def solution(mesh):
    sizes = (4, 2, 8, 2)
    fine = Mesh(mesh.devices.reshape(sizes + (2,)), BLK + ("rhs",))
    in_specs = (P(BLK, "rhs"), P(BLK), P(BLK), P(BLK))
    out_specs = (P(BLK, "rhs"), P(None, "rhs"))
    return jax.shard_map(
        functools.partial(shards, sizes), mesh=fine, in_specs=in_specs, out_specs=out_specs, check_vma=False
    )
```

```python
import functools

import jax
import jax.numpy as jnp
from jax import lax
from jax.experimental import pallas as pl
from jax.experimental.pallas import tpu as pltpu
from jax.sharding import Mesh, PartitionSpec as P

LANES = 128
VMEM_BYTES = 12 * 2**20
ROW_STEP = 256
COL_STEP = 1024
PIECES = 4
COPIES = 4
BLK = ("y", "xh", "z", "core")


def split_parts(base):
    high = base.astype(jnp.bfloat16).astype(jnp.float32)
    rest = base - high
    mid = rest.astype(jnp.bfloat16).astype(jnp.float32)
    low = (rest - mid).astype(jnp.bfloat16).astype(jnp.float32)
    return high, mid, low


def point_values(axial, angle, area):
    axial = axial.astype(jnp.float32) - 4.0
    angle = angle.astype(jnp.float32)
    area = area.astype(jnp.float32)
    cos, sin = jnp.cos(angle), jnp.sin(angle)
    return axial, cos, sin, axial * axial + cos * cos + sin * sin, 1.0 / (area * area)


def lay_rows(base_ref, features):
    groups = features[0].shape[0]
    base_ref[...] = jnp.zeros_like(base_ref)
    for row, feature in enumerate(features):
        for group in range(groups):
            base_ref[row : row + 1, group * LANES : (group + 1) * LANES] = feature[group : group + 1, :]


def column_factors(geometry, base_ref, col_ref):
    axial, cos, sin, norm, scale = point_values(*geometry)
    lay_rows(base_ref, (scale, norm * scale, axial * scale, cos * scale, sin * scale))
    high, mid, low = split_parts(base_ref[...])
    col_ref[...] = jnp.concatenate([high, high, high, mid, mid, low], axis=0).astype(jnp.bfloat16)


def row_factors(geometry, base_ref, row_ref):
    axial, cos, sin, norm, scale = point_values(*geometry)
    count = base_ref.shape[1]
    scale = scale * count
    double = -2.0 * scale
    lay_rows(base_ref, ((norm + 0.01) * scale, scale, axial * double, cos * double, sin * double))
    high, mid, low = split_parts(base_ref[...])
    stacked = jnp.concatenate([high, mid, low, high, mid, high], axis=0)
    for group in range(count // LANES):
        part = stacked[:, group * LANES : (group + 1) * LANES]
        row_ref[group * LANES : (group + 1) * LANES, :] = part.T.astype(jnp.bfloat16)


def tile_product(row_ref, col_ref, directions_ref, out_ref, offset=0, width=None, arrive=None):
    width = width or col_ref.shape[1]
    step_cols = min(COL_STEP, width)

    def step_fn(step, carried):
        start = pl.multiple_of(step * step_cols, step_cols)
        if arrive is not None:
            arrive(step)
        cols = pl.ds(offset + start, step_cols)
        factor, directions = col_ref[:, cols], directions_ref[cols, :]
        for low in range(0, row_ref.shape[0], ROW_STEP):
            rows = slice(low, low + ROW_STEP)
            inverse = jnp.dot(row_ref[rows, :], factor, preferred_element_type=jnp.float32)
            values = lax.rsqrt(inverse).astype(jnp.bfloat16)
            out_ref[rows, :] += jnp.dot(values, directions, preferred_element_type=jnp.float32)
        return carried

    lax.fori_loop(0, width // step_cols, step_fn, 0)


def geometry_of(ref):
    groups = ref.shape[0] // 3
    return tuple(ref[k * groups : (k + 1) * groups, :].astype(jnp.float32) for k in range(3))


def geometry_copy(message_ref, geometry_ref, sem):
    rows = geometry_ref.shape[0]
    return pltpu.make_async_copy(message_ref.at[pl.ds(message_ref.shape[0] - rows, rows)], geometry_ref, sem)


def pack_body(directions_ref, axial_ref, angle_ref, area_ref, out_ref, sems):
    count = directions_ref.shape[0]
    part = count // COPIES
    copies = [
        pltpu.make_async_copy(
            directions_ref.at[pl.ds(k * part, part)], out_ref.at[pl.ds(k * part, part)], sems.at[k]
        )
        for k in range(COPIES)
    ]
    for copy in copies:
        copy.start()
    groups = axial_ref.shape[0]
    for k, ref in enumerate((axial_ref, angle_ref, area_ref)):
        out_ref[count + k * groups : count + (k + 1) * groups, :] = ref[...]
    for copy in copies:
        copy.wait()


def home_body(message_ref, out_ref, row_ref, base_ref, col_ref):
    count = row_ref.shape[0]
    geometry = geometry_of(message_ref.at[pl.ds(count, message_ref.shape[0] - count)])
    row_factors(geometry, base_ref, row_ref)
    column_factors(geometry, base_ref, col_ref)
    out_ref[...] = jnp.zeros_like(out_ref)
    tile_product(row_ref, col_ref, message_ref, out_ref)


def guest_body(has_total, n_later, row_ref, message_ref, *refs):
    refs = list(refs)
    if has_total:
        refs.pop(0)
    later = [refs.pop(0) for _ in range(n_later)]
    out_ref = refs.pop(0)
    outs = [(refs.pop(0), refs.pop(0)) for _ in range(n_later)]
    base_ref, col_ref, directions_ref, geometry_ref, sems = refs
    part = min(COL_STEP, row_ref.shape[0])
    steps = row_ref.shape[0] // part

    def piece_copy(step):
        rows = pl.ds(pl.multiple_of(step * part, part), part)
        return pltpu.make_async_copy(message_ref.at[rows], directions_ref.at[rows], sems.at[step])

    first = geometry_copy(message_ref, geometry_ref.at[0], sems.at[steps])
    first.start()
    for step in range(steps):
        piece_copy(step).start()
    copies = []
    for k, (ref, (dirs, _)) in enumerate(zip(later, outs)):
        at = steps + 1 + 2 * k
        copies.append(geometry_copy(ref, geometry_ref.at[k + 1], sems.at[at]))
        copies.append(pltpu.make_async_copy(ref.at[pl.ds(0, dirs.shape[0])], dirs, sems.at[at + 1]))
    for copy in copies:
        copy.start()
    first.wait()
    column_factors(geometry_of(geometry_ref.at[0]), base_ref, col_ref)
    if not has_total:
        out_ref[...] = jnp.zeros_like(out_ref)
    tile_product(row_ref, col_ref, directions_ref, out_ref, arrive=lambda step: piece_copy(step).wait())
    for copy in copies:
        copy.wait()
    for k, (_, factors) in enumerate(outs):
        column_factors(geometry_of(geometry_ref.at[k + 1]), base_ref, factors)


def piece_body(offset, width, row_ref, col_ref, directions_ref, total_ref, out_ref):
    tile_product(row_ref, col_ref, directions_ref, out_ref, offset, width)


def half_gram_body(own_ref, pair_ref, first_ref, second_ref, out_ref, sum_ref, directions_ref, sem):
    copy = pltpu.make_async_copy(pair_ref, directions_ref, sem)
    copy.start()
    first, second = first_ref[...], second_ref[...]
    value = 0.5 * first + second
    high = value.astype(jnp.bfloat16)
    low = (value - high.astype(jnp.float32)).astype(jnp.bfloat16)
    both = jnp.concatenate([high, low], axis=1)
    for k, ref in enumerate((own_ref, directions_ref)):
        if k == 1:
            copy.wait()
        part = lax.dot_general(
            ref[: value.shape[0], :], both, (((0,), (0,)), ((), ())), preferred_element_type=jnp.float32
        )
        out_ref[k] = part[:, :LANES] + part[:, LANES:]
    sum_ref[...] = first + second


def tile_cost(count):
    return pl.CostEstimate(flops=count * count * 128, bytes_accessed=0, transcendentals=0)


def near(value):
    return pltpu.with_memory_space_constraint(value, pltpu.VMEM)


def kernel_call(body, name, operands, places, outs, scratch, cost, aliases=None):
    vmem = pl.BlockSpec(memory_space=pltpu.VMEM)
    anywhere = pl.BlockSpec(memory_space=pl.ANY)
    return pl.pallas_call(
        body,
        out_shape=[pltpu.VMEM(*out) for out in outs],
        in_specs=[vmem if place else anywhere for place in places],
        out_specs=[vmem] * len(outs),
        input_output_aliases=aliases or {},
        scratch_shapes=scratch,
        cost_estimate=cost,
        compiler_params=pltpu.CompilerParams(vmem_limit_bytes=VMEM_BYTES),
        name=name,
    )(*[near(value) if place else value for value, place in zip(operands, places)])


def pack(directions, geometry):
    count = directions.shape[0]
    out = (count + sum(part.shape[0] for part in geometry), LANES)
    return kernel_call(
        pack_body, "pack", [directions, *geometry], [False, True, True, True], [(out, jnp.bfloat16)],
        [pltpu.SemaphoreType.DMA((COPIES,))], pl.CostEstimate(flops=0, bytes_accessed=2**20, transcendentals=0),
    )[0]


def tile_scratch(count):
    return [pltpu.VMEM((8, count), jnp.float32), pltpu.VMEM((48, count), jnp.bfloat16)]


def home_tile(message, count):
    outs = [((count, LANES), jnp.float32), ((count, 48), jnp.bfloat16)]
    return kernel_call(home_body, "home_tile", [message], [True], outs, tile_scratch(count), tile_cost(count))


def guest_tile(rows, message, total=None, later=()):
    count = rows.shape[0]
    totals = [] if total is None else [total]
    scratch = tile_scratch(count) + [
        pltpu.VMEM((count, LANES), jnp.bfloat16),
        pltpu.VMEM((1 + len(later), message.shape[0] - count, LANES), jnp.bfloat16),
        pltpu.SemaphoreType.DMA((count // min(COL_STEP, count) + 1 + 2 * len(later),)),
    ]
    outs = [((count, LANES), jnp.float32)]
    outs += [((count, LANES), jnp.bfloat16), ((48, count), jnp.bfloat16)] * len(later)
    return kernel_call(
        functools.partial(guest_body, bool(totals), len(later)), "guest_tile", [rows, message, *totals, *later],
        [True, False] + [True] * len(totals) + [False] * len(later), outs, scratch, tile_cost(count),
        {2: 0} if totals else None,
    )


def piece_tile(rows, guest, total, piece):
    count = rows.shape[0]
    directions, factors = guest
    width = count // PIECES
    return kernel_call(
        functools.partial(piece_body, piece * width, width), "piece_tile", [rows, factors, directions, total],
        [True] * 4, [((count, LANES), jnp.float32)], [], tile_cost(count), {3: 0},
    )[0]


def half_gram(message, pair, first, second):
    count = first.shape[0]
    outs = [((2, LANES, LANES), jnp.float32), ((count, LANES), jnp.float32)]
    scratch = [pltpu.VMEM((count, LANES), jnp.bfloat16), pltpu.SemaphoreType.DMA]
    return kernel_call(
        half_gram_body, "half_gram", [message, pair, first, second], [True, False, True, True], outs, scratch,
        tile_cost(count), {2: 1},
    )


def along_blk(value, sizes, target):
    ny, nx, nz, nc = sizes

    def index(y, x, z, c):
        return ((y % ny * nx + x % nx) * nz + z % nz) * nc + c % nc

    pairs = []
    for y in range(ny):
        for x in range(nx):
            for z in range(nz):
                for c in range(nc):
                    pairs.append((index(y, x, z, c), index(*target(y, x, z, c))))
    return lax.ppermute(value, BLK, pairs)


def from_neighbour(value, parity):
    count = lax.axis_size(BLK)
    pairs = []
    for block in range(count):
        chip, core = divmod(block, 2)
        first = chip % 2 == parity
        other = 2 * (chip + 1) + 1 - core if first else 2 * (chip - 1) + core
        pairs.append((block, other % count))
    return lax.ppermute(value, BLK, pairs)


def from_far(value):
    count = lax.axis_size(BLK)
    return lax.ppermute(
        value, BLK, [(b, (b - 3 if b % 2 == 0 else b + 3) % count) for b in range(count)]
    )


def core_swap(value):
    return lax.ppermute(value, "core", [(0, 1), (1, 0)])


def shards(sizes, directions, axial_pos, azimuth, panel_area):
    count = axial_pos.shape[0]
    geometry = [part.reshape(count // LANES, LANES) for part in (axial_pos, azimuth, panel_area)]
    message = pack(directions, geometry)
    other = core_swap(message)
    even = from_neighbour(message, 0)
    odd = from_neighbour(message, 1)

    first, rows = home_tile(message, count)
    first, late = lax.optimization_barrier((first, message))
    far = from_far(late)
    (first,) = guest_tile(rows, other, first)
    first, even, later = lax.optimization_barrier((first, even, directions))
    pair = lax.ppermute(later, "rhs", [(0, 1), (1, 0)])
    even_other = core_swap(even)
    (second,) = guest_tile(rows, even)
    second, odd = lax.optimization_barrier((second, odd))
    odd_other = core_swap(odd)
    (second,) = guest_tile(rows, odd, second)
    second, far = lax.optimization_barrier((second, far))
    first, *fetched = guest_tile(rows, far, first, (even_other, odd_other))
    even_other, odd_other = tuple(fetched[:2]), tuple(fetched[2:])
    half, product = half_gram(message, pair, first, second)

    core = lax.axis_index("core")
    keep = lax.dynamic_index_in_dim(half, core, 0, keepdims=False)
    value = keep + core_swap(lax.dynamic_index_in_dim(half, 1 - core, 0, keepdims=False))

    value, product = lax.optimization_barrier((value, product))
    crossed = lax.ppermute(value, ("core", "rhs"), [(2, 3), (3, 2)])
    product = piece_tile(rows, even_other, product, 0)
    value, crossed, product = lax.optimization_barrier((value, crossed, product))
    value = value + jnp.where(core == 0, value, crossed).T

    work = [(even_other, piece) for piece in range(1, PIECES)] + [(odd_other, piece) for piece in range(PIECES)]
    stages = (
        ((0, 0, 4), 2), ((0, 0, 2), 1), ((0, 0, 1), 1), ((2, 0, 0), 1), ((1, 0, 0), 1), ((0, 1, 0), 1),
    )
    for move, pieces in stages:
        value, product = lax.optimization_barrier((value, product))
        moved = along_blk(
            value, sizes, lambda y, x, z, c, d=move: (y + d[0], x + d[1], z + d[2], c)
        )
        for _ in range(pieces):
            guest, piece = work.pop(0)
            product = piece_tile(rows, guest, product, piece)
        value, product, moved = lax.optimization_barrier((value, product, moved))
        value = value + moved
    value = value / (count * lax.axis_size(BLK))
    swapped = core_swap(value)
    upper = core == lax.axis_index("rhs")
    gram = jnp.concatenate([jnp.where(upper, value, swapped), jnp.where(upper, swapped, value)], axis=0)
    return product, gram


def solution(mesh):
    sizes = (4, 2, 8, 2)
    fine = Mesh(mesh.devices.reshape(sizes + (2,)), BLK + ("rhs",))
    in_specs = (P(BLK, "rhs"), P(BLK), P(BLK), P(BLK))
    out_specs = (P(BLK, "rhs"), P(None, "rhs"))
    return jax.shard_map(
        functools.partial(shards, sizes), mesh=fine, in_specs=in_specs, out_specs=out_specs, check_vma=False
    )
```

```python
import functools

import jax
import jax.numpy as jnp
from jax import lax
from jax.experimental import pallas as pl
from jax.experimental.pallas import tpu as pltpu
from jax.sharding import Mesh, PartitionSpec as P

LANES = 128
VMEM_BYTES = 12 * 2**20
ROW_STEP = 256
COL_STEP = 1024
PIECES = 4
PIECE_ROWS = 1024
COPIES = 4
BLK = ("y", "xh", "z", "core")


def split_parts(base):
    high = base.astype(jnp.bfloat16).astype(jnp.float32)
    rest = base - high
    mid = rest.astype(jnp.bfloat16).astype(jnp.float32)
    low = (rest - mid).astype(jnp.bfloat16).astype(jnp.float32)
    return high, mid, low


def point_values(axial, angle, area):
    axial = axial.astype(jnp.float32) - 4.0
    angle = angle.astype(jnp.float32)
    area = area.astype(jnp.float32)
    cos, sin = jnp.cos(angle), jnp.sin(angle)
    return axial, cos, sin, axial * axial + cos * cos + sin * sin, 1.0 / (area * area)


def lay_rows(base_ref, features):
    groups = features[0].shape[0]
    base_ref[...] = jnp.zeros_like(base_ref)
    for row, feature in enumerate(features):
        for group in range(groups):
            base_ref[row : row + 1, group * LANES : (group + 1) * LANES] = feature[group : group + 1, :]


def column_factors(geometry, base_ref, col_ref):
    axial, cos, sin, norm, scale = point_values(*geometry)
    lay_rows(base_ref, (scale, norm * scale, axial * scale, cos * scale, sin * scale))
    high, mid, low = split_parts(base_ref[...])
    col_ref[...] = jnp.concatenate([high, high, high, mid, mid, low], axis=0).astype(jnp.bfloat16)


def row_factors(geometry, base_ref, row_ref):
    axial, cos, sin, norm, scale = point_values(*geometry)
    count = base_ref.shape[1]
    scale = scale * count
    double = -2.0 * scale
    lay_rows(base_ref, ((norm + 0.01) * scale, scale, axial * double, cos * double, sin * double))
    high, mid, low = split_parts(base_ref[...])
    stacked = jnp.concatenate([high, mid, low, high, mid, high], axis=0)
    for group in range(count // LANES):
        part = stacked[:, group * LANES : (group + 1) * LANES]
        row_ref[group * LANES : (group + 1) * LANES, :] = part.T.astype(jnp.bfloat16)


def tile_product(row_ref, col_ref, directions_ref, out_ref, offset=0, width=None, arrive=None, row_step=ROW_STEP):
    width = width or col_ref.shape[1]
    step_cols = min(COL_STEP, width)

    def step_fn(step, carried):
        start = pl.multiple_of(step * step_cols, step_cols)
        if arrive is not None:
            arrive(step)
        cols = pl.ds(offset + start, step_cols)
        factor, directions = col_ref[:, cols], directions_ref[cols, :]
        for low in range(0, row_ref.shape[0], row_step):
            rows = slice(low, low + row_step)
            inverse = jnp.dot(row_ref[rows, :], factor, preferred_element_type=jnp.float32)
            values = lax.rsqrt(inverse).astype(jnp.bfloat16)
            out_ref[rows, :] += jnp.dot(values, directions, preferred_element_type=jnp.float32)
        return carried

    lax.fori_loop(0, width // step_cols, step_fn, 0)


def geometry_of(ref):
    groups = ref.shape[0] // 3
    return tuple(ref[k * groups : (k + 1) * groups, :].astype(jnp.float32) for k in range(3))


def geometry_copy(message_ref, geometry_ref, sem):
    rows = geometry_ref.shape[0]
    return pltpu.make_async_copy(message_ref.at[pl.ds(message_ref.shape[0] - rows, rows)], geometry_ref, sem)


def pack_body(directions_ref, axial_ref, angle_ref, area_ref, out_ref, sems):
    count = directions_ref.shape[0]
    part = count // COPIES
    copies = [
        pltpu.make_async_copy(
            directions_ref.at[pl.ds(k * part, part)], out_ref.at[pl.ds(k * part, part)], sems.at[k]
        )
        for k in range(COPIES)
    ]
    groups = axial_ref.shape[0]
    for k, ref in enumerate((axial_ref, angle_ref, area_ref)):
        rows = out_ref.at[pl.ds(count + k * groups, groups)]
        copies.append(pltpu.make_async_copy(ref, rows, sems.at[COPIES + k]))
    for copy in copies:
        copy.start()
    for copy in copies:
        copy.wait()


def home_body(message_ref, out_ref, row_ref, base_ref, col_ref):
    count = row_ref.shape[0]
    geometry = geometry_of(message_ref.at[pl.ds(count, message_ref.shape[0] - count)])
    row_factors(geometry, base_ref, row_ref)
    column_factors(geometry, base_ref, col_ref)
    out_ref[...] = jnp.zeros_like(out_ref)
    tile_product(row_ref, col_ref, message_ref, out_ref)


def guest_body(has_total, n_held, n_later, row_ref, message_ref, *refs):
    refs = list(refs)
    del refs[: has_total + n_held]
    later = [refs.pop(0) for _ in range(n_later)]
    out_ref = refs.pop(0)
    del refs[:n_held]
    outs = [refs.pop(0) for _ in range(n_later)]
    base_ref, col_ref, directions_ref, geometry_ref, sems = refs
    part = min(COL_STEP, row_ref.shape[0])
    steps = row_ref.shape[0] // part

    def piece_copy(step):
        rows = pl.ds(pl.multiple_of(step * part, part), part)
        return pltpu.make_async_copy(message_ref.at[rows], directions_ref.at[rows], sems.at[step])

    copies = [
        geometry_copy(ref, geometry_ref.at[k], sems.at[steps + k]) for k, ref in enumerate([message_ref, *later])
    ]
    copies[0].start()
    for step in range(steps):
        piece_copy(step).start()
    for copy in copies[1:]:
        copy.start()
    copies[0].wait()
    column_factors(geometry_of(geometry_ref.at[0]), base_ref, col_ref)
    if not has_total:
        out_ref[...] = jnp.zeros_like(out_ref)
    tile_product(row_ref, col_ref, directions_ref, out_ref, arrive=lambda step: piece_copy(step).wait())
    for k, factors in enumerate(outs):
        copies[k + 1].wait()
        column_factors(geometry_of(geometry_ref.at[k + 1]), base_ref, factors)


def piece_body(offset, last, row_ref, col_ref, message_ref, total_ref, out_ref, directions_ref, sem):
    width = directions_ref.shape[0]
    copy = pltpu.make_async_copy(message_ref.at[pl.ds(offset, width)], directions_ref, sem)
    copy.start()
    factor = col_ref[:, offset : offset + width]
    for low in range(0, row_ref.shape[0], PIECE_ROWS):
        rows = slice(low, low + PIECE_ROWS)
        inverse = jnp.dot(row_ref[rows, :], factor, preferred_element_type=jnp.float32)
        values = lax.rsqrt(inverse).astype(jnp.bfloat16)
        if low == 0:
            copy.wait()
        part = jnp.dot(values, directions_ref[...], preferred_element_type=jnp.float32)
        if last:
            out_ref[rows, :] = total_ref[rows, :] + part
        else:
            out_ref[rows, :] += part


def fold_body(core_ref, value_ref, crossed_ref, out_ref):
    first = core_ref[0] == 0

    @pl.when(first)
    def _():
        out_ref[...] = value_ref[...] + value_ref[...].T

    @pl.when(jnp.logical_not(first))
    def _():
        out_ref[...] = value_ref[...] + crossed_ref[...].T


def half_gram_body(
    core_ref, own_ref, pair_ref, first_ref, second_ref, keep_ref, give_ref, sum_ref, directions_ref, sems
):
    copies = [
        pltpu.make_async_copy(ref, directions_ref.at[k], sems.at[k]) for k, ref in enumerate((own_ref, pair_ref))
    ]
    for copy in copies:
        copy.start()
    first, second = first_ref[...], second_ref[...]
    value = 0.5 * first + second
    sum_ref[...] = first + second
    high = value.astype(jnp.bfloat16)
    low = (value - high.astype(jnp.float32)).astype(jnp.bfloat16)
    both = jnp.concatenate([high, low], axis=1)
    blocks = []
    for k, copy in enumerate(copies):
        copy.wait()
        part = lax.dot_general(
            directions_ref[k], both, (((0,), (0,)), ((), ())), preferred_element_type=jnp.float32
        )
        blocks.append(part[:, :LANES] + part[:, LANES:])
    on_first = core_ref[0] == 0
    keep_ref[...] = jnp.where(on_first, blocks[0], blocks[1])
    give_ref[...] = jnp.where(on_first, blocks[1], blocks[0])


def tile_cost(count):
    return pl.CostEstimate(flops=count * count * 16, bytes_accessed=0, transcendentals=0)


def kernel_call(body, name, operands, places, outs, scratch, cost, aliases=None):
    spaces = {"v": pltpu.VMEM, "s": pltpu.SMEM, "a": pl.ANY, "h": pltpu.HBM}
    fixed = {"v": pltpu.VMEM, "h": pltpu.HBM}
    operands = [
        pltpu.with_memory_space_constraint(value, fixed[place]) if place in fixed else value
        for value, place in zip(operands, places)
    ]
    return pl.pallas_call(
        body,
        out_shape=outs,
        in_specs=[pl.BlockSpec(memory_space=spaces[place]) for place in places],
        out_specs=[pl.BlockSpec(memory_space=pltpu.VMEM)] * len(outs),
        input_output_aliases=aliases or {},
        scratch_shapes=scratch,
        cost_estimate=cost,
        compiler_params=pltpu.CompilerParams(vmem_limit_bytes=VMEM_BYTES),
        name=name,
    )(*operands)


def pack(directions, geometry):
    count = directions.shape[0]
    out = (count + sum(part.shape[0] for part in geometry), LANES)
    return kernel_call(
        pack_body, "pack", [directions, *geometry], "hhhh", [pltpu.VMEM(out, jnp.bfloat16)],
        [pltpu.SemaphoreType.DMA((COPIES + 3,))], pl.CostEstimate(flops=0, bytes_accessed=2**20, transcendentals=0),
    )[0]


def tile_scratch(count):
    return [pltpu.VMEM((8, count), jnp.float32), pltpu.VMEM((48, count), jnp.bfloat16)]


def home_tile(message, count):
    outs = [pltpu.VMEM((count, LANES), jnp.float32), pltpu.VMEM((count, 48), jnp.bfloat16)]
    return kernel_call(home_body, "home_tile", [message], "v", outs, tile_scratch(count), tile_cost(count))


def guest_tile(rows, message, total=None, held=(), later=(), place="h"):
    count = rows.shape[0]
    totals = [] if total is None else [total]
    scratch = tile_scratch(count) + [
        pltpu.VMEM((count, LANES), jnp.bfloat16),
        pltpu.VMEM((1 + len(later), message.shape[0] - count, LANES), jnp.bfloat16),
        pltpu.SemaphoreType.DMA((count // min(COL_STEP, count) + 1 + len(later),)),
    ]
    outs = [pltpu.VMEM((count, LANES), jnp.float32)] * (1 + len(held))
    outs += [pltpu.VMEM((48, count), jnp.bfloat16)] * len(later)
    aliases = {2: 0} if totals else {}
    aliases.update({2 + len(totals) + k: 1 + k for k in range(len(held))})
    return kernel_call(
        functools.partial(guest_body, len(totals), len(held), len(later)), "guest_tile",
        [rows, message, *totals, *held, *later],
        "v" + place + "v" * (len(totals) + len(held)) + "h" * len(later),
        outs, scratch, tile_cost(count), aliases,
    )


def piece_tile(rows, guest, total, piece, last):
    count = rows.shape[0]
    message, factors = guest
    width = count // PIECES
    out = jax.ShapeDtypeStruct if last else pltpu.VMEM
    return kernel_call(
        functools.partial(piece_body, piece * width, last), "piece_tile", [rows, factors, message, total], "vvhv",
        [out((count, LANES), jnp.float32)], [pltpu.VMEM((width, LANES), jnp.bfloat16), pltpu.SemaphoreType.DMA],
        tile_cost(count), None if last else {3: 0},
    )[0]


def half_gram(core, own, pair, first, second):
    count = first.shape[0]
    block = pltpu.VMEM((LANES, LANES), jnp.float32)
    return kernel_call(
        half_gram_body, "half_gram", [core, own, pair, first, second], "shhvv",
        [block, block, pltpu.VMEM((count, LANES), jnp.float32)],
        [pltpu.VMEM((2, count, LANES), jnp.bfloat16), pltpu.SemaphoreType.DMA((2,))], tile_cost(count), {3: 2},
    )


def fold(core, value, crossed):
    out = pltpu.VMEM((LANES, LANES), jnp.float32)
    cost = pl.CostEstimate(flops=0, bytes_accessed=2**17, transcendentals=0)
    return kernel_call(fold_body, "fold", [core, value, crossed], "svv", [out], [], cost)[0]


def along_blk(value, sizes, target):
    ny, nx, nz, nc = sizes

    def index(y, x, z, c):
        return ((y % ny * nx + x % nx) * nz + z % nz) * nc + c % nc

    pairs = []
    for y in range(ny):
        for x in range(nx):
            for z in range(nz):
                for c in range(nc):
                    pairs.append((index(y, x, z, c), index(*target(y, x, z, c))))
    return lax.ppermute(value, BLK, pairs)


def from_neighbour(value, parity):
    count = lax.axis_size(BLK)
    pairs = []
    for block in range(count):
        chip, core = divmod(block, 2)
        first = chip % 2 == parity
        other = 2 * (chip + 1) + 1 - core if first else 2 * (chip - 1) + core
        pairs.append((block, other % count))
    return lax.ppermute(value, BLK, pairs)


def from_far(value):
    count = lax.axis_size(BLK)
    return lax.ppermute(
        value, BLK, [(b, (b - 3 if b % 2 == 0 else b + 3) % count) for b in range(count)]
    )


def core_swap(value):
    return lax.ppermute(value, "core", [(0, 1), (1, 0)])


def shards(sizes, directions, axial_pos, azimuth, panel_area):
    count = axial_pos.shape[0]
    geometry = [part.reshape(count // LANES, LANES) for part in (axial_pos, azimuth, panel_area)]
    message = pack(directions, geometry)
    other = core_swap(message)
    even = from_neighbour(message, 0)
    odd = from_neighbour(message, 1)

    first, rows = home_tile(message, count)
    first, late = lax.optimization_barrier((first, message))
    far = from_far(late)
    (first,) = guest_tile(rows, other, first, place="a")
    first, even, later = lax.optimization_barrier((first, even, directions))
    pair = lax.ppermute(later, "rhs", [(0, 1), (1, 0)])
    even_other = core_swap(even)
    second, first = guest_tile(rows, even, None, (first,), place="a")
    second, odd = lax.optimization_barrier((second, odd))
    odd_other = core_swap(odd)
    second, first = guest_tile(rows, odd, second, (first,))
    second, far = lax.optimization_barrier((second, far))
    first, second, *factors = guest_tile(rows, far, first, (second,), (even_other, odd_other))
    core = lax.axis_index("core").astype(jnp.int32)
    keep, give, product = half_gram(core.reshape(1), directions, pair, first, second)

    value = keep + core_swap(give)
    value, product = lax.optimization_barrier((value, product))
    crossed = lax.ppermute(value, ("core", "rhs"), [(2, 3), (3, 2)])
    work = [(guest, piece) for guest in zip((even_other, odd_other), factors) for piece in range(PIECES)]

    def advance(product):
        guest, piece = work.pop(0)
        return piece_tile(rows, guest, product, piece, not work)

    product = advance(product)
    value, crossed, product = lax.optimization_barrier((value, crossed, product))
    value = fold(core.reshape(1), value, crossed)

    stages = (
        ((0, 0, 4), 2), ((0, 0, 2), 1), ((0, 0, 1), 1), ((2, 0, 0), 1), ((1, 0, 0), 1), ((0, 1, 0), 1),
    )
    for move, pieces in stages:
        sent = value.astype(jnp.bfloat16)
        value, product, sent = lax.optimization_barrier((value, product, sent))
        moved = along_blk(
            sent, sizes, lambda y, x, z, c, d=move: (y + d[0], x + d[1], z + d[2], c)
        )
        for _ in range(pieces):
            product = advance(product)
        sent, product, moved = lax.optimization_barrier((sent, product, moved))
        value = sent.astype(jnp.float32) + moved.astype(jnp.float32)
    value = value / (count * lax.axis_size(BLK))
    swapped = core_swap(value)
    upper = core == lax.axis_index("rhs")
    gram = jnp.concatenate([jnp.where(upper, value, swapped), jnp.where(upper, swapped, value)], axis=0)
    return product, gram


def solution(mesh):
    sizes = (4, 2, 8, 2)
    fine = Mesh(mesh.devices.reshape(sizes + (2,)), BLK + ("rhs",))
    in_specs = (P(BLK, "rhs"), P(BLK), P(BLK), P(BLK))
    out_specs = (P(BLK, "rhs"), P(None, "rhs"))
    return jax.shard_map(
        functools.partial(shards, sizes), mesh=fine, in_specs=in_specs, out_specs=out_specs, check_vma=False
    )
```

```python
import functools

import jax
import jax.numpy as jnp
from jax import lax
from jax.experimental import pallas as pl
from jax.experimental.pallas import tpu as pltpu
from jax.sharding import Mesh, PartitionSpec as P

LANES = 128
VMEM_BYTES = 12 * 2**20
ROW_STEP = 256
COL_STEP = 1024
PIECES = 4
PIECE_ROWS = 1024
COPIES = 4
BLK = ("y", "xh", "z", "core")


def split_parts(base):
    high = base.astype(jnp.bfloat16).astype(jnp.float32)
    rest = base - high
    mid = rest.astype(jnp.bfloat16).astype(jnp.float32)
    low = (rest - mid).astype(jnp.bfloat16).astype(jnp.float32)
    return high, mid, low


def point_values(axial, angle, area):
    axial = axial.astype(jnp.float32) - 4.0
    angle = angle.astype(jnp.float32)
    area = area.astype(jnp.float32)
    cos, sin = jnp.cos(angle), jnp.sin(angle)
    return axial, cos, sin, axial * axial + cos * cos + sin * sin, 1.0 / (area * area)


def lay_rows(base_ref, features):
    groups = features[0].shape[0]
    base_ref[...] = jnp.zeros_like(base_ref)
    for row, feature in enumerate(features):
        for group in range(groups):
            base_ref[row : row + 1, group * LANES : (group + 1) * LANES] = feature[group : group + 1, :]


def column_factors(geometry, base_ref, col_ref):
    axial, cos, sin, norm, scale = point_values(*geometry)
    lay_rows(base_ref, (scale, norm * scale, axial * scale, cos * scale, sin * scale))
    high, mid, low = split_parts(base_ref[...])
    col_ref[...] = jnp.concatenate([high, high, high, mid, mid, low], axis=0).astype(jnp.bfloat16)


def row_factors(geometry, base_ref, row_ref):
    axial, cos, sin, norm, scale = point_values(*geometry)
    count = base_ref.shape[1]
    scale = scale * count
    double = -2.0 * scale
    lay_rows(base_ref, ((norm + 0.01) * scale, scale, axial * double, cos * double, sin * double))
    high, mid, low = split_parts(base_ref[...])
    stacked = jnp.concatenate([high, mid, low, high, mid, high], axis=0)
    for group in range(count // LANES):
        part = stacked[:, group * LANES : (group + 1) * LANES]
        row_ref[group * LANES : (group + 1) * LANES, :] = part.T.astype(jnp.bfloat16)


def tile_product(row_ref, col_ref, directions_ref, out_ref, offset=0, width=None, arrive=None, row_step=ROW_STEP):
    width = width or col_ref.shape[1]
    step_cols = min(COL_STEP, width)

    def step_fn(step, carried):
        start = pl.multiple_of(step * step_cols, step_cols)
        if arrive is not None:
            arrive(step)
        cols = pl.ds(offset + start, step_cols)
        factor, directions = col_ref[:, cols], directions_ref[cols, :]
        for low in range(0, row_ref.shape[0], row_step):
            rows = slice(low, low + row_step)
            inverse = jnp.dot(row_ref[rows, :], factor, preferred_element_type=jnp.float32)
            values = lax.rsqrt(inverse).astype(jnp.bfloat16)
            out_ref[rows, :] += jnp.dot(values, directions, preferred_element_type=jnp.float32)
        return carried

    lax.fori_loop(0, width // step_cols, step_fn, 0)


def geometry_of(ref):
    groups = ref.shape[0] // 3
    return tuple(ref[k * groups : (k + 1) * groups, :].astype(jnp.float32) for k in range(3))


def geometry_copy(message_ref, geometry_ref, sem):
    rows = geometry_ref.shape[0]
    return pltpu.make_async_copy(message_ref.at[pl.ds(message_ref.shape[0] - rows, rows)], geometry_ref, sem)


def pack_body(directions_ref, axial_ref, angle_ref, area_ref, out_ref, sems):
    count = directions_ref.shape[0]
    part = count // COPIES
    copies = [
        pltpu.make_async_copy(
            directions_ref.at[pl.ds(k * part, part)], out_ref.at[pl.ds(k * part, part)], sems.at[k]
        )
        for k in range(COPIES)
    ]
    groups = axial_ref.shape[0]
    for k, ref in enumerate((axial_ref, angle_ref, area_ref)):
        rows = out_ref.at[pl.ds(count + k * groups, groups)]
        copies.append(pltpu.make_async_copy(ref, rows, sems.at[COPIES + k]))
    for copy in copies:
        copy.start()
    for copy in copies:
        copy.wait()


def home_body(message_ref, out_ref, row_ref, base_ref, col_ref):
    count = row_ref.shape[0]
    geometry = geometry_of(message_ref.at[pl.ds(count, message_ref.shape[0] - count)])
    row_factors(geometry, base_ref, row_ref)
    column_factors(geometry, base_ref, col_ref)
    out_ref[...] = jnp.zeros_like(out_ref)
    tile_product(row_ref, col_ref, message_ref, out_ref)


def guest_body(has_total, n_held, row_ref, message_ref, *refs):
    out_ref, *refs = refs[has_total + n_held :]
    base_ref, col_ref, directions_ref, geometry_ref, sems = refs[n_held:]
    part = min(COL_STEP, row_ref.shape[0])
    steps = row_ref.shape[0] // part

    def piece_copy(step):
        rows = pl.ds(pl.multiple_of(step * part, part), part)
        return pltpu.make_async_copy(message_ref.at[rows], directions_ref.at[rows], sems.at[step])

    geometry = geometry_copy(message_ref, geometry_ref, sems.at[steps])
    geometry.start()
    for step in range(steps):
        piece_copy(step).start()
    geometry.wait()
    column_factors(geometry_of(geometry_ref), base_ref, col_ref)
    if not has_total:
        out_ref[...] = jnp.zeros_like(out_ref)
    tile_product(row_ref, col_ref, directions_ref, out_ref, arrive=lambda step: piece_copy(step).wait())


def piece_body(offset, last, row_ref, message_ref, total_ref, out_ref, base_ref, col_ref, directions_ref, geometry_ref, sems):
    width = directions_ref.shape[0]
    geometry = geometry_copy(message_ref, geometry_ref, sems.at[0])
    copy = pltpu.make_async_copy(message_ref.at[pl.ds(offset, width)], directions_ref, sems.at[1])
    geometry.start()
    copy.start()
    geometry.wait()
    part = slice(offset // LANES, (offset + width) // LANES)
    column_factors([value[part] for value in geometry_of(geometry_ref)], base_ref, col_ref)
    for low in range(0, row_ref.shape[0], PIECE_ROWS):
        rows = slice(low, low + PIECE_ROWS)
        inverse = jnp.dot(row_ref[rows, :], col_ref[...], preferred_element_type=jnp.float32)
        values = lax.rsqrt(inverse).astype(jnp.bfloat16)
        if low == 0:
            copy.wait()
        part = jnp.dot(values, directions_ref[...], preferred_element_type=jnp.float32)
        if last:
            out_ref[rows, :] = total_ref[rows, :] + part
        else:
            out_ref[rows, :] += part


def fold_body(core_ref, keep_ref, swapped_ref, crossed_ref, far_crossed_ref, out_ref):
    first = core_ref[0] == 0
    value = keep_ref[...] + swapped_ref[...]

    @pl.when(first)
    def _():
        out_ref[...] = value + value.T

    @pl.when(jnp.logical_not(first))
    def _():
        out_ref[...] = value + (crossed_ref[...] + far_crossed_ref[...]).T


def half_gram_body(
    core_ref, own_ref, pair_ref, first_ref, second_ref, keep_ref, give_ref, sum_ref, directions_ref, sems
):
    copies = [
        pltpu.make_async_copy(ref, directions_ref.at[k], sems.at[k]) for k, ref in enumerate((own_ref, pair_ref))
    ]
    for copy in copies:
        copy.start()
    first, second = first_ref[...], second_ref[...]
    value = 0.5 * first + second
    sum_ref[...] = first + second
    high = value.astype(jnp.bfloat16)
    low = (value - high.astype(jnp.float32)).astype(jnp.bfloat16)
    both = jnp.concatenate([high, low], axis=1)
    blocks = []
    for k, copy in enumerate(copies):
        copy.wait()
        part = lax.dot_general(
            directions_ref[k], both, (((0,), (0,)), ((), ())), preferred_element_type=jnp.float32
        )
        blocks.append(part[:, :LANES] + part[:, LANES:])
    on_first = core_ref[0] == 0
    keep_ref[...] = jnp.where(on_first, blocks[0], blocks[1])
    give_ref[...] = jnp.where(on_first, blocks[1], blocks[0])


def tile_cost(count):
    return pl.CostEstimate(flops=count * count * 16, bytes_accessed=0, transcendentals=0)


def kernel_call(body, name, operands, places, outs, scratch, cost, aliases=None):
    spaces = {"v": pltpu.VMEM, "s": pltpu.SMEM, "a": pl.ANY, "h": pltpu.HBM}
    fixed = {"v": pltpu.VMEM, "h": pltpu.HBM}
    operands = [
        pltpu.with_memory_space_constraint(value, fixed[place]) if place in fixed else value
        for value, place in zip(operands, places)
    ]
    return pl.pallas_call(
        body,
        out_shape=outs,
        in_specs=[pl.BlockSpec(memory_space=spaces[place]) for place in places],
        out_specs=[pl.BlockSpec(memory_space=pltpu.VMEM)] * len(outs),
        input_output_aliases=aliases or {},
        scratch_shapes=scratch,
        cost_estimate=cost,
        compiler_params=pltpu.CompilerParams(vmem_limit_bytes=VMEM_BYTES),
        name=name,
    )(*operands)


def pack(directions, geometry):
    count = directions.shape[0]
    out = (count + sum(part.shape[0] for part in geometry), LANES)
    return kernel_call(
        pack_body, "pack", [directions, *geometry], "hhhh", [pltpu.VMEM(out, jnp.bfloat16)],
        [pltpu.SemaphoreType.DMA((COPIES + 3,))], pl.CostEstimate(flops=0, bytes_accessed=2**20, transcendentals=0),
    )[0]


def tile_scratch(count):
    return [pltpu.VMEM((8, count), jnp.float32), pltpu.VMEM((48, count), jnp.bfloat16)]


def home_tile(message, count):
    outs = [pltpu.VMEM((count, LANES), jnp.float32), pltpu.VMEM((count, 48), jnp.bfloat16)]
    return kernel_call(home_body, "home_tile", [message], "v", outs, tile_scratch(count), tile_cost(count))


def guest_tile(rows, message, total=None, held=()):
    count = rows.shape[0]
    totals = [] if total is None else [total]
    scratch = tile_scratch(count) + [
        pltpu.VMEM((count, LANES), jnp.bfloat16),
        pltpu.VMEM((message.shape[0] - count, LANES), jnp.bfloat16),
        pltpu.SemaphoreType.DMA((count // min(COL_STEP, count) + 1,)),
    ]
    aliases = {2: 0} if totals else {}
    aliases.update({2 + len(totals) + k: 1 + k for k in range(len(held))})
    return kernel_call(
        functools.partial(guest_body, len(totals), len(held)), "guest_tile", [rows, message, *totals, *held],
        "va" + "v" * (len(totals) + len(held)), [pltpu.VMEM((count, LANES), jnp.float32)] * (1 + len(held)),
        scratch, tile_cost(count), aliases,
    )


def piece_tile(rows, message, total, piece, last):
    count = rows.shape[0]
    width = count // PIECES
    out = jax.ShapeDtypeStruct if last else pltpu.VMEM
    scratch = tile_scratch(width) + [
        pltpu.VMEM((width, LANES), jnp.bfloat16),
        pltpu.VMEM((message.shape[0] - count, LANES), jnp.bfloat16),
        pltpu.SemaphoreType.DMA((2,)),
    ]
    return kernel_call(
        functools.partial(piece_body, piece * width, last), "piece_tile", [rows, message, total], "vav",
        [out((count, LANES), jnp.float32)], scratch, tile_cost(count), None if last else {2: 0},
    )[0]


def half_gram(core, own, pair, first, second):
    count = first.shape[0]
    block = pltpu.VMEM((LANES, LANES), jnp.float32)
    return kernel_call(
        half_gram_body, "half_gram", [core, own, pair, first, second], "shavv",
        [block, block, pltpu.VMEM((count, LANES), jnp.float32)],
        [pltpu.VMEM((2, count, LANES), jnp.bfloat16), pltpu.SemaphoreType.DMA((2,))], tile_cost(count), {3: 2},
    )


def fold(core, *blocks):
    out = pltpu.VMEM((LANES, LANES), jnp.float32)
    cost = pl.CostEstimate(flops=0, bytes_accessed=2**17, transcendentals=0)
    return kernel_call(fold_body, "fold", [core, *blocks], "svvvv", [out], [], cost)[0]


def along_blk(value, sizes, target):
    ny, nx, nz, nc = sizes

    def index(y, x, z, c):
        return ((y % ny * nx + x % nx) * nz + z % nz) * nc + c % nc

    pairs = []
    for y in range(ny):
        for x in range(nx):
            for z in range(nz):
                for c in range(nc):
                    pairs.append((index(y, x, z, c), index(*target(y, x, z, c))))
    return lax.ppermute(value, BLK, pairs)


def from_neighbour(value, parity):
    count = lax.axis_size(BLK)
    pairs = []
    for block in range(count):
        chip, core = divmod(block, 2)
        first = chip % 2 == parity
        other = 2 * (chip + 1) + 1 - core if first else 2 * (chip - 1) + core
        pairs.append((block, other % count))
    return lax.ppermute(value, BLK, pairs)


def from_far(value):
    count = lax.axis_size(BLK)
    return lax.ppermute(
        value, BLK, [(b, (b - 3 if b % 2 == 0 else b + 3) % count) for b in range(count)]
    )


def core_swap(value):
    return lax.ppermute(value, "core", [(0, 1), (1, 0)])


def shards(sizes, directions, axial_pos, azimuth, panel_area):
    count = axial_pos.shape[0]
    geometry = [part.reshape(count // LANES, LANES) for part in (axial_pos, azimuth, panel_area)]
    message = pack(directions, geometry)
    other = core_swap(message)
    even = from_neighbour(message, 0)
    odd = from_neighbour(message, 1)

    first, rows = home_tile(message, count)
    first, late = lax.optimization_barrier((first, message))
    far = from_far(late)
    (first,) = guest_tile(rows, other, first)
    first, even, later = lax.optimization_barrier((first, even, directions))
    pair = lax.ppermute(later, "rhs", [(0, 1), (1, 0)])
    even_other = core_swap(even)
    second, first = guest_tile(rows, even, None, (first,))
    second, odd = lax.optimization_barrier((second, odd))
    odd_other = core_swap(odd)
    second, first = guest_tile(rows, odd, second, (first,))
    second, far = lax.optimization_barrier((second, far))
    first, second = guest_tile(rows, far, first, (second,))
    core = lax.axis_index("core").astype(jnp.int32)
    keep, give, product = half_gram(core.reshape(1), directions, pair, first, second)

    swapped = core_swap(give)
    crossed = lax.ppermute(keep, ("core", "rhs"), [(2, 3), (3, 2)])
    far_crossed = lax.ppermute(give, ("core", "rhs"), [(0, 3), (1, 2)])
    value = fold(core.reshape(1), keep, swapped, crossed, far_crossed)

    work = [(guest, piece) for guest in (even_other, odd_other) for piece in range(PIECES)]
    stages = (
        ((0, 0, 4), 2, False), ((0, 0, 2), 2, True), ((0, 0, 1), 1, False),
        ((2, 0, 0), 1, True), ((1, 0, 0), 1, False), ((0, 1, 0), 1, True),
    )
    for move, pieces, rounded in stages:
        sent = value.astype(jnp.bfloat16) if rounded else value
        product, sent = lax.optimization_barrier((product, sent))
        moved = along_blk(sent, sizes, lambda y, x, z, c, d=move: (y ^ d[0], x ^ d[1], z ^ d[2], c))
        for _ in range(pieces):
            guest, piece = work.pop(0)
            product = piece_tile(rows, guest, product, piece, not work)
        sent, product, moved = lax.optimization_barrier((sent, product, moved))
        value = sent.astype(jnp.float32) + moved.astype(jnp.float32)
    value = value / (count * lax.axis_size(BLK))
    swapped = core_swap(value)
    upper = core == lax.axis_index("rhs")
    gram = jnp.concatenate([jnp.where(upper, value, swapped), jnp.where(upper, swapped, value)], axis=0)
    return product, gram


def solution(mesh):
    sizes = (4, 2, 8, 2)
    fine = Mesh(mesh.devices.reshape(sizes + (2,)), BLK + ("rhs",))
    in_specs = (P(BLK, "rhs"), P(BLK), P(BLK), P(BLK))
    out_specs = (P(BLK, "rhs"), P(None, "rhs"))
    return jax.shard_map(
        functools.partial(shards, sizes), mesh=fine, in_specs=in_specs, out_specs=out_specs, check_vma=False
    )
```

```python
import functools

import jax
import jax.numpy as jnp
from jax import lax
from jax.experimental import pallas as pl
from jax.experimental.pallas import tpu as pltpu
from jax.sharding import Mesh, PartitionSpec as P

LANES = 128
VMEM_BYTES = 12 * 2**20
ROW_STEP = 256
COL_STEP = 1024
PIECES = 4
PIECE_ROWS = 1024
COPIES = 4
BLK = ("y", "xh", "z", "core")


def split_parts(base):
    high = base.astype(jnp.bfloat16).astype(jnp.float32)
    rest = base - high
    mid = rest.astype(jnp.bfloat16).astype(jnp.float32)
    low = (rest - mid).astype(jnp.bfloat16).astype(jnp.float32)
    return high, mid, low


def point_values(axial, angle, area):
    axial = axial.astype(jnp.float32) - 4.0
    angle = angle.astype(jnp.float32)
    area = area.astype(jnp.float32)
    cos, sin = jnp.cos(angle), jnp.sin(angle)
    return axial, cos, sin, axial * axial + cos * cos + sin * sin, 1.0 / (area * area)


def lay_rows(base_ref, features):
    groups = features[0].shape[0]
    base_ref[...] = jnp.zeros_like(base_ref)
    for row, feature in enumerate(features):
        for group in range(groups):
            base_ref[row : row + 1, group * LANES : (group + 1) * LANES] = feature[group : group + 1, :]


def column_factors(geometry, base_ref, col_ref):
    axial, cos, sin, norm, scale = point_values(*geometry)
    lay_rows(base_ref, (scale, norm * scale, axial * scale, cos * scale, sin * scale))
    high, mid, low = split_parts(base_ref[...])
    col_ref[...] = jnp.concatenate([high, high, high, mid, mid, low], axis=0).astype(jnp.bfloat16)


def row_factors(geometry, base_ref, row_ref):
    axial, cos, sin, norm, scale = point_values(*geometry)
    count = base_ref.shape[1]
    scale = scale * count
    double = -2.0 * scale
    lay_rows(base_ref, ((norm + 0.01) * scale, scale, axial * double, cos * double, sin * double))
    high, mid, low = split_parts(base_ref[...])
    stacked = jnp.concatenate([high, mid, low, high, mid, high], axis=0)
    for group in range(count // LANES):
        part = stacked[:, group * LANES : (group + 1) * LANES]
        row_ref[group * LANES : (group + 1) * LANES, :] = part.T.astype(jnp.bfloat16)


def tile_product(row_ref, col_ref, directions_ref, out_ref, offset=0, width=None, arrive=None, row_step=ROW_STEP):
    width = width or col_ref.shape[1]
    step_cols = min(COL_STEP, width)

    def step_fn(step, carried):
        start = pl.multiple_of(step * step_cols, step_cols)
        if arrive is not None:
            arrive(step)
        cols = pl.ds(offset + start, step_cols)
        factor, directions = col_ref[:, cols], directions_ref[cols, :]
        for low in range(0, row_ref.shape[0], row_step):
            rows = slice(low, low + row_step)
            inverse = jnp.dot(row_ref[rows, :], factor, preferred_element_type=jnp.float32)
            values = lax.rsqrt(inverse).astype(jnp.bfloat16)
            out_ref[rows, :] += jnp.dot(values, directions, preferred_element_type=jnp.float32)
        return carried

    lax.fori_loop(0, width // step_cols, step_fn, 0)


def geometry_of(ref):
    groups = ref.shape[0] // 3
    return tuple(ref[k * groups : (k + 1) * groups, :].astype(jnp.float32) for k in range(3))


def geometry_copy(message_ref, geometry_ref, sem):
    rows = geometry_ref.shape[0]
    return pltpu.make_async_copy(message_ref.at[pl.ds(message_ref.shape[0] - rows, rows)], geometry_ref, sem)


def pack_body(directions_ref, axial_ref, angle_ref, area_ref, out_ref, sems):
    count = directions_ref.shape[0]
    part = count // COPIES
    copies = [
        pltpu.make_async_copy(
            directions_ref.at[pl.ds(k * part, part)], out_ref.at[pl.ds(k * part, part)], sems.at[k]
        )
        for k in range(COPIES)
    ]
    groups = axial_ref.shape[0]
    for k, ref in enumerate((axial_ref, angle_ref, area_ref)):
        rows = out_ref.at[pl.ds(count + k * groups, groups)]
        copies.append(pltpu.make_async_copy(ref, rows, sems.at[COPIES + k]))
    for copy in copies:
        copy.start()
    for copy in copies:
        copy.wait()


def home_body(message_ref, out_ref, row_ref, base_ref, col_ref):
    count = row_ref.shape[0]
    geometry = geometry_of(message_ref.at[pl.ds(count, message_ref.shape[0] - count)])
    row_factors(geometry, base_ref, row_ref)
    column_factors(geometry, base_ref, col_ref)
    out_ref[...] = jnp.zeros_like(out_ref)
    tile_product(row_ref, col_ref, message_ref, out_ref)


def guest_body(has_total, n_held, row_ref, message_ref, *refs):
    out_ref, *refs = refs[has_total + n_held :]
    base_ref, col_ref, directions_ref, geometry_ref, sems = refs[n_held:]
    part = min(COL_STEP, row_ref.shape[0])
    steps = row_ref.shape[0] // part

    def piece_copy(step):
        rows = pl.ds(pl.multiple_of(step * part, part), part)
        return pltpu.make_async_copy(message_ref.at[rows], directions_ref.at[rows], sems.at[step])

    geometry = geometry_copy(message_ref, geometry_ref, sems.at[steps])
    geometry.start()
    for step in range(steps):
        piece_copy(step).start()
    geometry.wait()
    column_factors(geometry_of(geometry_ref), base_ref, col_ref)
    if not has_total:
        out_ref[...] = jnp.zeros_like(out_ref)
    tile_product(row_ref, col_ref, directions_ref, out_ref, arrive=lambda step: piece_copy(step).wait())


def piece_body(offset, last, row_ref, message_ref, total_ref, out_ref, base_ref, col_ref, directions_ref, geometry_ref, sems):
    width = directions_ref.shape[0]
    geometry = geometry_copy(message_ref, geometry_ref, sems.at[0])
    copy = pltpu.make_async_copy(message_ref.at[pl.ds(offset, width)], directions_ref, sems.at[1])
    geometry.start()
    copy.start()
    geometry.wait()
    part = slice(offset // LANES, (offset + width) // LANES)
    column_factors([value[part] for value in geometry_of(geometry_ref)], base_ref, col_ref)
    for low in range(0, row_ref.shape[0], PIECE_ROWS):
        rows = slice(low, low + PIECE_ROWS)
        inverse = jnp.dot(row_ref[rows, :], col_ref[...], preferred_element_type=jnp.float32)
        values = lax.rsqrt(inverse).astype(jnp.bfloat16)
        if low == 0:
            copy.wait()
        part = jnp.dot(values, directions_ref[...], preferred_element_type=jnp.float32)
        if last:
            out_ref[rows, :] = total_ref[rows, :] + part
        else:
            out_ref[rows, :] += part


def fold_body(core_ref, value_ref, crossed_ref, out_ref):
    first = core_ref[0] == 0

    @pl.when(first)
    def _():
        out_ref[...] = value_ref[...] + value_ref[...].T

    @pl.when(jnp.logical_not(first))
    def _():
        out_ref[...] = value_ref[...] + crossed_ref[...].T


def half_gram_body(
    core_ref, own_ref, pair_ref, first_ref, second_ref, keep_ref, give_ref, sum_ref, directions_ref, sems
):
    copies = [
        pltpu.make_async_copy(ref, directions_ref.at[k], sems.at[k]) for k, ref in enumerate((own_ref, pair_ref))
    ]
    for copy in copies:
        copy.start()
    first, second = first_ref[...], second_ref[...]
    value = 0.5 * first + second
    sum_ref[...] = first + second
    high = value.astype(jnp.bfloat16)
    low = (value - high.astype(jnp.float32)).astype(jnp.bfloat16)
    both = jnp.concatenate([high, low], axis=1)
    blocks = []
    for k, copy in enumerate(copies):
        copy.wait()
        part = lax.dot_general(
            directions_ref[k], both, (((0,), (0,)), ((), ())), preferred_element_type=jnp.float32
        )
        blocks.append(part[:, :LANES] + part[:, LANES:])
    on_first = core_ref[0] == 0
    keep_ref[...] = jnp.where(on_first, blocks[0], blocks[1])
    give_ref[...] = jnp.where(on_first, blocks[1], blocks[0])


def tile_cost(count):
    return pl.CostEstimate(flops=count * count * 16, bytes_accessed=0, transcendentals=0)


def kernel_call(body, name, operands, places, outs, scratch, cost, aliases=None):
    spaces = {"v": pltpu.VMEM, "s": pltpu.SMEM, "a": pl.ANY, "h": pltpu.HBM}
    fixed = {"v": pltpu.VMEM, "h": pltpu.HBM}
    operands = [
        pltpu.with_memory_space_constraint(value, fixed[place]) if place in fixed else value
        for value, place in zip(operands, places)
    ]
    return pl.pallas_call(
        body,
        out_shape=outs,
        in_specs=[pl.BlockSpec(memory_space=spaces[place]) for place in places],
        out_specs=[pl.BlockSpec(memory_space=pltpu.VMEM)] * len(outs),
        input_output_aliases=aliases or {},
        scratch_shapes=scratch,
        cost_estimate=cost,
        compiler_params=pltpu.CompilerParams(vmem_limit_bytes=VMEM_BYTES),
        name=name,
    )(*operands)


def pack(directions, geometry):
    count = directions.shape[0]
    out = (count + sum(part.shape[0] for part in geometry), LANES)
    return kernel_call(
        pack_body, "pack", [directions, *geometry], "hhhh", [pltpu.VMEM(out, jnp.bfloat16)],
        [pltpu.SemaphoreType.DMA((COPIES + 3,))], pl.CostEstimate(flops=0, bytes_accessed=2**20, transcendentals=0),
    )[0]


def tile_scratch(count):
    return [pltpu.VMEM((8, count), jnp.float32), pltpu.VMEM((48, count), jnp.bfloat16)]


def home_tile(message, count):
    outs = [pltpu.VMEM((count, LANES), jnp.float32), pltpu.VMEM((count, 48), jnp.bfloat16)]
    return kernel_call(home_body, "home_tile", [message], "v", outs, tile_scratch(count), tile_cost(count))


def guest_tile(rows, message, total=None, held=()):
    count = rows.shape[0]
    totals = [] if total is None else [total]
    scratch = tile_scratch(count) + [
        pltpu.VMEM((count, LANES), jnp.bfloat16),
        pltpu.VMEM((message.shape[0] - count, LANES), jnp.bfloat16),
        pltpu.SemaphoreType.DMA((count // min(COL_STEP, count) + 1,)),
    ]
    aliases = {2: 0} if totals else {}
    aliases.update({2 + len(totals) + k: 1 + k for k in range(len(held))})
    return kernel_call(
        functools.partial(guest_body, len(totals), len(held)), "guest_tile", [rows, message, *totals, *held],
        "va" + "v" * (len(totals) + len(held)), [pltpu.VMEM((count, LANES), jnp.float32)] * (1 + len(held)),
        scratch, tile_cost(count), aliases,
    )


def piece_tile(rows, message, total, piece, last):
    count = rows.shape[0]
    width = count // PIECES
    out = jax.ShapeDtypeStruct if last else pltpu.VMEM
    scratch = tile_scratch(width) + [
        pltpu.VMEM((width, LANES), jnp.bfloat16),
        pltpu.VMEM((message.shape[0] - count, LANES), jnp.bfloat16),
        pltpu.SemaphoreType.DMA((2,)),
    ]
    return kernel_call(
        functools.partial(piece_body, piece * width, last), "piece_tile", [rows, message, total], "vav",
        [out((count, LANES), jnp.float32)], scratch, tile_cost(count), None if last else {2: 0},
    )[0]


def half_gram(core, own, pair, first, second):
    count = first.shape[0]
    block = pltpu.VMEM((LANES, LANES), jnp.float32)
    return kernel_call(
        half_gram_body, "half_gram", [core, own, pair, first, second], "shavv",
        [block, block, pltpu.VMEM((count, LANES), jnp.float32)],
        [pltpu.VMEM((2, count, LANES), jnp.bfloat16), pltpu.SemaphoreType.DMA((2,))], tile_cost(count), {3: 2},
    )


def fold(core, *blocks):
    out = pltpu.VMEM((LANES, LANES), jnp.float32)
    cost = pl.CostEstimate(flops=0, bytes_accessed=2**17, transcendentals=0)
    return kernel_call(fold_body, "fold", [core, *blocks], "svv", [out], [], cost)[0]


def along_blk(value, sizes, target):
    ny, nx, nz, nc = sizes

    def index(y, x, z, c):
        return ((y % ny * nx + x % nx) * nz + z % nz) * nc + c % nc

    pairs = []
    for y in range(ny):
        for x in range(nx):
            for z in range(nz):
                for c in range(nc):
                    pairs.append((index(y, x, z, c), index(*target(y, x, z, c))))
    return lax.ppermute(value, BLK, pairs)


def from_neighbour(value, parity):
    count = lax.axis_size(BLK)
    pairs = []
    for block in range(count):
        chip, core = divmod(block, 2)
        first = chip % 2 == parity
        other = 2 * (chip + 1) + 1 - core if first else 2 * (chip - 1) + core
        pairs.append((block, other % count))
    return lax.ppermute(value, BLK, pairs)


def from_far(value):
    count = lax.axis_size(BLK)
    return lax.ppermute(
        value, BLK, [(b, (b - 3 if b % 2 == 0 else b + 3) % count) for b in range(count)]
    )


def core_swap(value):
    return lax.ppermute(value, "core", [(0, 1), (1, 0)])


def shards(sizes, directions, axial_pos, azimuth, panel_area):
    count = axial_pos.shape[0]
    geometry = [part.reshape(count // LANES, LANES) for part in (axial_pos, azimuth, panel_area)]
    message = pack(directions, geometry)
    other = core_swap(message)
    even = from_neighbour(message, 0)
    odd = from_neighbour(message, 1)

    first, rows = home_tile(message, count)
    first, late = lax.optimization_barrier((first, message))
    far = from_far(late)
    (first,) = guest_tile(rows, other, first)
    first, even, later = lax.optimization_barrier((first, even, directions))
    pair = lax.ppermute(later, "rhs", [(0, 1), (1, 0)])
    even_other = core_swap(even)
    second, first = guest_tile(rows, even, None, (first,))
    second, odd = lax.optimization_barrier((second, odd))
    odd_other = core_swap(odd)
    second, first = guest_tile(rows, odd, second, (first,))
    second, far = lax.optimization_barrier((second, far))
    first, second = guest_tile(rows, far, first, (second,))
    core = lax.axis_index("core").astype(jnp.int32)
    keep, give, product = half_gram(core.reshape(1), directions, pair, first, second)

    work = [(guest, piece) for guest in (even_other, odd_other) for piece in range(PIECES)]

    def advance(product, pieces):
        for _ in range(pieces):
            guest, piece = work.pop(0)
            product = piece_tile(rows, guest, product, piece, not work)
        return product

    value = keep + core_swap(give)
    value, product = lax.optimization_barrier((value, product))
    crossed = lax.ppermute(value, ("core", "rhs"), [(2, 3), (3, 2)])
    product = advance(product, 1)
    value, crossed, product = lax.optimization_barrier((value, crossed, product))
    value = fold(core.reshape(1), value, crossed)

    def moved_by(sent, move):
        return along_blk(
            sent, sizes, lambda y, x, z, c: (y ^ move[0], x ^ move[1], z ^ move[2], c ^ move[3])
        )

    stages = (
        ((0, 0, 4, 0), 2, True), ((0, 0, 2, 0), 1, True), ((0, 0, 1, 0), 1, False),
        ((2, 0, 0, 0), 1, True), ((1, 0, 0, 0), 1, False),
    )
    for move, pieces, rounded in stages:
        sent = value.astype(jnp.bfloat16) if rounded else value
        product, sent = lax.optimization_barrier((product, sent))
        moved = moved_by(sent, move)
        product = advance(product, pieces)
        sent, product, moved = lax.optimization_barrier((sent, product, moved))
        value = sent.astype(jnp.float32) + moved.astype(jnp.float32)

    product, value = lax.optimization_barrier((product, value))
    moved = [moved_by(value, move) for move in ((0, 1, 0, 0), (0, 0, 0, 1), (0, 1, 0, 1))]
    product = advance(product, len(work))
    product, value, *moved = lax.optimization_barrier((product, value, *moved))
    scale = 1.0 / (count * lax.axis_size(BLK))
    value, swapped = (value + moved[0]) * scale, (moved[1] + moved[2]) * scale
    upper = core == lax.axis_index("rhs")
    gram = jnp.concatenate([jnp.where(upper, value, swapped), jnp.where(upper, swapped, value)], axis=0)
    return product, gram


def solution(mesh):
    sizes = (4, 2, 8, 2)
    fine = Mesh(mesh.devices.reshape(sizes + (2,)), BLK + ("rhs",))
    in_specs = (P(BLK, "rhs"), P(BLK), P(BLK), P(BLK))
    out_specs = (P(BLK, "rhs"), P(None, "rhs"))
    return jax.shard_map(
        functools.partial(shards, sizes), mesh=fine, in_specs=in_specs, out_specs=out_specs, check_vma=False
    )
```

```python
import functools

import jax
import jax.numpy as jnp
from jax import lax
from jax.experimental import pallas as pl
from jax.experimental.pallas import tpu as pltpu
from jax.sharding import Mesh, PartitionSpec as P

LANES = 128
VMEM_BYTES = 12 * 2**20
STEP = 256
HALVES = 2
PIECES = 4
COPIES = 4
BLK = ("y", "xh", "z", "core")


def split_parts(base):
    high = base.astype(jnp.bfloat16).astype(jnp.float32)
    rest = base - high
    mid = rest.astype(jnp.bfloat16).astype(jnp.float32)
    low = (rest - mid).astype(jnp.bfloat16).astype(jnp.float32)
    return high, mid, low


def point_values(axial, angle, area):
    axial = axial.astype(jnp.float32) - 4.0
    angle = angle.astype(jnp.float32)
    area = area.astype(jnp.float32)
    cos, sin = jnp.cos(angle), jnp.sin(angle)
    return axial, cos, sin, axial * axial + cos * cos + sin * sin, 1.0 / (area * area)


def lay_rows(base_ref, features):
    groups = features[0].shape[0]
    base_ref[...] = jnp.zeros_like(base_ref)
    for row, feature in enumerate(features):
        for group in range(groups):
            base_ref[row : row + 1, group * LANES : (group + 1) * LANES] = feature[group : group + 1, :]


def guest_factors(geometry, base_ref, row_ref):
    axial, cos, sin, norm, scale = point_values(*geometry)
    lay_rows(base_ref, (scale, norm * scale, axial * scale, cos * scale, sin * scale))
    high, mid, low = split_parts(base_ref[...])
    stacked = jnp.concatenate([high, high, high, mid, mid, low], axis=0)
    for group in range(row_ref.shape[0] // LANES):
        part = stacked[:, group * LANES : (group + 1) * LANES]
        row_ref[group * LANES : (group + 1) * LANES, :] = part.T.astype(jnp.bfloat16)


def home_factors(geometry, base_ref, col_ref):
    axial, cos, sin, norm, scale = point_values(*geometry)
    scale = scale * base_ref.shape[1]
    double = -2.0 * scale
    lay_rows(base_ref, ((norm + 0.01) * scale, scale, axial * double, cos * double, sin * double))
    high, mid, low = split_parts(base_ref[...])
    col_ref[...] = jnp.concatenate([high, mid, low, high, mid, high], axis=0).astype(jnp.bfloat16)


def add_panels(total, row_ref, directions_ref, home, start, count, where=0):
    for low in range(0, count, STEP):
        at = start + low
        inverse = jnp.dot(row_ref[pl.ds(at, STEP), :], home, preferred_element_type=jnp.float32)
        values = lax.rsqrt(inverse).astype(jnp.bfloat16)
        directions = directions_ref[:, pl.ds(where + at, STEP)]
        total = total + jnp.dot(directions, values, preferred_element_type=jnp.float32)
    return total


def tile_product(home_ref, row_ref, directions_ref, out_ref, arrive=None):
    count = row_ref.shape[0] // HALVES

    def step_fn(step, carried):
        if arrive is not None:
            arrive(step)
        start = pl.multiple_of(step * count, count)
        out_ref[...] = add_panels(out_ref[...], row_ref, directions_ref, home_ref[...], start, count)
        return carried

    lax.fori_loop(0, HALVES, step_fn, 0)


def geometry_of(ref):
    groups = ref.shape[0] // 3
    return tuple(ref[k * groups : (k + 1) * groups, :].astype(jnp.float32) for k in range(3))


def geometry_copy(message_ref, geometry_ref, sem):
    count = message_ref.shape[1] - LANES
    return pltpu.make_async_copy(
        message_ref.at[pl.ds(0, geometry_ref.shape[0]), pl.ds(count, LANES)], geometry_ref, sem
    )


def pack_body(directions_ref, axial_ref, angle_ref, area_ref, out_ref, held_ref, sems):
    count = directions_ref.shape[0]
    part = count // COPIES
    copies = []
    for k in range(COPIES):
        rows = pl.ds(k * part, part)
        copies.append(pltpu.make_async_copy(directions_ref.at[rows], held_ref.at[rows], sems.at[k]))
    groups = axial_ref.shape[0]
    for k, ref in enumerate((axial_ref, angle_ref, area_ref)):
        place = out_ref.at[pl.ds(k * groups, groups), pl.ds(count, LANES)]
        copies.append(pltpu.make_async_copy(ref, place, sems.at[COPIES + k]))
    for copy in copies:
        copy.start()
    out_ref[3 * groups :, count:] = jnp.zeros((LANES - 3 * groups, LANES), jnp.bfloat16)
    for k in range(COPIES):
        copies[k].wait()
        for low in range(k * part, (k + 1) * part, LANES):
            out_ref[:, low : low + LANES] = held_ref[low : low + LANES, :].T
    for copy in copies[COPIES:]:
        copy.wait()


def home_body(message_ref, out_ref, home_ref, base_ref, row_ref):
    count = row_ref.shape[0]
    geometry = geometry_of(message_ref.at[pl.ds(0, 3 * count // LANES), pl.ds(count, LANES)])
    home_factors(geometry, base_ref, home_ref)
    guest_factors(geometry, base_ref, row_ref)
    out_ref[...] = jnp.zeros_like(out_ref)
    tile_product(home_ref, row_ref, message_ref, out_ref)


def guest_body(has_total, n_held, n_sources, *refs):
    refs = list(refs)
    choice_ref = refs.pop(0) if n_sources > 1 else None
    home_ref = refs.pop(0)
    sources = [refs.pop(0) for _ in range(n_sources)]
    out_ref, *refs = refs[has_total + n_held :]
    base_ref, row_ref, directions_ref, geometry_ref, sems = refs[n_held:]
    part = row_ref.shape[0] // HALVES

    def part_copy(ref, step):
        columns = pl.ds(pl.multiple_of(step * part, part), part)
        return pltpu.make_async_copy(ref.at[:, columns], directions_ref.at[:, columns], sems.at[step])

    def fetch(ref):
        geometry_copy(ref, geometry_ref, sems.at[HALVES]).start()
        for step in range(HALVES):
            part_copy(ref, step).start()

    if choice_ref is None:
        fetch(sources[0])
    else:
        for k, ref in enumerate(sources):
            pl.when(choice_ref[0] == k)(functools.partial(fetch, ref))
    geometry_copy(sources[0], geometry_ref, sems.at[HALVES]).wait()
    guest_factors(geometry_of(geometry_ref), base_ref, row_ref)
    if not has_total:
        out_ref[...] = jnp.zeros_like(out_ref)
    tile_product(
        home_ref, row_ref, directions_ref, out_ref, arrive=lambda step: part_copy(sources[0], step).wait()
    )


def piece_body(
    offset, last, home_ref, message_ref, total_ref, out_ref, base_ref, row_ref, directions_ref, geometry_ref, sems
):
    width = row_ref.shape[0]
    geometry = geometry_copy(message_ref, geometry_ref, sems.at[0])
    copy = pltpu.make_async_copy(message_ref.at[:, pl.ds(offset, width)], directions_ref, sems.at[1])
    geometry.start()
    copy.start()
    geometry.wait()
    part = slice(offset // LANES, (offset + width) // LANES)
    guest_factors([value[part] for value in geometry_of(geometry_ref)], base_ref, row_ref)
    copy.wait()
    total = add_panels(total_ref[...], row_ref, directions_ref, home_ref[...], 0, width)
    out_ref[...] = total.T if last else total


def fold_body(core_ref, value_ref, crossed_ref, out_ref):
    first = core_ref[0] == 0

    @pl.when(first)
    def _():
        out_ref[...] = value_ref[...] + value_ref[...].T

    @pl.when(jnp.logical_not(first))
    def _():
        out_ref[...] = value_ref[...].T + crossed_ref[...]


def half_gram_body(
    core_ref, own_ref, pair_ref, first_ref, second_ref, keep_ref, give_ref, sum_ref, directions_ref, sems
):
    copies = [
        pltpu.make_async_copy(ref, directions_ref.at[k], sems.at[k]) for k, ref in enumerate((own_ref, pair_ref))
    ]
    for copy in copies:
        copy.start()
    first, second = first_ref[...], second_ref[...]
    value = 0.5 * first + second
    sum_ref[...] = first + second
    high = value.astype(jnp.bfloat16)
    low = (value - high.astype(jnp.float32)).astype(jnp.bfloat16)
    both = jnp.concatenate([high, low], axis=0)
    for copy in copies:
        copy.wait()
    directions = jnp.concatenate([directions_ref[0], directions_ref[1]], axis=1)
    part = jnp.dot(both, directions, preferred_element_type=jnp.float32)
    part = part[:LANES] + part[LANES:]
    on_first = core_ref[0] == 0
    keep_ref[...] = jnp.where(on_first, part[:, :LANES], part[:, LANES:])
    give_ref[...] = jnp.where(on_first, part[:, LANES:], part[:, :LANES])


def tile_cost(count):
    return pl.CostEstimate(flops=count * count * 16, bytes_accessed=0, transcendentals=0)


def kernel_call(body, name, operands, places, outs, scratch, cost, aliases=None):
    spaces = {"v": pltpu.VMEM, "s": pltpu.SMEM, "a": pl.ANY, "h": pltpu.HBM}
    fixed = {"v": pltpu.VMEM, "h": pltpu.HBM}
    operands = [
        pltpu.with_memory_space_constraint(value, fixed[place]) if place in fixed else value
        for value, place in zip(operands, places)
    ]
    return pl.pallas_call(
        body,
        out_shape=outs,
        in_specs=[pl.BlockSpec(memory_space=spaces[place]) for place in places],
        out_specs=[pl.BlockSpec(memory_space=pltpu.VMEM)] * len(outs),
        input_output_aliases=aliases or {},
        scratch_shapes=scratch,
        cost_estimate=cost,
        compiler_params=pltpu.CompilerParams(vmem_limit_bytes=VMEM_BYTES),
        name=name,
    )(*operands)


def pack(directions, geometry):
    count = directions.shape[0]
    return kernel_call(
        pack_body, "pack", [directions, *geometry], "hhhh", [pltpu.VMEM((LANES, count + LANES), jnp.bfloat16)],
        [pltpu.VMEM((count, LANES), jnp.bfloat16), pltpu.SemaphoreType.DMA((COPIES + 3,))],
        pl.CostEstimate(flops=0, bytes_accessed=2**20, transcendentals=0),
    )[0]


def tile_scratch(count):
    return [pltpu.VMEM((8, count), jnp.float32), pltpu.VMEM((count, 48), jnp.bfloat16)]


def fetch_scratch(count, geometry_rows, copies):
    return tile_scratch(count) + [
        pltpu.VMEM((LANES, count), jnp.bfloat16),
        pltpu.VMEM((geometry_rows, LANES), jnp.bfloat16),
        pltpu.SemaphoreType.DMA((copies,)),
    ]


def home_tile(message, count):
    outs = [pltpu.VMEM((LANES, count), jnp.float32), pltpu.VMEM((48, count), jnp.bfloat16)]
    return kernel_call(home_body, "home_tile", [message], "v", outs, tile_scratch(count), tile_cost(count))


def guest_tile(home, sources, total=None, held=(), choice=None):
    count = home.shape[1]
    totals = [] if total is None else [total]
    choices = [] if choice is None else [choice]
    place = len(choices) + 1 + len(sources)
    aliases = {place: 0} if totals else {}
    aliases.update({place + len(totals) + k: 1 + k for k in range(len(held))})
    return kernel_call(
        functools.partial(guest_body, len(totals), len(held), len(sources)), "guest_tile",
        [*choices, home, *sources, *totals, *held],
        "s" * len(choices) + "v" + "a" * len(sources) + "v" * (len(totals) + len(held)),
        [pltpu.VMEM((LANES, count), jnp.float32)] * (1 + len(held)),
        fetch_scratch(count, 3 * count // LANES, HALVES + 1), tile_cost(count), aliases,
    )


def piece_tile(home, message, total, piece, last):
    count = home.shape[1]
    width = count // PIECES
    out = jax.ShapeDtypeStruct((count, LANES), jnp.float32) if last else pltpu.VMEM((LANES, count), jnp.float32)
    return kernel_call(
        functools.partial(piece_body, piece * width, last), "piece_tile", [home, message, total], "vav", [out],
        fetch_scratch(width, 3 * count // LANES, 2), tile_cost(count), None if last else {2: 0},
    )[0]


def half_gram(core, own, pair, first, second):
    count = first.shape[1]
    block = pltpu.VMEM((LANES, LANES), jnp.float32)
    return kernel_call(
        half_gram_body, "half_gram", [core, own, pair, first, second], "shavv",
        [block, block, pltpu.VMEM((LANES, count), jnp.float32)],
        [pltpu.VMEM((2, count, LANES), jnp.bfloat16), pltpu.SemaphoreType.DMA((2,))], tile_cost(count), {3: 2},
    )


def fold(core, *blocks):
    out = pltpu.VMEM((LANES, LANES), jnp.float32)
    cost = pl.CostEstimate(flops=0, bytes_accessed=2**17, transcendentals=0)
    return kernel_call(fold_body, "fold", [core, *blocks], "svv", [out], [], cost)[0]


def along_blk(value, sizes, target):
    ny, nx, nz, nc = sizes

    def index(y, x, z, c):
        return ((y % ny * nx + x % nx) * nz + z % nz) * nc + c % nc

    pairs = []
    for y in range(ny):
        for x in range(nx):
            for z in range(nz):
                for c in range(nc):
                    pairs.append((index(y, x, z, c), index(*target(y, x, z, c))))
    return lax.ppermute(value, BLK, pairs)


def from_neighbour(value, parity):
    count = lax.axis_size(BLK)
    pairs = []
    for block in range(count):
        chip, core = divmod(block, 2)
        first = chip % 2 == parity
        other = 2 * (chip + 1) + 1 - core if first else 2 * (chip - 1) + core
        pairs.append((block, other % count))
    return lax.ppermute(value, BLK, pairs)


def from_far(length):
    count = lax.axis_size(BLK)
    direct, passed = [], []
    for block in range(count):
        place = block // 2 % length
        if block % 2 == 0:
            source, between, over = block - 3, block - 2, place == 1
        else:
            source, between, over = block + 3, block + 1, place == length - 2
        if over:
            passed.append((between % count, block))
        else:
            direct.append((source % count, block))
    return tuple(functools.partial(lax.ppermute, axis_name=BLK, perm=pairs) for pairs in (direct, passed))


def core_swap(value):
    return lax.ppermute(value, "core", [(0, 1), (1, 0)])


def shards(sizes, directions, axial_pos, azimuth, panel_area):
    count = axial_pos.shape[0]
    geometry = [part.reshape(count // LANES, LANES) for part in (axial_pos, azimuth, panel_area)]
    message = pack(directions, geometry)
    other = core_swap(message)
    even = from_neighbour(message, 0)
    odd = from_neighbour(message, 1)

    first, home = home_tile(message, count)
    first, late = lax.optimization_barrier((first, message))
    direct, passed = from_far(sizes[2])
    far = direct(late)
    (first,) = guest_tile(home, (other,), first)
    first, even, later = lax.optimization_barrier((first, even, directions))
    pair = lax.ppermute(later, "rhs", [(0, 1), (1, 0)])
    even_other = core_swap(even)
    second, first = guest_tile(home, (even,), None, (first,))
    second, odd = lax.optimization_barrier((second, odd))
    over = passed(odd)
    odd_other = core_swap(odd)
    second, first = guest_tile(home, (odd,), second, (first,))
    second, far, over = lax.optimization_barrier((second, far, over))
    core = lax.axis_index("core").astype(jnp.int32)
    place = lax.axis_index("z")
    is_over = jnp.where(core == 0, place == 1, place == sizes[2] - 2).astype(jnp.int32).reshape(1)
    first, second = guest_tile(home, (far, over), first, (second,), is_over)
    keep, give, product = half_gram(core.reshape(1), directions, pair, first, second)

    work = [(guest, piece) for guest in (even_other, odd_other) for piece in range(PIECES)]

    def advance(product, pieces):
        for _ in range(pieces):
            guest, piece = work.pop(0)
            product = piece_tile(home, guest, product, piece, not work)
        return product

    value = keep + core_swap(give)
    value, product = lax.optimization_barrier((value, product))
    crossed = lax.ppermute(value, ("core", "rhs"), [(2, 3), (3, 2)])
    product = advance(product, 1)
    value, crossed, product = lax.optimization_barrier((value, crossed, product))
    value = fold(core.reshape(1), value, crossed)

    def moved_by(sent, move):
        return along_blk(
            sent, sizes, lambda y, x, z, c: (y ^ move[0], x ^ move[1], z ^ move[2], c ^ move[3])
        )

    stages = (
        ((0, 0, 4, 0), 2, True), ((0, 0, 2, 0), 1, True), ((0, 0, 1, 0), 1, False),
        ((2, 0, 0, 0), 1, True), ((1, 0, 0, 0), 1, False),
    )
    for move, pieces, rounded in stages:
        sent = value.astype(jnp.bfloat16) if rounded else value
        product, sent = lax.optimization_barrier((product, sent))
        moved = moved_by(sent, move)
        product = advance(product, pieces)
        sent, product, moved = lax.optimization_barrier((sent, product, moved))
        value = sent.astype(jnp.float32) + moved.astype(jnp.float32)

    product, value = lax.optimization_barrier((product, value))
    moved = [moved_by(value, move) for move in ((0, 1, 0, 0), (0, 0, 0, 1), (0, 1, 0, 1))]
    product = advance(product, len(work))
    product, value, *moved = lax.optimization_barrier((product, value, *moved))
    scale = 1.0 / (count * lax.axis_size(BLK))
    value, swapped = (value + moved[0]) * scale, (moved[1] + moved[2]) * scale
    upper = core == lax.axis_index("rhs")
    gram = jnp.concatenate([jnp.where(upper, value, swapped), jnp.where(upper, swapped, value)], axis=0)
    return product, gram


def solution(mesh):
    sizes = (4, 2, 8, 2)
    fine = Mesh(mesh.devices.reshape(sizes + (2,)), BLK + ("rhs",))
    in_specs = (P(BLK, "rhs"), P(BLK), P(BLK), P(BLK))
    out_specs = (P(BLK, "rhs"), P(None, "rhs"))
    return jax.shard_map(
        functools.partial(shards, sizes), mesh=fine, in_specs=in_specs, out_specs=out_specs, check_vma=False
    )
```

```python
import functools

import jax
import jax.numpy as jnp
from jax import lax
from jax.experimental import pallas as pl
from jax.experimental.pallas import tpu as pltpu
from jax.sharding import Mesh, PartitionSpec as P

LANES = 128
VMEM_BYTES = 12 * 2**20
STEP = 256
HALVES = 2
PIECES = 4
COPIES = 4
BLK = ("y", "xh", "z", "core")


def split_parts(base):
    high = base.astype(jnp.bfloat16).astype(jnp.float32)
    rest = base - high
    mid = rest.astype(jnp.bfloat16).astype(jnp.float32)
    low = (rest - mid).astype(jnp.bfloat16).astype(jnp.float32)
    return high, mid, low


def point_values(axial, angle, area):
    axial = axial.astype(jnp.float32) - 4.0
    angle = angle.astype(jnp.float32)
    area = area.astype(jnp.float32)
    cos, sin = jnp.cos(angle), jnp.sin(angle)
    return axial, cos, sin, axial * axial + cos * cos + sin * sin, 1.0 / (area * area)


def lay_rows(base_ref, features):
    groups = features[0].shape[0]
    base_ref[...] = jnp.zeros_like(base_ref)
    for row, feature in enumerate(features):
        for group in range(groups):
            base_ref[row : row + 1, group * LANES : (group + 1) * LANES] = feature[group : group + 1, :]


def guest_factors(geometry, base_ref, row_ref):
    axial, cos, sin, norm, scale = point_values(*geometry)
    lay_rows(base_ref, (scale, norm * scale, axial * scale, cos * scale, sin * scale))
    high, mid, low = split_parts(base_ref[...])
    stacked = jnp.concatenate([high, high, high, mid, mid, low], axis=0)
    for group in range(row_ref.shape[0] // LANES):
        part = stacked[:, group * LANES : (group + 1) * LANES]
        row_ref[group * LANES : (group + 1) * LANES, :] = part.T.astype(jnp.bfloat16)


def home_factors(geometry, base_ref, col_ref):
    axial, cos, sin, norm, scale = point_values(*geometry)
    scale = scale * base_ref.shape[1]
    double = -2.0 * scale
    lay_rows(base_ref, ((norm + 0.01) * scale, scale, axial * double, cos * double, sin * double))
    high, mid, low = split_parts(base_ref[...])
    col_ref[...] = jnp.concatenate([high, mid, low, high, mid, high], axis=0).astype(jnp.bfloat16)


def add_panels(total, row_ref, directions_ref, home, start, count, where=0):
    for low in range(0, count, STEP):
        at = start + low
        inverse = jnp.dot(row_ref[pl.ds(at, STEP), :], home, preferred_element_type=jnp.float32)
        values = lax.rsqrt(inverse).astype(jnp.bfloat16)
        directions = directions_ref[:, pl.ds(where + at, STEP)]
        total = total + jnp.dot(directions, values, preferred_element_type=jnp.float32)
    return total


def tile_product(home_ref, row_ref, directions_ref, out_ref, arrive=None):
    count = row_ref.shape[0] // HALVES

    def step_fn(step, carried):
        if arrive is not None:
            arrive(step)
        start = pl.multiple_of(step * count, count)
        out_ref[...] = add_panels(out_ref[...], row_ref, directions_ref, home_ref[...], start, count)
        return carried

    lax.fori_loop(0, HALVES, step_fn, 0)


def geometry_of(ref):
    groups = ref.shape[0] // 3
    return tuple(ref[k * groups : (k + 1) * groups, :].astype(jnp.float32) for k in range(3))


def geometry_copy(message_ref, geometry_ref, sem):
    count = message_ref.shape[1] - LANES
    return pltpu.make_async_copy(
        message_ref.at[pl.ds(0, geometry_ref.shape[0]), pl.ds(count, LANES)], geometry_ref, sem
    )


def pack_body(directions_ref, axial_ref, angle_ref, area_ref, out_ref, held_ref, sems):
    count = directions_ref.shape[0]
    part = count // COPIES
    copies = []
    for k in range(COPIES):
        rows = pl.ds(k * part, part)
        copies.append(pltpu.make_async_copy(directions_ref.at[rows], held_ref.at[rows], sems.at[k]))
    groups = axial_ref.shape[0]
    for k, ref in enumerate((axial_ref, angle_ref, area_ref)):
        place = out_ref.at[pl.ds(k * groups, groups), pl.ds(count, LANES)]
        copies.append(pltpu.make_async_copy(ref, place, sems.at[COPIES + k]))
    for copy in copies:
        copy.start()
    out_ref[3 * groups :, count:] = jnp.zeros((LANES - 3 * groups, LANES), jnp.bfloat16)
    for k in range(COPIES):
        copies[k].wait()
        for low in range(k * part, (k + 1) * part, LANES):
            out_ref[:, low : low + LANES] = held_ref[low : low + LANES, :].T
    for copy in copies[COPIES:]:
        copy.wait()


def home_body(message_ref, out_ref, home_ref, base_ref, row_ref):
    count = row_ref.shape[0]
    geometry = geometry_of(message_ref.at[pl.ds(0, 3 * count // LANES), pl.ds(count, LANES)])
    home_factors(geometry, base_ref, home_ref)
    guest_factors(geometry, base_ref, row_ref)
    out_ref[...] = jnp.zeros_like(out_ref)
    tile_product(home_ref, row_ref, message_ref, out_ref)


def guest_body(has_total, n_held, n_sources, *refs):
    refs = list(refs)
    choice_ref = refs.pop(0) if n_sources > 1 else None
    home_ref = refs.pop(0)
    sources = [refs.pop(0) for _ in range(n_sources)]
    out_ref, *refs = refs[has_total + n_held :]
    base_ref, row_ref, directions_ref, geometry_ref, sems = refs[n_held:]
    part = row_ref.shape[0] // HALVES

    def part_copy(ref, step):
        columns = pl.ds(pl.multiple_of(step * part, part), part)
        return pltpu.make_async_copy(ref.at[:, columns], directions_ref.at[:, columns], sems.at[step])

    def fetch(ref):
        geometry_copy(ref, geometry_ref, sems.at[HALVES]).start()
        for step in range(HALVES):
            part_copy(ref, step).start()

    if choice_ref is None:
        fetch(sources[0])
    else:
        for k, ref in enumerate(sources):
            pl.when(choice_ref[0] == k)(functools.partial(fetch, ref))
    geometry_copy(sources[0], geometry_ref, sems.at[HALVES]).wait()
    guest_factors(geometry_of(geometry_ref), base_ref, row_ref)
    if not has_total:
        out_ref[...] = jnp.zeros_like(out_ref)
    tile_product(
        home_ref, row_ref, directions_ref, out_ref, arrive=lambda step: part_copy(sources[0], step).wait()
    )


def piece_body(
    offset, last, home_ref, message_ref, total_ref, out_ref, base_ref, row_ref, directions_ref, geometry_ref, sems
):
    width = row_ref.shape[0]
    geometry = geometry_copy(message_ref, geometry_ref, sems.at[0])
    copy = pltpu.make_async_copy(message_ref.at[:, pl.ds(offset, width)], directions_ref, sems.at[1])
    geometry.start()
    copy.start()
    geometry.wait()
    part = slice(offset // LANES, (offset + width) // LANES)
    guest_factors([value[part] for value in geometry_of(geometry_ref)], base_ref, row_ref)
    copy.wait()
    total = add_panels(total_ref[...], row_ref, directions_ref, home_ref[...], 0, width)
    out_ref[...] = total.T if last else total


def fold_body(core_ref, value_ref, crossed_ref, out_ref):
    first = core_ref[0] == 0

    @pl.when(first)
    def _():
        out_ref[...] = value_ref[...] + value_ref[...].T

    @pl.when(jnp.logical_not(first))
    def _():
        out_ref[...] = value_ref[...].T + crossed_ref[...]


def half_gram_body(
    core_ref, own_ref, pair_ref, first_ref, second_ref, keep_ref, give_ref, sum_ref, directions_ref, sems
):
    copies = [
        pltpu.make_async_copy(ref, directions_ref.at[k], sems.at[k]) for k, ref in enumerate((own_ref, pair_ref))
    ]
    for copy in copies:
        copy.start()
    first, second = first_ref[...], second_ref[...]
    value = 0.5 * first + second
    sum_ref[...] = first + second
    high = value.astype(jnp.bfloat16)
    low = (value - high.astype(jnp.float32)).astype(jnp.bfloat16)
    both = jnp.concatenate([high, low], axis=0)
    for copy in copies:
        copy.wait()
    directions = jnp.concatenate([directions_ref[0], directions_ref[1]], axis=1)
    part = jnp.dot(both, directions, preferred_element_type=jnp.float32)
    part = part[:LANES] + part[LANES:]
    on_first = core_ref[0] == 0
    keep_ref[...] = jnp.where(on_first, part[:, :LANES], part[:, LANES:])
    give_ref[...] = jnp.where(on_first, part[:, LANES:], part[:, :LANES])


def tile_cost(count):
    return pl.CostEstimate(flops=count * count * 16, bytes_accessed=0, transcendentals=0)


def kernel_call(body, name, operands, places, outs, scratch, cost, aliases=None):
    spaces = {"v": pltpu.VMEM, "s": pltpu.SMEM, "a": pl.ANY, "h": pltpu.HBM}
    fixed = {"v": pltpu.VMEM, "h": pltpu.HBM}
    operands = [
        pltpu.with_memory_space_constraint(value, fixed[place]) if place in fixed else value
        for value, place in zip(operands, places)
    ]
    return pl.pallas_call(
        body,
        out_shape=outs,
        in_specs=[pl.BlockSpec(memory_space=spaces[place]) for place in places],
        out_specs=[pl.BlockSpec(memory_space=pltpu.VMEM)] * len(outs),
        input_output_aliases=aliases or {},
        scratch_shapes=scratch,
        cost_estimate=cost,
        compiler_params=pltpu.CompilerParams(vmem_limit_bytes=VMEM_BYTES),
        name=name,
    )(*operands)


def pack(directions, geometry):
    count = directions.shape[0]
    return kernel_call(
        pack_body, "pack", [directions, *geometry], "hhhh", [pltpu.VMEM((LANES, count + LANES), jnp.bfloat16)],
        [pltpu.VMEM((count, LANES), jnp.bfloat16), pltpu.SemaphoreType.DMA((COPIES + 3,))],
        pl.CostEstimate(flops=0, bytes_accessed=2**20, transcendentals=0),
    )[0]


def tile_scratch(count):
    return [pltpu.VMEM((8, count), jnp.float32), pltpu.VMEM((count, 48), jnp.bfloat16)]


def fetch_scratch(count, geometry_rows, copies):
    return tile_scratch(count) + [
        pltpu.VMEM((LANES, count), jnp.bfloat16),
        pltpu.VMEM((geometry_rows, LANES), jnp.bfloat16),
        pltpu.SemaphoreType.DMA((copies,)),
    ]


def home_tile(message, count):
    outs = [pltpu.VMEM((LANES, count), jnp.float32), pltpu.VMEM((48, count), jnp.bfloat16)]
    return kernel_call(home_body, "home_tile", [message], "v", outs, tile_scratch(count), tile_cost(count))


def guest_tile(home, sources, total=None, held=(), choice=None):
    count = home.shape[1]
    totals = [] if total is None else [total]
    choices = [] if choice is None else [choice]
    place = len(choices) + 1 + len(sources)
    aliases = {place: 0} if totals else {}
    aliases.update({place + len(totals) + k: 1 + k for k in range(len(held))})
    return kernel_call(
        functools.partial(guest_body, len(totals), len(held), len(sources)), "guest_tile",
        [*choices, home, *sources, *totals, *held],
        "s" * len(choices) + "v" + "a" * len(sources) + "v" * (len(totals) + len(held)),
        [pltpu.VMEM((LANES, count), jnp.float32)] * (1 + len(held)),
        fetch_scratch(count, 3 * count // LANES, HALVES + 1), tile_cost(count), aliases,
    )


def piece_tile(home, message, total, piece, last):
    count = home.shape[1]
    width = count // PIECES
    out = jax.ShapeDtypeStruct((count, LANES), jnp.float32) if last else pltpu.VMEM((LANES, count), jnp.float32)
    return kernel_call(
        functools.partial(piece_body, piece * width, last), "piece_tile", [home, message, total], "vav", [out],
        fetch_scratch(width, 3 * count // LANES, 2), tile_cost(count), None if last else {2: 0},
    )[0]


def half_gram(core, own, pair, first, second):
    count = first.shape[1]
    block = pltpu.VMEM((LANES, LANES), jnp.float32)
    return kernel_call(
        half_gram_body, "half_gram", [core, own, pair, first, second], "shavv",
        [block, block, pltpu.VMEM((LANES, count), jnp.float32)],
        [pltpu.VMEM((2, count, LANES), jnp.bfloat16), pltpu.SemaphoreType.DMA((2,))], tile_cost(count), {3: 2},
    )


def fold(core, *blocks):
    out = pltpu.VMEM((LANES, LANES), jnp.float32)
    cost = pl.CostEstimate(flops=0, bytes_accessed=2**17, transcendentals=0)
    return kernel_call(fold_body, "fold", [core, *blocks], "svv", [out], [], cost)[0]


def along_blk(value, sizes, target):
    ny, nx, nz, nc = sizes

    def index(y, x, z, c):
        return ((y % ny * nx + x % nx) * nz + z % nz) * nc + c % nc

    pairs = []
    for y in range(ny):
        for x in range(nx):
            for z in range(nz):
                for c in range(nc):
                    pairs.append((index(y, x, z, c), index(*target(y, x, z, c))))
    return lax.ppermute(value, BLK, pairs)


def from_neighbour(value, parity):
    count = lax.axis_size(BLK)
    pairs = []
    for block in range(count):
        chip, core = divmod(block, 2)
        first = chip % 2 == parity
        other = 2 * (chip + 1) + 1 - core if first else 2 * (chip - 1) + core
        pairs.append((block, other % count))
    return lax.ppermute(value, BLK, pairs)


def from_far(value):
    count = lax.axis_size(BLK)
    return lax.ppermute(
        value, BLK, [((b - 3 if b % 2 == 0 else b + 3) % count, b) for b in range(count)]
    )


def core_swap(value):
    return lax.ppermute(value, "core", [(0, 1), (1, 0)])


def shards(sizes, directions, axial_pos, azimuth, panel_area):
    count = axial_pos.shape[0]
    geometry = [part.reshape(count // LANES, LANES) for part in (axial_pos, azimuth, panel_area)]
    message = pack(directions, geometry)
    other = core_swap(message)
    even = from_neighbour(message, 0)
    odd = from_neighbour(message, 1)

    first, home = home_tile(message, count)
    first, late = lax.optimization_barrier((first, message))
    far = from_far(late)
    (first,) = guest_tile(home, (other,), first)
    first, even, later = lax.optimization_barrier((first, even, directions))
    pair = lax.ppermute(later, "rhs", [(0, 1), (1, 0)])
    even_other = core_swap(even)
    second, first = guest_tile(home, (even,), None, (first,))
    second, odd = lax.optimization_barrier((second, odd))
    odd_other = core_swap(odd)
    second, first = guest_tile(home, (odd,), second, (first,))
    second, far = lax.optimization_barrier((second, far))
    core = lax.axis_index("core").astype(jnp.int32)
    first, second = guest_tile(home, (far,), first, (second,))
    keep, give, product = half_gram(core.reshape(1), directions, pair, first, second)

    work = [(guest, piece) for guest in (even_other, odd_other) for piece in range(PIECES)]

    def advance(product, pieces):
        for _ in range(pieces):
            guest, piece = work.pop(0)
            product = piece_tile(home, guest, product, piece, not work)
        return product

    value = keep + core_swap(give)
    value, product = lax.optimization_barrier((value, product))
    crossed = lax.ppermute(value, ("core", "rhs"), [(2, 3), (3, 2)])
    product = advance(product, 1)
    value, crossed, product = lax.optimization_barrier((value, crossed, product))
    value = fold(core.reshape(1), value, crossed)

    def moved_by(sent, move):
        return along_blk(
            sent, sizes, lambda y, x, z, c: (y ^ move[0], x ^ move[1], z ^ move[2], c ^ move[3])
        )

    stages = (
        ((0, 0, 4, 0), 2, True), ((0, 0, 2, 0), 1, True), ((0, 0, 1, 0), 1, False),
        ((2, 0, 0, 0), 1, True), ((1, 0, 0, 0), 1, False),
    )
    for move, pieces, rounded in stages:
        sent = value.astype(jnp.bfloat16) if rounded else value
        product, sent = lax.optimization_barrier((product, sent))
        moved = moved_by(sent, move)
        product = advance(product, pieces)
        sent, product, moved = lax.optimization_barrier((sent, product, moved))
        value = sent.astype(jnp.float32) + moved.astype(jnp.float32)

    product, value = lax.optimization_barrier((product, value))
    moved = [moved_by(value, move) for move in ((0, 1, 0, 0), (0, 0, 0, 1), (0, 1, 0, 1))]
    product = advance(product, len(work))
    product, value, *moved = lax.optimization_barrier((product, value, *moved))
    scale = 1.0 / (count * lax.axis_size(BLK))
    value, swapped = (value + moved[0]) * scale, (moved[1] + moved[2]) * scale
    upper = core == lax.axis_index("rhs")
    gram = jnp.concatenate([jnp.where(upper, value, swapped), jnp.where(upper, swapped, value)], axis=0)
    return product, gram


def solution(mesh):
    sizes = (4, 2, 8, 2)
    fine = Mesh(mesh.devices.reshape(sizes + (2,)), BLK + ("rhs",))
    in_specs = (P(BLK, "rhs"), P(BLK), P(BLK), P(BLK))
    out_specs = (P(BLK, "rhs"), P(None, "rhs"))
    return jax.shard_map(
        functools.partial(shards, sizes), mesh=fine, in_specs=in_specs, out_specs=out_specs, check_vma=False
    )
```

```python
import functools

import jax
import jax.numpy as jnp
from jax import lax
from jax.experimental import pallas as pl
from jax.experimental.pallas import tpu as pltpu
from jax.sharding import Mesh, PartitionSpec as P

LANES = 128
VMEM_BYTES = 12 * 2**20
STEP = 256
HALVES = 2
PIECES = 4
COPIES = 4
BLK = ("y", "xh", "z", "core")


def split_parts(base):
    high = base.astype(jnp.bfloat16).astype(jnp.float32)
    rest = base - high
    mid = rest.astype(jnp.bfloat16).astype(jnp.float32)
    low = (rest - mid).astype(jnp.bfloat16).astype(jnp.float32)
    return high, mid, low


def point_values(axial, angle, area):
    axial = axial.astype(jnp.float32) - 4.0
    angle = angle.astype(jnp.float32)
    area = area.astype(jnp.float32)
    cos, sin = jnp.cos(angle), jnp.sin(angle)
    return axial, cos, sin, axial * axial + cos * cos + sin * sin, 1.0 / (area * area)


def lay_rows(base_ref, features):
    groups = features[0].shape[0]
    base_ref[...] = jnp.zeros_like(base_ref)
    for row, feature in enumerate(features):
        for group in range(groups):
            base_ref[row : row + 1, group * LANES : (group + 1) * LANES] = feature[group : group + 1, :]


def guest_factors(geometry, base_ref, row_ref):
    axial, cos, sin, norm, scale = point_values(*geometry)
    lay_rows(base_ref, (scale, norm * scale, axial * scale, cos * scale, sin * scale))
    high, mid, low = split_parts(base_ref[...])
    stacked = jnp.concatenate([high, high, high, mid, mid, low], axis=0)
    for group in range(row_ref.shape[0] // LANES):
        part = stacked[:, group * LANES : (group + 1) * LANES]
        row_ref[group * LANES : (group + 1) * LANES, :] = part.T.astype(jnp.bfloat16)


def home_factors(geometry, base_ref, col_ref):
    axial, cos, sin, norm, scale = point_values(*geometry)
    scale = scale * base_ref.shape[1]
    double = -2.0 * scale
    lay_rows(base_ref, ((norm + 0.01) * scale, scale, axial * double, cos * double, sin * double))
    high, mid, low = split_parts(base_ref[...])
    col_ref[...] = jnp.concatenate([high, mid, low, high, mid, high], axis=0).astype(jnp.bfloat16)


def add_panels(total, row_ref, directions_ref, home, start, count, where=0):
    for low in range(0, count, STEP):
        at = start + low
        inverse = jnp.dot(row_ref[pl.ds(at, STEP), :], home, preferred_element_type=jnp.float32)
        values = lax.rsqrt(inverse).astype(jnp.bfloat16)
        directions = directions_ref[:, pl.ds(where + at, STEP)]
        total = total + jnp.dot(directions, values, preferred_element_type=jnp.float32)
    return total


def tile_product(home_ref, row_ref, directions_ref, out_ref, arrive=None):
    count = row_ref.shape[0] // HALVES

    def step_fn(step, carried):
        if arrive is not None:
            arrive(step)
        start = pl.multiple_of(step * count, count)
        out_ref[...] = add_panels(out_ref[...], row_ref, directions_ref, home_ref[...], start, count)
        return carried

    lax.fori_loop(0, HALVES, step_fn, 0)


def geometry_of(ref):
    groups = ref.shape[0] // 3
    return tuple(ref[k * groups : (k + 1) * groups, :].astype(jnp.float32) for k in range(3))


def geometry_copy(message_ref, geometry_ref, sem):
    count = message_ref.shape[1] - LANES
    return pltpu.make_async_copy(
        message_ref.at[pl.ds(0, geometry_ref.shape[0]), pl.ds(count, LANES)], geometry_ref, sem
    )


def pack_body(directions_ref, axial_ref, angle_ref, area_ref, out_ref, held_ref, sems):
    count = directions_ref.shape[0]
    part = count // COPIES
    copies = []
    for k in range(COPIES):
        rows = pl.ds(k * part, part)
        copies.append(pltpu.make_async_copy(directions_ref.at[rows], held_ref.at[rows], sems.at[k]))
    groups = axial_ref.shape[0]
    for k, ref in enumerate((axial_ref, angle_ref, area_ref)):
        place = out_ref.at[pl.ds(k * groups, groups), pl.ds(count, LANES)]
        copies.append(pltpu.make_async_copy(ref, place, sems.at[COPIES + k]))
    for copy in copies:
        copy.start()
    out_ref[3 * groups :, count:] = jnp.zeros((LANES - 3 * groups, LANES), jnp.bfloat16)
    for k in range(COPIES):
        copies[k].wait()
        for low in range(k * part, (k + 1) * part, LANES):
            out_ref[:, low : low + LANES] = held_ref[low : low + LANES, :].T
    for copy in copies[COPIES:]:
        copy.wait()


def home_body(message_ref, out_ref, home_ref, base_ref, row_ref):
    count = row_ref.shape[0]
    geometry = geometry_of(message_ref.at[pl.ds(0, 3 * count // LANES), pl.ds(count, LANES)])
    home_factors(geometry, base_ref, home_ref)
    guest_factors(geometry, base_ref, row_ref)
    out_ref[...] = jnp.zeros_like(out_ref)
    tile_product(home_ref, row_ref, message_ref, out_ref)


def guest_body(has_total, n_held, n_sources, *refs):
    refs = list(refs)
    choice_ref = refs.pop(0) if n_sources > 1 else None
    home_ref = refs.pop(0)
    sources = [refs.pop(0) for _ in range(n_sources)]
    out_ref, *refs = refs[has_total + n_held :]
    base_ref, row_ref, directions_ref, geometry_ref, sems = refs[n_held:]
    part = row_ref.shape[0] // HALVES

    def part_copy(ref, step):
        columns = pl.ds(pl.multiple_of(step * part, part), part)
        return pltpu.make_async_copy(ref.at[:, columns], directions_ref.at[:, columns], sems.at[step])

    def fetch(ref):
        geometry_copy(ref, geometry_ref, sems.at[HALVES]).start()
        for step in range(HALVES):
            part_copy(ref, step).start()

    if choice_ref is None:
        fetch(sources[0])
    else:
        for k, ref in enumerate(sources):
            pl.when(choice_ref[0] == k)(functools.partial(fetch, ref))
    geometry_copy(sources[0], geometry_ref, sems.at[HALVES]).wait()
    guest_factors(geometry_of(geometry_ref), base_ref, row_ref)
    if not has_total:
        out_ref[...] = jnp.zeros_like(out_ref)
    tile_product(
        home_ref, row_ref, directions_ref, out_ref, arrive=lambda step: part_copy(sources[0], step).wait()
    )


def piece_body(
    offset, last, home_ref, message_ref, total_ref, out_ref, base_ref, row_ref, directions_ref, geometry_ref, sems
):
    width = row_ref.shape[0]
    geometry = geometry_copy(message_ref, geometry_ref, sems.at[0])
    copy = pltpu.make_async_copy(message_ref.at[:, pl.ds(offset, width)], directions_ref, sems.at[1])
    geometry.start()
    copy.start()
    geometry.wait()
    part = slice(offset // LANES, (offset + width) // LANES)
    guest_factors([value[part] for value in geometry_of(geometry_ref)], base_ref, row_ref)
    copy.wait()
    total = add_panels(total_ref[...], row_ref, directions_ref, home_ref[...], 0, width)
    out_ref[...] = total.T if last else total


def fold_body(core_ref, value_ref, crossed_ref, out_ref):
    first = core_ref[0] == 0

    @pl.when(first)
    def _():
        out_ref[...] = value_ref[...] + value_ref[...].T

    @pl.when(jnp.logical_not(first))
    def _():
        out_ref[...] = value_ref[...].T + crossed_ref[...]


def half_gram_body(
    core_ref, own_ref, pair_ref, first_ref, second_ref, keep_ref, give_ref, sum_ref, directions_ref, sems
):
    copies = [
        pltpu.make_async_copy(ref, directions_ref.at[k], sems.at[k]) for k, ref in enumerate((own_ref, pair_ref))
    ]
    for copy in copies:
        copy.start()
    first, second = first_ref[...], second_ref[...]
    value = 0.5 * first + second
    sum_ref[...] = first + second
    high = value.astype(jnp.bfloat16)
    low = (value - high.astype(jnp.float32)).astype(jnp.bfloat16)
    both = jnp.concatenate([high, low], axis=0)
    for copy in copies:
        copy.wait()
    directions = jnp.concatenate([directions_ref[0], directions_ref[1]], axis=1)
    part = jnp.dot(both, directions, preferred_element_type=jnp.float32)
    part = part[:LANES] + part[LANES:]
    on_first = core_ref[0] == 0
    keep_ref[...] = jnp.where(on_first, part[:, :LANES], part[:, LANES:])
    give_ref[...] = jnp.where(on_first, part[:, LANES:], part[:, :LANES])


def tile_cost(count):
    return pl.CostEstimate(flops=count * count * 16, bytes_accessed=0, transcendentals=0)


def kernel_call(body, name, operands, places, outs, scratch, cost, aliases=None):
    spaces = {"v": pltpu.VMEM, "s": pltpu.SMEM, "a": pl.ANY, "h": pltpu.HBM}
    fixed = {"v": pltpu.VMEM, "h": pltpu.HBM}
    operands = [
        pltpu.with_memory_space_constraint(value, fixed[place]) if place in fixed else value
        for value, place in zip(operands, places)
    ]
    return pl.pallas_call(
        body,
        out_shape=outs,
        in_specs=[pl.BlockSpec(memory_space=spaces[place]) for place in places],
        out_specs=[pl.BlockSpec(memory_space=pltpu.VMEM)] * len(outs),
        input_output_aliases=aliases or {},
        scratch_shapes=scratch,
        cost_estimate=cost,
        compiler_params=pltpu.CompilerParams(vmem_limit_bytes=VMEM_BYTES),
        name=name,
    )(*operands)


def pack(directions, geometry):
    count = directions.shape[0]
    return kernel_call(
        pack_body, "pack", [directions, *geometry], "hhhh", [pltpu.VMEM((LANES, count + LANES), jnp.bfloat16)],
        [pltpu.VMEM((count, LANES), jnp.bfloat16), pltpu.SemaphoreType.DMA((COPIES + 3,))],
        pl.CostEstimate(flops=0, bytes_accessed=2**20, transcendentals=0),
    )[0]


def tile_scratch(count):
    return [pltpu.VMEM((8, count), jnp.float32), pltpu.VMEM((count, 48), jnp.bfloat16)]


def fetch_scratch(count, geometry_rows, copies):
    return tile_scratch(count) + [
        pltpu.VMEM((LANES, count), jnp.bfloat16),
        pltpu.VMEM((geometry_rows, LANES), jnp.bfloat16),
        pltpu.SemaphoreType.DMA((copies,)),
    ]


def home_tile(message, count):
    outs = [pltpu.VMEM((LANES, count), jnp.float32), pltpu.VMEM((48, count), jnp.bfloat16)]
    return kernel_call(home_body, "home_tile", [message], "v", outs, tile_scratch(count), tile_cost(count))


def guest_tile(home, sources, total=None, held=(), choice=None):
    count = home.shape[1]
    totals = [] if total is None else [total]
    choices = [] if choice is None else [choice]
    place = len(choices) + 1 + len(sources)
    aliases = {place: 0} if totals else {}
    aliases.update({place + len(totals) + k: 1 + k for k in range(len(held))})
    return kernel_call(
        functools.partial(guest_body, len(totals), len(held), len(sources)), "guest_tile",
        [*choices, home, *sources, *totals, *held],
        "s" * len(choices) + "v" + "a" * len(sources) + "v" * (len(totals) + len(held)),
        [pltpu.VMEM((LANES, count), jnp.float32)] * (1 + len(held)),
        fetch_scratch(count, 3 * count // LANES, HALVES + 1), tile_cost(count), aliases,
    )


def piece_tile(home, message, total, piece, last):
    count = home.shape[1]
    width = count // PIECES
    out = jax.ShapeDtypeStruct((count, LANES), jnp.float32) if last else pltpu.VMEM((LANES, count), jnp.float32)
    return kernel_call(
        functools.partial(piece_body, piece * width, last), "piece_tile", [home, message, total], "vav", [out],
        fetch_scratch(width, 3 * count // LANES, 2), tile_cost(count), None if last else {2: 0},
    )[0]


def half_gram(core, own, pair, first, second):
    count = first.shape[1]
    block = pltpu.VMEM((LANES, LANES), jnp.float32)
    return kernel_call(
        half_gram_body, "half_gram", [core, own, pair, first, second], "shavv",
        [block, block, pltpu.VMEM((LANES, count), jnp.float32)],
        [pltpu.VMEM((2, count, LANES), jnp.bfloat16), pltpu.SemaphoreType.DMA((2,))], tile_cost(count), {3: 2},
    )


def fold(core, *blocks):
    out = pltpu.VMEM((LANES, LANES), jnp.float32)
    cost = pl.CostEstimate(flops=0, bytes_accessed=2**17, transcendentals=0)
    return kernel_call(fold_body, "fold", [core, *blocks], "svv", [out], [], cost)[0]


def along_blk(value, sizes, target):
    ny, nx, nz, nc = sizes

    def index(y, x, z, c):
        return ((y % ny * nx + x % nx) * nz + z % nz) * nc + c % nc

    pairs = []
    for y in range(ny):
        for x in range(nx):
            for z in range(nz):
                for c in range(nc):
                    pairs.append((index(y, x, z, c), index(*target(y, x, z, c))))
    return lax.ppermute(value, BLK, pairs)


def from_neighbour(value, parity):
    count = lax.axis_size(BLK)
    pairs = []
    for block in range(count):
        chip, core = divmod(block, 2)
        first = chip % 2 == parity
        other = 2 * (chip + 1) + 1 - core if first else 2 * (chip - 1) + core
        pairs.append((block, other % count))
    return lax.ppermute(value, BLK, pairs)


def from_far(value):
    count = lax.axis_size(BLK)
    return lax.ppermute(
        value, BLK, [((b - 3 if b % 2 == 0 else b + 3) % count, b) for b in range(count)]
    )


def core_swap(value):
    return lax.ppermute(value, "core", [(0, 1), (1, 0)])


def shards(sizes, directions, axial_pos, azimuth, panel_area):
    count = axial_pos.shape[0]
    geometry = [part.reshape(count // LANES, LANES) for part in (axial_pos, azimuth, panel_area)]
    message = pack(directions, geometry)
    other = core_swap(message)
    even = from_neighbour(message, 0)
    odd = from_neighbour(message, 1)

    first, home = home_tile(message, count)
    first, late = lax.optimization_barrier((first, message))
    far = from_far(late)
    (first,) = guest_tile(home, (other,), first)
    first, even, later = lax.optimization_barrier((first, even, directions))
    pair = lax.ppermute(later, "rhs", [(0, 1), (1, 0)])
    even_other = core_swap(even)
    second, first = guest_tile(home, (even,), None, (first,))
    second, odd = lax.optimization_barrier((second, odd))
    odd_other = core_swap(odd)
    second, first = guest_tile(home, (odd,), second, (first,))
    second, far = lax.optimization_barrier((second, far))
    core = lax.axis_index("core").astype(jnp.int32)
    first, second = guest_tile(home, (far,), first, (second,))
    keep, give, product = half_gram(core.reshape(1), directions, pair, first, second)

    work = [(guest, piece) for guest in (even_other, odd_other) for piece in range(PIECES)]

    def advance(product, pieces):
        for _ in range(pieces):
            guest, piece = work.pop(0)
            product = piece_tile(home, guest, product, piece, not work)
        return product

    value = keep + core_swap(give)
    value, product = lax.optimization_barrier((value, product))
    crossed = lax.ppermute(value, ("core", "rhs"), [(2, 3), (3, 2)])
    product = advance(product, 1)
    value, crossed, product = lax.optimization_barrier((value, crossed, product))
    value = fold(core.reshape(1), value, crossed)

    def moved_by(sent, move):
        return along_blk(
            sent, sizes, lambda y, x, z, c: (y ^ move[0], x ^ move[1], z ^ move[2], c ^ move[3])
        )

    stages = (
        (((0, 0, 4, 0),), 2),
        (((0, 0, 1, 0), (0, 0, 2, 0), (0, 0, 3, 0)), 2),
        (((1, 0, 0, 0), (2, 0, 0, 0), (3, 0, 0, 0)), 2),
    )
    for moves, pieces in stages:
        sent = value.astype(jnp.bfloat16)
        product, sent = lax.optimization_barrier((product, sent))
        moved = [moved_by(sent, move) for move in moves]
        product = advance(product, pieces)
        sent, product, *moved = lax.optimization_barrier((sent, product, *moved))
        value, *moved = [term.astype(jnp.float32) for term in (sent, *moved)]
        value = value + moved[0]
        if len(moved) > 1:
            value = value + (moved[1] + moved[2])

    product, value = lax.optimization_barrier((product, value))
    moved = [moved_by(value, move) for move in ((0, 1, 0, 0), (0, 0, 0, 1), (0, 1, 0, 1))]
    product = advance(product, len(work))
    product, value, *moved = lax.optimization_barrier((product, value, *moved))
    scale = 1.0 / (count * lax.axis_size(BLK))
    value, swapped = (value + moved[0]) * scale, (moved[1] + moved[2]) * scale
    upper = core == lax.axis_index("rhs")
    gram = jnp.concatenate([jnp.where(upper, value, swapped), jnp.where(upper, swapped, value)], axis=0)
    return product, gram


def solution(mesh):
    sizes = (4, 2, 8, 2)
    fine = Mesh(mesh.devices.reshape(sizes + (2,)), BLK + ("rhs",))
    in_specs = (P(BLK, "rhs"), P(BLK), P(BLK), P(BLK))
    out_specs = (P(BLK, "rhs"), P(None, "rhs"))
    return jax.shard_map(
        functools.partial(shards, sizes), mesh=fine, in_specs=in_specs, out_specs=out_specs, check_vma=False
    )
```

```python
import functools

import jax
import jax.numpy as jnp
from jax import lax
from jax.experimental import pallas as pl
from jax.experimental.pallas import tpu as pltpu
from jax.sharding import Mesh, PartitionSpec as P

LANES = 128
VMEM_BYTES = 12 * 2**20
STEP = 256
HALVES = 2
PIECES = 4
COPIES = 4
BLK = ("y", "xh", "z", "core")


def split_parts(base):
    high = base.astype(jnp.bfloat16).astype(jnp.float32)
    rest = base - high
    mid = rest.astype(jnp.bfloat16).astype(jnp.float32)
    low = (rest - mid).astype(jnp.bfloat16).astype(jnp.float32)
    return high, mid, low


def point_values(axial, angle, area):
    axial = axial.astype(jnp.float32) - 4.0
    angle = angle.astype(jnp.float32)
    area = area.astype(jnp.float32)
    cos, sin = jnp.cos(angle), jnp.sin(angle)
    return axial, cos, sin, axial * axial + cos * cos + sin * sin, 1.0 / (area * area)


def lay_rows(base_ref, features):
    groups = features[0].shape[0]
    base_ref[...] = jnp.zeros_like(base_ref)
    for row, feature in enumerate(features):
        for group in range(groups):
            base_ref[row : row + 1, group * LANES : (group + 1) * LANES] = feature[group : group + 1, :]


def guest_factors(geometry, base_ref, row_ref):
    axial, cos, sin, norm, scale = point_values(*geometry)
    lay_rows(base_ref, (scale, norm * scale, axial * scale, cos * scale, sin * scale))
    high, mid, low = split_parts(base_ref[...])
    stacked = jnp.concatenate([high, high, high, mid, mid, low], axis=0)
    for group in range(row_ref.shape[0] // LANES):
        part = stacked[:, group * LANES : (group + 1) * LANES]
        row_ref[group * LANES : (group + 1) * LANES, :] = part.T.astype(jnp.bfloat16)


def home_factors(geometry, base_ref, col_ref):
    axial, cos, sin, norm, scale = point_values(*geometry)
    scale = scale * base_ref.shape[1]
    double = -2.0 * scale
    lay_rows(base_ref, ((norm + 0.01) * scale, scale, axial * double, cos * double, sin * double))
    high, mid, low = split_parts(base_ref[...])
    col_ref[...] = jnp.concatenate([high, mid, low, high, mid, high], axis=0).astype(jnp.bfloat16)


def add_panels(total, row_ref, directions_ref, home, start, count, where=0):
    for low in range(0, count, STEP):
        at = start + low
        inverse = jnp.dot(row_ref[pl.ds(at, STEP), :], home, preferred_element_type=jnp.float32)
        values = lax.rsqrt(inverse).astype(jnp.bfloat16)
        directions = directions_ref[:, pl.ds(where + at, STEP)]
        total = total + jnp.dot(directions, values, preferred_element_type=jnp.float32)
    return total


def tile_product(home_ref, row_ref, directions_ref, out_ref, arrive=None):
    count = row_ref.shape[0] // HALVES

    def step_fn(step, carried):
        if arrive is not None:
            arrive(step)
        start = pl.multiple_of(step * count, count)
        out_ref[...] = add_panels(out_ref[...], row_ref, directions_ref, home_ref[...], start, count)
        return carried

    lax.fori_loop(0, HALVES, step_fn, 0)


def geometry_of(ref):
    groups = ref.shape[0] // 3
    return tuple(ref[k * groups : (k + 1) * groups, :].astype(jnp.float32) for k in range(3))


def geometry_copy(message_ref, geometry_ref, sem):
    count = message_ref.shape[1] - LANES
    return pltpu.make_async_copy(
        message_ref.at[pl.ds(0, geometry_ref.shape[0]), pl.ds(count, LANES)], geometry_ref, sem
    )


def pack_body(directions_ref, axial_ref, angle_ref, area_ref, out_ref, held_ref, sems):
    count = directions_ref.shape[0]
    part = count // COPIES
    copies = []
    for k in range(COPIES):
        rows = pl.ds(k * part, part)
        copies.append(pltpu.make_async_copy(directions_ref.at[rows], held_ref.at[rows], sems.at[k]))
    groups = axial_ref.shape[0]
    for k, ref in enumerate((axial_ref, angle_ref, area_ref)):
        place = out_ref.at[pl.ds(k * groups, groups), pl.ds(count, LANES)]
        copies.append(pltpu.make_async_copy(ref, place, sems.at[COPIES + k]))
    for copy in copies:
        copy.start()
    out_ref[3 * groups :, count:] = jnp.zeros((LANES - 3 * groups, LANES), jnp.bfloat16)
    for k in range(COPIES):
        copies[k].wait()
        for low in range(k * part, (k + 1) * part, LANES):
            out_ref[:, low : low + LANES] = held_ref[low : low + LANES, :].T
    for copy in copies[COPIES:]:
        copy.wait()


def home_body(message_ref, out_ref, home_ref, base_ref, row_ref):
    count = row_ref.shape[0]
    geometry = geometry_of(message_ref.at[pl.ds(0, 3 * count // LANES), pl.ds(count, LANES)])
    home_factors(geometry, base_ref, home_ref)
    guest_factors(geometry, base_ref, row_ref)
    out_ref[...] = jnp.zeros_like(out_ref)
    tile_product(home_ref, row_ref, message_ref, out_ref)


def guest_body(has_total, n_held, n_sources, *refs):
    refs = list(refs)
    choice_ref = refs.pop(0) if n_sources > 1 else None
    home_ref = refs.pop(0)
    sources = [refs.pop(0) for _ in range(n_sources)]
    out_ref, *refs = refs[has_total + n_held :]
    base_ref, row_ref, directions_ref, geometry_ref, sems = refs[n_held:]
    part = row_ref.shape[0] // HALVES

    def part_copy(ref, step):
        columns = pl.ds(pl.multiple_of(step * part, part), part)
        return pltpu.make_async_copy(ref.at[:, columns], directions_ref.at[:, columns], sems.at[step])

    def fetch(ref):
        geometry_copy(ref, geometry_ref, sems.at[HALVES]).start()
        for step in range(HALVES):
            part_copy(ref, step).start()

    if choice_ref is None:
        fetch(sources[0])
    else:
        for k, ref in enumerate(sources):
            pl.when(choice_ref[0] == k)(functools.partial(fetch, ref))
    geometry_copy(sources[0], geometry_ref, sems.at[HALVES]).wait()
    guest_factors(geometry_of(geometry_ref), base_ref, row_ref)
    if not has_total:
        out_ref[...] = jnp.zeros_like(out_ref)
    tile_product(
        home_ref, row_ref, directions_ref, out_ref, arrive=lambda step: part_copy(sources[0], step).wait()
    )


def piece_body(
    offset, last, home_ref, message_ref, total_ref, out_ref, base_ref, row_ref, directions_ref, geometry_ref, sems
):
    width = row_ref.shape[0]
    geometry = geometry_copy(message_ref, geometry_ref, sems.at[0])
    copy = pltpu.make_async_copy(message_ref.at[:, pl.ds(offset, width)], directions_ref, sems.at[1])
    geometry.start()
    copy.start()
    geometry.wait()
    part = slice(offset // LANES, (offset + width) // LANES)
    guest_factors([value[part] for value in geometry_of(geometry_ref)], base_ref, row_ref)
    copy.wait()
    total = add_panels(total_ref[...], row_ref, directions_ref, home_ref[...], 0, width)
    out_ref[...] = total.T if last else total


def fold_body(core_ref, value_ref, crossed_ref, out_ref):
    first = core_ref[0] == 0

    @pl.when(first)
    def _():
        out_ref[...] = value_ref[...] + value_ref[...].T

    @pl.when(jnp.logical_not(first))
    def _():
        out_ref[...] = value_ref[...].T + crossed_ref[...]


def half_gram_body(
    core_ref, own_ref, pair_ref, first_ref, second_ref, keep_ref, give_ref, sum_ref, directions_ref, sems
):
    copies = [
        pltpu.make_async_copy(ref, directions_ref.at[k], sems.at[k]) for k, ref in enumerate((own_ref, pair_ref))
    ]
    for copy in copies:
        copy.start()
    first, second = first_ref[...], second_ref[...]
    value = 0.5 * first + second
    sum_ref[...] = first + second
    high = value.astype(jnp.bfloat16)
    low = (value - high.astype(jnp.float32)).astype(jnp.bfloat16)
    both = jnp.concatenate([high, low], axis=0)
    for copy in copies:
        copy.wait()
    directions = jnp.concatenate([directions_ref[0], directions_ref[1]], axis=1)
    part = jnp.dot(both, directions, preferred_element_type=jnp.float32)
    part = part[:LANES] + part[LANES:]
    on_first = core_ref[0] == 0
    keep_ref[...] = jnp.where(on_first, part[:, :LANES], part[:, LANES:])
    give_ref[...] = jnp.where(on_first, part[:, LANES:], part[:, :LANES])


def tile_cost(count):
    return pl.CostEstimate(flops=count * count * 16, bytes_accessed=0, transcendentals=0)


def kernel_call(body, name, operands, places, outs, scratch, cost, aliases=None):
    spaces = {"v": pltpu.VMEM, "s": pltpu.SMEM, "a": pl.ANY, "h": pltpu.HBM}
    fixed = {"v": pltpu.VMEM, "h": pltpu.HBM}
    operands = [
        pltpu.with_memory_space_constraint(value, fixed[place]) if place in fixed else value
        for value, place in zip(operands, places)
    ]
    return pl.pallas_call(
        body,
        out_shape=outs,
        in_specs=[pl.BlockSpec(memory_space=spaces[place]) for place in places],
        out_specs=[pl.BlockSpec(memory_space=pltpu.VMEM)] * len(outs),
        input_output_aliases=aliases or {},
        scratch_shapes=scratch,
        cost_estimate=cost,
        compiler_params=pltpu.CompilerParams(vmem_limit_bytes=VMEM_BYTES),
        name=name,
    )(*operands)


def pack(directions, geometry):
    count = directions.shape[0]
    return kernel_call(
        pack_body, "pack", [directions, *geometry], "hhhh", [pltpu.VMEM((LANES, count + LANES), jnp.bfloat16)],
        [pltpu.VMEM((count, LANES), jnp.bfloat16), pltpu.SemaphoreType.DMA((COPIES + 3,))],
        pl.CostEstimate(flops=0, bytes_accessed=2**20, transcendentals=0),
    )[0]


def tile_scratch(count):
    return [pltpu.VMEM((8, count), jnp.float32), pltpu.VMEM((count, 48), jnp.bfloat16)]


def fetch_scratch(count, geometry_rows, copies):
    return tile_scratch(count) + [
        pltpu.VMEM((LANES, count), jnp.bfloat16),
        pltpu.VMEM((geometry_rows, LANES), jnp.bfloat16),
        pltpu.SemaphoreType.DMA((copies,)),
    ]


def home_tile(message, count):
    outs = [pltpu.VMEM((LANES, count), jnp.float32), pltpu.VMEM((48, count), jnp.bfloat16)]
    return kernel_call(home_body, "home_tile", [message], "v", outs, tile_scratch(count), tile_cost(count))


def guest_tile(home, sources, total=None, held=(), choice=None):
    count = home.shape[1]
    totals = [] if total is None else [total]
    choices = [] if choice is None else [choice]
    place = len(choices) + 1 + len(sources)
    aliases = {place: 0} if totals else {}
    aliases.update({place + len(totals) + k: 1 + k for k in range(len(held))})
    return kernel_call(
        functools.partial(guest_body, len(totals), len(held), len(sources)), "guest_tile",
        [*choices, home, *sources, *totals, *held],
        "s" * len(choices) + "v" + "a" * len(sources) + "v" * (len(totals) + len(held)),
        [pltpu.VMEM((LANES, count), jnp.float32)] * (1 + len(held)),
        fetch_scratch(count, 3 * count // LANES, HALVES + 1), tile_cost(count), aliases,
    )


def piece_tile(home, message, total, piece, last):
    count = home.shape[1]
    width = count // PIECES
    out = jax.ShapeDtypeStruct((count, LANES), jnp.float32) if last else pltpu.VMEM((LANES, count), jnp.float32)
    return kernel_call(
        functools.partial(piece_body, piece * width, last), "piece_tile", [home, message, total], "vhv", [out],
        fetch_scratch(width, 3 * count // LANES, 2), tile_cost(count), None if last else {2: 0},
    )[0]


def half_gram(core, own, pair, first, second):
    count = first.shape[1]
    block = pltpu.VMEM((LANES, LANES), jnp.float32)
    return kernel_call(
        half_gram_body, "half_gram", [core, own, pair, first, second], "shavv",
        [block, block, pltpu.VMEM((LANES, count), jnp.float32)],
        [pltpu.VMEM((2, count, LANES), jnp.bfloat16), pltpu.SemaphoreType.DMA((2,))], tile_cost(count), {3: 2},
    )


def fold(core, *blocks):
    out = pltpu.VMEM((LANES, LANES), jnp.float32)
    cost = pl.CostEstimate(flops=0, bytes_accessed=2**17, transcendentals=0)
    return kernel_call(fold_body, "fold", [core, *blocks], "svv", [out], [], cost)[0]


def along_blk(value, sizes, target):
    ny, nx, nz, nc = sizes

    def index(y, x, z, c):
        return ((y % ny * nx + x % nx) * nz + z % nz) * nc + c % nc

    pairs = []
    for y in range(ny):
        for x in range(nx):
            for z in range(nz):
                for c in range(nc):
                    pairs.append((index(y, x, z, c), index(*target(y, x, z, c))))
    return lax.ppermute(value, BLK, pairs)


def from_neighbour(value, parity):
    count = lax.axis_size(BLK)
    pairs = []
    for block in range(count):
        chip, core = divmod(block, 2)
        first = chip % 2 == parity
        other = 2 * (chip + 1) + 1 - core if first else 2 * (chip - 1) + core
        pairs.append((block, other % count))
    return lax.ppermute(value, BLK, pairs)


def from_far(value):
    count = lax.axis_size(BLK)
    return lax.ppermute(
        value, BLK, [((b - 3 if b % 2 == 0 else b + 3) % count, b) for b in range(count)]
    )


def core_swap(value):
    return lax.ppermute(value, "core", [(0, 1), (1, 0)])


def shards(sizes, directions, axial_pos, azimuth, panel_area):
    count = axial_pos.shape[0]
    geometry = [part.reshape(count // LANES, LANES) for part in (axial_pos, azimuth, panel_area)]
    message = pack(directions, geometry)
    other = core_swap(message)
    even = from_neighbour(message, 0)
    odd = from_neighbour(message, 1)

    first, home = home_tile(message, count)
    first, late = lax.optimization_barrier((first, message))
    far = from_far(late)
    (first,) = guest_tile(home, (other,), first)
    first, even, later = lax.optimization_barrier((first, even, directions))
    pair = lax.ppermute(later, "rhs", [(0, 1), (1, 0)])
    even_other = core_swap(even)
    second, first = guest_tile(home, (even,), None, (first,))
    second, odd = lax.optimization_barrier((second, odd))
    odd_other = core_swap(odd)
    second, first = guest_tile(home, (odd,), second, (first,))
    second, far = lax.optimization_barrier((second, far))
    core = lax.axis_index("core").astype(jnp.int32)
    first, second = guest_tile(home, (far,), first, (second,))
    keep, give, product = half_gram(core.reshape(1), directions, pair, first, second)

    work = [(guest, piece) for guest in (even_other, odd_other) for piece in range(PIECES)]

    def advance(product, pieces):
        for _ in range(pieces):
            guest, piece = work.pop(0)
            product = piece_tile(home, guest, product, piece, not work)
        return product

    value = keep + core_swap(give)
    value, product = lax.optimization_barrier((value, product))
    crossed = lax.ppermute(value, ("core", "rhs"), [(2, 3), (3, 2)])
    product = advance(product, 1)
    value, crossed, product = lax.optimization_barrier((value, crossed, product))
    value = fold(core.reshape(1), value, crossed)

    def moved_by(sent, move):
        return along_blk(
            sent, sizes, lambda y, x, z, c: (y ^ move[0], x ^ move[1], z ^ move[2], c ^ move[3])
        )

    stages = (
        (((0, 0, 4, 0),), 3),
        (((0, 0, 1, 0), (0, 0, 2, 0), (0, 0, 3, 0)), 2),
        (((1, 0, 0, 0), (2, 0, 0, 0), (3, 0, 0, 0)), 1),
    )
    for moves, pieces in stages:
        sent = value.astype(jnp.bfloat16)
        product, sent = lax.optimization_barrier((product, sent))
        moved = [moved_by(sent, move) for move in moves]
        product = advance(product, pieces)
        sent, product, *moved = lax.optimization_barrier((sent, product, *moved))
        value, *moved = [term.astype(jnp.float32) for term in (sent, *moved)]
        value = value + moved[0]
        if len(moved) > 1:
            value = value + (moved[1] + moved[2])

    product, value = lax.optimization_barrier((product, value))
    moved = [moved_by(value, move) for move in ((0, 1, 0, 0), (0, 0, 0, 1), (0, 1, 0, 1))]
    product = advance(product, len(work))
    product, value, *moved = lax.optimization_barrier((product, value, *moved))
    scale = 1.0 / (count * lax.axis_size(BLK))
    value, swapped = (value + moved[0]) * scale, (moved[1] + moved[2]) * scale
    upper = core == lax.axis_index("rhs")
    gram = jnp.concatenate([jnp.where(upper, value, swapped), jnp.where(upper, swapped, value)], axis=0)
    return product, gram


def solution(mesh):
    sizes = (4, 2, 8, 2)
    fine = Mesh(mesh.devices.reshape(sizes + (2,)), BLK + ("rhs",))
    in_specs = (P(BLK, "rhs"), P(BLK), P(BLK), P(BLK))
    out_specs = (P(BLK, "rhs"), P(None, "rhs"))
    return jax.shard_map(
        functools.partial(shards, sizes), mesh=fine, in_specs=in_specs, out_specs=out_specs, check_vma=False
    )
```

```python
import functools

import jax
import jax.numpy as jnp
from jax import lax
from jax.experimental import pallas as pl
from jax.experimental.pallas import tpu as pltpu
from jax.sharding import Mesh, PartitionSpec as P

LANES = 128
VMEM_BYTES = 12 * 2**20
STEP = 256
HALVES = 2
PIECES = 4
COPIES = 4
BLK = ("y", "xh", "z", "core")


def split_parts(base):
    high = base.astype(jnp.bfloat16).astype(jnp.float32)
    rest = base - high
    mid = rest.astype(jnp.bfloat16).astype(jnp.float32)
    low = (rest - mid).astype(jnp.bfloat16).astype(jnp.float32)
    return high, mid, low


def point_values(axial, angle, area):
    axial = axial.astype(jnp.float32) - 4.0
    angle = angle.astype(jnp.float32)
    area = area.astype(jnp.float32)
    cos, sin = jnp.cos(angle), jnp.sin(angle)
    return axial, cos, sin, axial * axial + cos * cos + sin * sin, 1.0 / (area * area)


def lay_rows(base_ref, features):
    groups = features[0].shape[0]
    base_ref[...] = jnp.zeros_like(base_ref)
    for row, feature in enumerate(features):
        for group in range(groups):
            base_ref[row : row + 1, group * LANES : (group + 1) * LANES] = feature[group : group + 1, :]


def guest_factors(geometry, base_ref, row_ref):
    axial, cos, sin, norm, scale = point_values(*geometry)
    lay_rows(base_ref, (scale, norm * scale, axial * scale, cos * scale, sin * scale))
    high, mid, low = split_parts(base_ref[...])
    stacked = jnp.concatenate([high, high, high, mid, mid, low], axis=0)
    for group in range(row_ref.shape[0] // LANES):
        part = stacked[:, group * LANES : (group + 1) * LANES]
        row_ref[group * LANES : (group + 1) * LANES, :] = part.T.astype(jnp.bfloat16)


def home_factors(geometry, base_ref, col_ref):
    axial, cos, sin, norm, scale = point_values(*geometry)
    scale = scale * base_ref.shape[1]
    double = -2.0 * scale
    lay_rows(base_ref, ((norm + 0.01) * scale, scale, axial * double, cos * double, sin * double))
    high, mid, low = split_parts(base_ref[...])
    col_ref[...] = jnp.concatenate([high, mid, low, high, mid, high], axis=0).astype(jnp.bfloat16)


def add_panels(total, row_ref, directions_ref, home, start, count, where=0):
    for low in range(0, count, STEP):
        at = start + low
        inverse = jnp.dot(row_ref[pl.ds(at, STEP), :], home, preferred_element_type=jnp.float32)
        values = lax.rsqrt(inverse).astype(jnp.bfloat16)
        directions = directions_ref[:, pl.ds(where + at, STEP)]
        total = total + jnp.dot(directions, values, preferred_element_type=jnp.float32)
    return total


def tile_product(home_ref, row_ref, directions_ref, out_ref, arrive=None):
    count = row_ref.shape[0] // HALVES

    def step_fn(step, carried):
        if arrive is not None:
            arrive(step)
        start = pl.multiple_of(step * count, count)
        out_ref[...] = add_panels(out_ref[...], row_ref, directions_ref, home_ref[...], start, count)
        return carried

    lax.fori_loop(0, HALVES, step_fn, 0)


def geometry_of(ref):
    groups = ref.shape[0] // 3
    return tuple(ref[k * groups : (k + 1) * groups, :].astype(jnp.float32) for k in range(3))


def geometry_copy(message_ref, geometry_ref, sem):
    count = message_ref.shape[1] - LANES
    return pltpu.make_async_copy(
        message_ref.at[pl.ds(0, geometry_ref.shape[0]), pl.ds(count, LANES)], geometry_ref, sem
    )


def pack_body(directions_ref, axial_ref, angle_ref, area_ref, out_ref, held_ref, sems):
    count = directions_ref.shape[0]
    part = count // COPIES
    copies = []
    for k in range(COPIES):
        rows = pl.ds(k * part, part)
        copies.append(pltpu.make_async_copy(directions_ref.at[rows], held_ref.at[rows], sems.at[k]))
    groups = axial_ref.shape[0]
    for k, ref in enumerate((axial_ref, angle_ref, area_ref)):
        place = out_ref.at[pl.ds(k * groups, groups), pl.ds(count, LANES)]
        copies.append(pltpu.make_async_copy(ref, place, sems.at[COPIES + k]))
    for copy in copies:
        copy.start()
    out_ref[3 * groups :, count:] = jnp.zeros((LANES - 3 * groups, LANES), jnp.bfloat16)
    for k in range(COPIES):
        copies[k].wait()
        for low in range(k * part, (k + 1) * part, LANES):
            out_ref[:, low : low + LANES] = held_ref[low : low + LANES, :].T
    for copy in copies[COPIES:]:
        copy.wait()


def home_body(message_ref, out_ref, home_ref, base_ref, row_ref):
    count = row_ref.shape[0]
    geometry = geometry_of(message_ref.at[pl.ds(0, 3 * count // LANES), pl.ds(count, LANES)])
    home_factors(geometry, base_ref, home_ref)
    guest_factors(geometry, base_ref, row_ref)
    out_ref[...] = jnp.zeros_like(out_ref)
    tile_product(home_ref, row_ref, message_ref, out_ref)


def guest_body(has_total, n_held, n_sources, *refs):
    refs = list(refs)
    choice_ref = refs.pop(0) if n_sources > 1 else None
    home_ref = refs.pop(0)
    sources = [refs.pop(0) for _ in range(n_sources)]
    out_ref, *refs = refs[has_total + n_held :]
    base_ref, row_ref, directions_ref, geometry_ref, sems = refs[n_held:]
    part = row_ref.shape[0] // HALVES

    def part_copy(ref, step):
        columns = pl.ds(pl.multiple_of(step * part, part), part)
        return pltpu.make_async_copy(ref.at[:, columns], directions_ref.at[:, columns], sems.at[step])

    def fetch(ref):
        geometry_copy(ref, geometry_ref, sems.at[HALVES]).start()
        for step in range(HALVES):
            part_copy(ref, step).start()

    if choice_ref is None:
        fetch(sources[0])
    else:
        for k, ref in enumerate(sources):
            pl.when(choice_ref[0] == k)(functools.partial(fetch, ref))
    geometry_copy(sources[0], geometry_ref, sems.at[HALVES]).wait()
    guest_factors(geometry_of(geometry_ref), base_ref, row_ref)
    if not has_total:
        out_ref[...] = jnp.zeros_like(out_ref)
    tile_product(
        home_ref, row_ref, directions_ref, out_ref, arrive=lambda step: part_copy(sources[0], step).wait()
    )


def piece_body(
    offset, last, home_ref, message_ref, total_ref, out_ref, base_ref, row_ref, directions_ref, geometry_ref, sems
):
    width = row_ref.shape[0]
    geometry = geometry_copy(message_ref, geometry_ref, sems.at[0])
    copy = pltpu.make_async_copy(message_ref.at[:, pl.ds(offset, width)], directions_ref, sems.at[1])
    geometry.start()
    copy.start()
    geometry.wait()
    part = slice(offset // LANES, (offset + width) // LANES)
    guest_factors([value[part] for value in geometry_of(geometry_ref)], base_ref, row_ref)
    copy.wait()
    total = add_panels(total_ref[...], row_ref, directions_ref, home_ref[...], 0, width)
    out_ref[...] = total.T if last else total


def fold_body(core_ref, value_ref, crossed_ref, out_ref):
    first = core_ref[0] == 0

    @pl.when(first)
    def _():
        out_ref[...] = value_ref[...] + value_ref[...].T

    @pl.when(jnp.logical_not(first))
    def _():
        out_ref[...] = value_ref[...].T + crossed_ref[...]


def half_gram_body(
    core_ref, own_ref, pair_ref, first_ref, second_ref, keep_ref, give_ref, sum_ref, directions_ref, sems
):
    copies = [
        pltpu.make_async_copy(ref, directions_ref.at[k], sems.at[k]) for k, ref in enumerate((own_ref, pair_ref))
    ]
    for copy in copies:
        copy.start()
    first, second = first_ref[...], second_ref[...]
    value = 0.5 * first + second
    sum_ref[...] = first + second
    high = value.astype(jnp.bfloat16)
    low = (value - high.astype(jnp.float32)).astype(jnp.bfloat16)
    both = jnp.concatenate([high, low], axis=0)
    for copy in copies:
        copy.wait()
    directions = jnp.concatenate([directions_ref[0], directions_ref[1]], axis=1)
    part = jnp.dot(both, directions, preferred_element_type=jnp.float32)
    part = part[:LANES] + part[LANES:]
    on_first = core_ref[0] == 0
    keep_ref[...] = jnp.where(on_first, part[:, :LANES], part[:, LANES:])
    give_ref[...] = jnp.where(on_first, part[:, LANES:], part[:, :LANES])


def tile_cost(count):
    return pl.CostEstimate(flops=count * count * 16, bytes_accessed=0, transcendentals=0)


def kernel_call(body, name, operands, places, outs, scratch, cost, aliases=None):
    spaces = {"v": pltpu.VMEM, "s": pltpu.SMEM, "a": pl.ANY, "h": pltpu.HBM}
    fixed = {"v": pltpu.VMEM, "h": pltpu.HBM}
    operands = [
        pltpu.with_memory_space_constraint(value, fixed[place]) if place in fixed else value
        for value, place in zip(operands, places)
    ]
    return pl.pallas_call(
        body,
        out_shape=outs,
        in_specs=[pl.BlockSpec(memory_space=spaces[place]) for place in places],
        out_specs=[pl.BlockSpec(memory_space=pltpu.VMEM)] * len(outs),
        input_output_aliases=aliases or {},
        scratch_shapes=scratch,
        cost_estimate=cost,
        compiler_params=pltpu.CompilerParams(vmem_limit_bytes=VMEM_BYTES),
        name=name,
    )(*operands)


def pack(directions, geometry):
    count = directions.shape[0]
    return kernel_call(
        pack_body, "pack", [directions, *geometry], "hhhh", [pltpu.VMEM((LANES, count + LANES), jnp.bfloat16)],
        [pltpu.VMEM((count, LANES), jnp.bfloat16), pltpu.SemaphoreType.DMA((COPIES + 3,))],
        pl.CostEstimate(flops=0, bytes_accessed=2**20, transcendentals=0),
    )[0]


def tile_scratch(count):
    return [pltpu.VMEM((8, count), jnp.float32), pltpu.VMEM((count, 48), jnp.bfloat16)]


def fetch_scratch(count, geometry_rows, copies):
    return tile_scratch(count) + [
        pltpu.VMEM((LANES, count), jnp.bfloat16),
        pltpu.VMEM((geometry_rows, LANES), jnp.bfloat16),
        pltpu.SemaphoreType.DMA((copies,)),
    ]


def home_tile(message, count):
    outs = [pltpu.VMEM((LANES, count), jnp.float32), pltpu.VMEM((48, count), jnp.bfloat16)]
    return kernel_call(home_body, "home_tile", [message], "v", outs, tile_scratch(count), tile_cost(count))


def guest_tile(home, sources, total=None, held=(), choice=None):
    count = home.shape[1]
    totals = [] if total is None else [total]
    choices = [] if choice is None else [choice]
    place = len(choices) + 1 + len(sources)
    aliases = {place: 0} if totals else {}
    aliases.update({place + len(totals) + k: 1 + k for k in range(len(held))})
    return kernel_call(
        functools.partial(guest_body, len(totals), len(held), len(sources)), "guest_tile",
        [*choices, home, *sources, *totals, *held],
        "s" * len(choices) + "v" + "a" * len(sources) + "v" * (len(totals) + len(held)),
        [pltpu.VMEM((LANES, count), jnp.float32)] * (1 + len(held)),
        fetch_scratch(count, 3 * count // LANES, HALVES + 1), tile_cost(count), aliases,
    )


def piece_tile(home, message, total, piece, last):
    count = home.shape[1]
    width = count // PIECES
    out = jax.ShapeDtypeStruct((count, LANES), jnp.float32) if last else pltpu.VMEM((LANES, count), jnp.float32)
    return kernel_call(
        functools.partial(piece_body, piece * width, last), "piece_tile", [home, message, total], "vav", [out],
        fetch_scratch(width, 3 * count // LANES, 2), tile_cost(count), None if last else {2: 0},
    )[0]


def half_gram(core, own, pair, first, second):
    count = first.shape[1]
    block = pltpu.VMEM((LANES, LANES), jnp.float32)
    return kernel_call(
        half_gram_body, "half_gram", [core, own, pair, first, second], "shavv",
        [block, block, pltpu.VMEM((LANES, count), jnp.float32)],
        [pltpu.VMEM((2, count, LANES), jnp.bfloat16), pltpu.SemaphoreType.DMA((2,))], tile_cost(count), {3: 2},
    )


def fold(core, *blocks):
    out = pltpu.VMEM((LANES, LANES), jnp.float32)
    cost = pl.CostEstimate(flops=0, bytes_accessed=2**17, transcendentals=0)
    return kernel_call(fold_body, "fold", [core, *blocks], "svv", [out], [], cost)[0]


def along_blk(value, sizes, target):
    ny, nx, nz, nc = sizes

    def index(y, x, z, c):
        return ((y % ny * nx + x % nx) * nz + z % nz) * nc + c % nc

    pairs = []
    for y in range(ny):
        for x in range(nx):
            for z in range(nz):
                for c in range(nc):
                    pairs.append((index(y, x, z, c), index(*target(y, x, z, c))))
    return lax.ppermute(value, BLK, pairs)


def from_neighbour(value, parity):
    count = lax.axis_size(BLK)
    pairs = []
    for block in range(count):
        chip, core = divmod(block, 2)
        first = chip % 2 == parity
        other = 2 * (chip + 1) + 1 - core if first else 2 * (chip - 1) + core
        pairs.append((block, other % count))
    return lax.ppermute(value, BLK, pairs)


def from_far(value):
    count = lax.axis_size(BLK)
    return lax.ppermute(
        value, BLK, [((b - 3 if b % 2 == 0 else b + 3) % count, b) for b in range(count)]
    )


def core_swap(value):
    return lax.ppermute(value, "core", [(0, 1), (1, 0)])


def shards(sizes, directions, axial_pos, azimuth, panel_area):
    count = axial_pos.shape[0]
    geometry = [part.reshape(count // LANES, LANES) for part in (axial_pos, azimuth, panel_area)]
    message = pack(directions, geometry)
    other = core_swap(message)
    even = from_neighbour(message, 0)
    odd = from_neighbour(message, 1)

    first, home = home_tile(message, count)
    first, late = lax.optimization_barrier((first, message))
    far = from_far(late)
    (first,) = guest_tile(home, (other,), first)
    first, even, later = lax.optimization_barrier((first, even, directions))
    pair = lax.ppermute(later, "rhs", [(0, 1), (1, 0)])
    even_other = core_swap(even)
    second, first = guest_tile(home, (even,), None, (first,))
    second, odd = lax.optimization_barrier((second, odd))
    odd_other = core_swap(odd)
    second, first = guest_tile(home, (odd,), second, (first,))
    second, far = lax.optimization_barrier((second, far))
    core = lax.axis_index("core").astype(jnp.int32)
    first, second = guest_tile(home, (far,), first, (second,))
    keep, give, product = half_gram(core.reshape(1), directions, pair, first, second)

    work = [(guest, piece) for guest in (even_other, odd_other) for piece in range(PIECES)]

    def advance(product, pieces):
        for _ in range(pieces):
            guest, piece = work.pop(0)
            product = piece_tile(home, guest, product, piece, not work)
        return product

    value = keep + core_swap(give)
    value, product = lax.optimization_barrier((value, product))
    crossed = lax.ppermute(value, ("core", "rhs"), [(2, 3), (3, 2)])
    product = advance(product, 1)
    value, crossed, product = lax.optimization_barrier((value, crossed, product))
    value = fold(core.reshape(1), value, crossed)

    def moved_by(sent, move):
        return along_blk(
            sent, sizes, lambda y, x, z, c: (y ^ move[0], x ^ move[1], z ^ move[2], c ^ move[3])
        )

    stages = (
        (((0, 0, 4, 0),), 3),
        (((0, 0, 1, 0), (0, 0, 2, 0), (0, 0, 3, 0)), 2),
        (((1, 0, 0, 0), (2, 0, 0, 0), (3, 0, 0, 0)), 1),
    )
    for moves, pieces in stages:
        sent = value.astype(jnp.bfloat16)
        product, sent = lax.optimization_barrier((product, sent))
        moved = [moved_by(sent, move) for move in moves]
        product = advance(product, pieces)
        sent, product, *moved = lax.optimization_barrier((sent, product, *moved))
        value, *moved = [term.astype(jnp.float32) for term in (sent, *moved)]
        value = value + moved[0]
        if len(moved) > 1:
            value = value + (moved[1] + moved[2])

    product, value = lax.optimization_barrier((product, value))
    moved = [moved_by(value, move) for move in ((0, 1, 0, 0), (0, 0, 0, 1), (0, 1, 0, 1))]
    product = advance(product, len(work))
    product, value, *moved = lax.optimization_barrier((product, value, *moved))
    scale = 1.0 / (count * lax.axis_size(BLK))
    value, swapped = (value + moved[0]) * scale, (moved[1] + moved[2]) * scale
    upper = core == lax.axis_index("rhs")
    gram = jnp.concatenate([jnp.where(upper, value, swapped), jnp.where(upper, swapped, value)], axis=0)
    return product, gram


def solution(mesh):
    sizes = (4, 2, 8, 2)
    fine = Mesh(mesh.devices.reshape(sizes + (2,)), BLK + ("rhs",))
    in_specs = (P(BLK, "rhs"), P(BLK), P(BLK), P(BLK))
    out_specs = (P(BLK, "rhs"), P(None, "rhs"))
    return jax.shard_map(
        functools.partial(shards, sizes), mesh=fine, in_specs=in_specs, out_specs=out_specs, check_vma=False
    )
```

```python
import functools

import jax
import jax.numpy as jnp
from jax import lax
from jax.experimental import pallas as pl
from jax.experimental.pallas import tpu as pltpu
from jax.sharding import Mesh, PartitionSpec as P

LANES = 128
VMEM_BYTES = 12 * 2**20
STEP = 256
HALVES = 2
PIECES = 4
COPIES = 4
BLK = ("y", "xh", "z", "core")


def split_parts(base):
    high = base.astype(jnp.bfloat16).astype(jnp.float32)
    rest = base - high
    mid = rest.astype(jnp.bfloat16).astype(jnp.float32)
    low = (rest - mid).astype(jnp.bfloat16).astype(jnp.float32)
    return high, mid, low


def point_values(axial, angle, area):
    axial = axial.astype(jnp.float32) - 4.0
    angle = angle.astype(jnp.float32)
    area = area.astype(jnp.float32)
    cos, sin = jnp.cos(angle), jnp.sin(angle)
    return axial, cos, sin, axial * axial + cos * cos + sin * sin, 1.0 / (area * area)


def lay_rows(base_ref, features):
    groups = features[0].shape[0]
    base_ref[...] = jnp.zeros_like(base_ref)
    for row, feature in enumerate(features):
        for group in range(groups):
            base_ref[row : row + 1, group * LANES : (group + 1) * LANES] = feature[group : group + 1, :]


def guest_factors(geometry, base_ref, row_ref):
    axial, cos, sin, norm, scale = point_values(*geometry)
    lay_rows(base_ref, (scale, norm * scale, axial * scale, cos * scale, sin * scale))
    high, mid, low = split_parts(base_ref[...])
    stacked = jnp.concatenate([high, high, high, mid, mid, low], axis=0)
    for group in range(row_ref.shape[0] // LANES):
        part = stacked[:, group * LANES : (group + 1) * LANES]
        row_ref[group * LANES : (group + 1) * LANES, :] = part.T.astype(jnp.bfloat16)


def home_factors(geometry, base_ref, col_ref):
    axial, cos, sin, norm, scale = point_values(*geometry)
    scale = scale * base_ref.shape[1]
    double = -2.0 * scale
    lay_rows(base_ref, ((norm + 0.01) * scale, scale, axial * double, cos * double, sin * double))
    high, mid, low = split_parts(base_ref[...])
    col_ref[...] = jnp.concatenate([high, mid, low, high, mid, high], axis=0).astype(jnp.bfloat16)


def add_panels(total, row_ref, directions_ref, home, start, count, where=0):
    for low in range(0, count, STEP):
        at = start + low
        inverse = jnp.dot(row_ref[pl.ds(at, STEP), :], home, preferred_element_type=jnp.float32)
        values = lax.rsqrt(inverse).astype(jnp.bfloat16)
        directions = directions_ref[:, pl.ds(where + at, STEP)]
        total = total + jnp.dot(directions, values, preferred_element_type=jnp.float32)
    return total


def tile_product(home_ref, row_ref, directions_ref, out_ref, arrive=None):
    count = row_ref.shape[0] // HALVES

    def step_fn(step, carried):
        if arrive is not None:
            arrive(step)
        start = pl.multiple_of(step * count, count)
        out_ref[...] = add_panels(out_ref[...], row_ref, directions_ref, home_ref[...], start, count)
        return carried

    lax.fori_loop(0, HALVES, step_fn, 0)


def geometry_of(ref):
    groups = ref.shape[0] // 3
    return tuple(ref[k * groups : (k + 1) * groups, :].astype(jnp.float32) for k in range(3))


def geometry_copy(message_ref, geometry_ref, sem):
    count = message_ref.shape[1] - LANES
    return pltpu.make_async_copy(
        message_ref.at[pl.ds(0, geometry_ref.shape[0]), pl.ds(count, LANES)], geometry_ref, sem
    )


def pack_body(directions_ref, axial_ref, angle_ref, area_ref, out_ref, held_ref, sems):
    count = directions_ref.shape[0]
    part = count // COPIES
    copies = []
    for k in range(COPIES):
        rows = pl.ds(k * part, part)
        copies.append(pltpu.make_async_copy(directions_ref.at[rows], held_ref.at[rows], sems.at[k]))
    groups = axial_ref.shape[0]
    for k, ref in enumerate((axial_ref, angle_ref, area_ref)):
        place = out_ref.at[pl.ds(k * groups, groups), pl.ds(count, LANES)]
        copies.append(pltpu.make_async_copy(ref, place, sems.at[COPIES + k]))
    for copy in copies:
        copy.start()
    out_ref[3 * groups :, count:] = jnp.zeros((LANES - 3 * groups, LANES), jnp.bfloat16)
    for k in range(COPIES):
        copies[k].wait()
        for low in range(k * part, (k + 1) * part, LANES):
            out_ref[:, low : low + LANES] = held_ref[low : low + LANES, :].T
    for copy in copies[COPIES:]:
        copy.wait()


def home_body(message_ref, out_ref, home_ref, base_ref, row_ref):
    count = row_ref.shape[0]
    geometry = geometry_of(message_ref.at[pl.ds(0, 3 * count // LANES), pl.ds(count, LANES)])
    home_factors(geometry, base_ref, home_ref)
    guest_factors(geometry, base_ref, row_ref)
    out_ref[...] = jnp.zeros_like(out_ref)
    tile_product(home_ref, row_ref, message_ref, out_ref)


def guest_body(has_total, n_held, n_sources, *refs):
    refs = list(refs)
    choice_ref = refs.pop(0) if n_sources > 1 else None
    home_ref = refs.pop(0)
    sources = [refs.pop(0) for _ in range(n_sources)]
    out_ref, *refs = refs[has_total + n_held :]
    base_ref, row_ref, directions_ref, geometry_ref, sems = refs[n_held:]
    part = row_ref.shape[0] // HALVES

    def part_copy(ref, step):
        columns = pl.ds(pl.multiple_of(step * part, part), part)
        return pltpu.make_async_copy(ref.at[:, columns], directions_ref.at[:, columns], sems.at[step])

    def fetch(ref):
        geometry_copy(ref, geometry_ref, sems.at[HALVES]).start()
        for step in range(HALVES):
            part_copy(ref, step).start()

    if choice_ref is None:
        fetch(sources[0])
    else:
        for k, ref in enumerate(sources):
            pl.when(choice_ref[0] == k)(functools.partial(fetch, ref))
    geometry_copy(sources[0], geometry_ref, sems.at[HALVES]).wait()
    guest_factors(geometry_of(geometry_ref), base_ref, row_ref)
    if not has_total:
        out_ref[...] = jnp.zeros_like(out_ref)
    tile_product(
        home_ref, row_ref, directions_ref, out_ref, arrive=lambda step: part_copy(sources[0], step).wait()
    )


def piece_body(
    offset, last, home_ref, message_ref, total_ref, out_ref, base_ref, row_ref, directions_ref, geometry_ref, sems
):
    width = row_ref.shape[0]
    geometry = geometry_copy(message_ref, geometry_ref, sems.at[0])
    copy = pltpu.make_async_copy(message_ref.at[:, pl.ds(offset, width)], directions_ref, sems.at[1])
    geometry.start()
    copy.start()
    geometry.wait()
    part = slice(offset // LANES, (offset + width) // LANES)
    guest_factors([value[part] for value in geometry_of(geometry_ref)], base_ref, row_ref)
    copy.wait()
    total = add_panels(total_ref[...], row_ref, directions_ref, home_ref[...], 0, width)
    out_ref[...] = total.T if last else total


def fold_body(core_ref, value_ref, crossed_ref, out_ref):
    first = core_ref[0] == 0

    @pl.when(first)
    def _():
        out_ref[...] = value_ref[...] + value_ref[...].T

    @pl.when(jnp.logical_not(first))
    def _():
        out_ref[...] = value_ref[...].T + crossed_ref[...]


def half_gram_body(
    core_ref, own_ref, pair_ref, first_ref, second_ref, keep_ref, give_ref, sum_ref, directions_ref, sems
):
    copies = [
        pltpu.make_async_copy(ref, directions_ref.at[k], sems.at[k]) for k, ref in enumerate((own_ref, pair_ref))
    ]
    for copy in copies:
        copy.start()
    first, second = first_ref[...], second_ref[...]
    value = 0.5 * first + second
    sum_ref[...] = first + second
    high = value.astype(jnp.bfloat16)
    low = (value - high.astype(jnp.float32)).astype(jnp.bfloat16)
    both = jnp.concatenate([high, low], axis=0)
    for copy in copies:
        copy.wait()
    directions = jnp.concatenate([directions_ref[0], directions_ref[1]], axis=1)
    part = jnp.dot(both, directions, preferred_element_type=jnp.float32)
    part = part[:LANES] + part[LANES:]
    on_first = core_ref[0] == 0
    keep_ref[...] = jnp.where(on_first, part[:, :LANES], part[:, LANES:])
    give_ref[...] = jnp.where(on_first, part[:, LANES:], part[:, :LANES])


def tile_cost(count):
    return pl.CostEstimate(flops=count * count * 16, bytes_accessed=0, transcendentals=0)


def kernel_call(body, name, operands, places, outs, scratch, cost, aliases=None):
    spaces = {"v": pltpu.VMEM, "s": pltpu.SMEM, "a": pl.ANY, "h": pltpu.HBM}
    fixed = {"v": pltpu.VMEM, "h": pltpu.HBM}
    operands = [
        pltpu.with_memory_space_constraint(value, fixed[place]) if place in fixed else value
        for value, place in zip(operands, places)
    ]
    return pl.pallas_call(
        body,
        out_shape=outs,
        in_specs=[pl.BlockSpec(memory_space=spaces[place]) for place in places],
        out_specs=[pl.BlockSpec(memory_space=pltpu.VMEM)] * len(outs),
        input_output_aliases=aliases or {},
        scratch_shapes=scratch,
        cost_estimate=cost,
        compiler_params=pltpu.CompilerParams(vmem_limit_bytes=VMEM_BYTES),
        name=name,
    )(*operands)


def pack(directions, geometry):
    count = directions.shape[0]
    return kernel_call(
        pack_body, "pack", [directions, *geometry], "hhhh", [pltpu.VMEM((LANES, count + LANES), jnp.bfloat16)],
        [pltpu.VMEM((count, LANES), jnp.bfloat16), pltpu.SemaphoreType.DMA((COPIES + 3,))],
        pl.CostEstimate(flops=0, bytes_accessed=2**20, transcendentals=0),
    )[0]


def tile_scratch(count):
    return [pltpu.VMEM((8, count), jnp.float32), pltpu.VMEM((count, 48), jnp.bfloat16)]


def fetch_scratch(count, geometry_rows, copies):
    return tile_scratch(count) + [
        pltpu.VMEM((LANES, count), jnp.bfloat16),
        pltpu.VMEM((geometry_rows, LANES), jnp.bfloat16),
        pltpu.SemaphoreType.DMA((copies,)),
    ]


def home_tile(message, count):
    outs = [pltpu.VMEM((LANES, count), jnp.float32), pltpu.VMEM((48, count), jnp.bfloat16)]
    return kernel_call(home_body, "home_tile", [message], "v", outs, tile_scratch(count), tile_cost(count))


def guest_tile(home, sources, total=None, held=(), choice=None):
    count = home.shape[1]
    totals = [] if total is None else [total]
    choices = [] if choice is None else [choice]
    place = len(choices) + 1 + len(sources)
    aliases = {place: 0} if totals else {}
    aliases.update({place + len(totals) + k: 1 + k for k in range(len(held))})
    return kernel_call(
        functools.partial(guest_body, len(totals), len(held), len(sources)), "guest_tile",
        [*choices, home, *sources, *totals, *held],
        "s" * len(choices) + "v" + "a" * len(sources) + "v" * (len(totals) + len(held)),
        [pltpu.VMEM((LANES, count), jnp.float32)] * (1 + len(held)),
        fetch_scratch(count, 3 * count // LANES, HALVES + 1), tile_cost(count), aliases,
    )


def piece_tile(home, message, total, piece, last):
    count = home.shape[1]
    width = count // PIECES
    out = jax.ShapeDtypeStruct((count, LANES), jnp.float32) if last else pltpu.VMEM((LANES, count), jnp.float32)
    return kernel_call(
        functools.partial(piece_body, piece * width, last), "piece_tile", [home, message, total], "vav", [out],
        fetch_scratch(width, 3 * count // LANES, 2), tile_cost(count), None if last else {2: 0},
    )[0]


def half_gram(core, own, pair, first, second):
    count = first.shape[1]
    block = pltpu.VMEM((LANES, LANES), jnp.float32)
    return kernel_call(
        half_gram_body, "half_gram", [core, own, pair, first, second], "shavv",
        [block, block, pltpu.VMEM((LANES, count), jnp.float32)],
        [pltpu.VMEM((2, count, LANES), jnp.bfloat16), pltpu.SemaphoreType.DMA((2,))], tile_cost(count), {3: 2},
    )


def fold(core, *blocks):
    out = pltpu.VMEM((LANES, LANES), jnp.float32)
    cost = pl.CostEstimate(flops=0, bytes_accessed=2**17, transcendentals=0)
    return kernel_call(fold_body, "fold", [core, *blocks], "svv", [out], [], cost)[0]


def along_blk(value, sizes, target):
    ny, nx, nz, nc = sizes

    def index(y, x, z, c):
        return ((y % ny * nx + x % nx) * nz + z % nz) * nc + c % nc

    pairs = []
    for y in range(ny):
        for x in range(nx):
            for z in range(nz):
                for c in range(nc):
                    pairs.append((index(y, x, z, c), index(*target(y, x, z, c))))
    return lax.ppermute(value, BLK, pairs)


def from_neighbour(value, parity):
    count = lax.axis_size(BLK)
    pairs = []
    for block in range(count):
        chip, core = divmod(block, 2)
        first = chip % 2 == parity
        other = 2 * (chip + 1) + 1 - core if first else 2 * (chip - 1) + core
        pairs.append((block, other % count))
    return lax.ppermute(value, BLK, pairs)


def from_far(value):
    count = lax.axis_size(BLK)
    return lax.ppermute(
        value, BLK, [((b - 3 if b % 2 == 0 else b + 3) % count, b) for b in range(count)]
    )


def core_swap(value):
    return lax.ppermute(value, "core", [(0, 1), (1, 0)])


def shards(sizes, directions, axial_pos, azimuth, panel_area):
    count = axial_pos.shape[0]
    geometry = [part.reshape(count // LANES, LANES) for part in (axial_pos, azimuth, panel_area)]
    message = pack(directions, geometry)
    other = core_swap(message)
    even = from_neighbour(message, 0)
    odd = from_neighbour(message, 1)

    first, home = home_tile(message, count)
    first, late = lax.optimization_barrier((first, message))
    far = from_far(late)
    (first,) = guest_tile(home, (other,), first)
    first, even, later = lax.optimization_barrier((first, even, directions))
    pair = lax.ppermute(later, "rhs", [(0, 1), (1, 0)])
    even_other = core_swap(even)
    second, first = guest_tile(home, (even,), None, (first,))
    second, odd = lax.optimization_barrier((second, odd))
    odd_other = core_swap(odd)
    second, first = guest_tile(home, (odd,), second, (first,))
    second, far = lax.optimization_barrier((second, far))
    core = lax.axis_index("core").astype(jnp.int32)
    first, second = guest_tile(home, (far,), first, (second,))
    keep, give, product = half_gram(core.reshape(1), directions, pair, first, second)

    work = [(guest, piece) for guest in (even_other, odd_other) for piece in range(PIECES)]

    def advance(product, pieces):
        for _ in range(pieces):
            guest, piece = work.pop(0)
            product = piece_tile(home, guest, product, piece, not work)
        return product

    value = keep + core_swap(give)
    value, product = lax.optimization_barrier((value, product))
    crossed = lax.ppermute(value, ("core", "rhs"), [(2, 3), (3, 2)])
    product = advance(product, 1)
    value, crossed, product = lax.optimization_barrier((value, crossed, product))
    value = fold(core.reshape(1), value, crossed)

    def moved_by(sent, move):
        return along_blk(
            sent, sizes, lambda y, x, z, c: (y ^ move[0], x ^ move[1], z ^ move[2], c ^ move[3])
        )

    stages = (
        (((1, 0, 0, 0), (2, 0, 0, 0), (3, 0, 0, 0)), 2),
        (((0, 0, 1, 0), (0, 0, 2, 0), (0, 0, 3, 0)), 2),
        (((0, 0, 4, 0),), 2),
    )
    for moves, pieces in stages:
        sent = value.astype(jnp.bfloat16)
        product, sent = lax.optimization_barrier((product, sent))
        moved = [moved_by(sent, move) for move in moves]
        product = advance(product, pieces)
        sent, product, *moved = lax.optimization_barrier((sent, product, *moved))
        value, *moved = [term.astype(jnp.float32) for term in (sent, *moved)]
        value = value + moved[0]
        if len(moved) > 1:
            value = value + (moved[1] + moved[2])

    product, value = lax.optimization_barrier((product, value))
    moved = [moved_by(value, move) for move in ((0, 1, 0, 0), (0, 0, 0, 1), (0, 1, 0, 1))]
    product = advance(product, len(work))
    product, value, *moved = lax.optimization_barrier((product, value, *moved))
    scale = 1.0 / (count * lax.axis_size(BLK))
    value, swapped = (value + moved[0]) * scale, (moved[1] + moved[2]) * scale
    upper = core == lax.axis_index("rhs")
    gram = jnp.concatenate([jnp.where(upper, value, swapped), jnp.where(upper, swapped, value)], axis=0)
    return product, gram


def solution(mesh):
    sizes = (4, 2, 8, 2)
    fine = Mesh(mesh.devices.reshape(sizes + (2,)), BLK + ("rhs",))
    in_specs = (P(BLK, "rhs"), P(BLK), P(BLK), P(BLK))
    out_specs = (P(BLK, "rhs"), P(None, "rhs"))
    return jax.shard_map(
        functools.partial(shards, sizes), mesh=fine, in_specs=in_specs, out_specs=out_specs, check_vma=False
    )
```
